512 devices in a mesh: section: 8 (over y_lo, x), peer: 64 (over y_hi, z, core).
Axes of the slice: x: 4, y: 8 (y_hi: 4, y_lo: 2; y = y_hi * 2 + y_lo), z: 8, core: 2. Of those that a mesh axis runs over, the one named last changes fastest.
Arguments:
- placing: int32 [8, 64, 1], replicated, may hold values from 0 to 63; in each aligned block of 64 rows (0 to 63, 64 to 127, ..., all dimensions but the last counted through in order) at most 2 rows name the same one
- acts: bfloat16 [8, 64, 2, 2, 5120], P('section', 'peer'), may hold values from -6 to 6
- cotan: bfloat16 [8, 64, 2, 2, 5120], P('section', 'peer'), may hold values from -48 to 48
- gain: bfloat16 [8, 5120], P('section'), may hold values from 0.5 to 1.5
- w_value: bfloat16 [8, 2560, 5120], P('section', 'peer'), may hold values from -0.078125 to 0.078125
- w_out: bfloat16 [8, 5120, 2560], P('section', 'peer'), may hold values from -1 to 1
- moment_one: float32 [8, 2560, 5120], P('section', 'peer'), may hold values from -0.0006 to 0.0006
- moment_two: float32 [8, 2560, 5120], P('section', 'peer'), may hold values from 1e-07 to 1e-05
Outputs:
- passed: bfloat16 [8, 64, 2, 2, 5120], P('section', 'peer')
- returned: bfloat16 [8, 64, 2, 2, 5120], P('section', 'peer')
- new_value: bfloat16 [8, 2560, 5120], P('section', 'peer')
- new_first: float32 [8, 2560, 5120], P('section', 'peer')
- new_second: float32 [8, 2560, 5120], P('section', 'peer')
The draws below stay inside these ranges and needn't reach their ends.
Inputs may be any that keep to these rules, and one draw needn't show every extreme that they name: `placing`: at every section no peer holds more than 2 micro-batches, and some peer holds exactly 2.
All inputs are finite; a program needn't handle non-finite values.
Results may differ from the reference program's by a relative error of at most 0.011.
Values may be sent and summed in bfloat16 or wider, within the bound.
No kernel may reach another device: no remote copies, remote signals or barrier semaphores. Data moves between devices by JAX's collectives and lax.ppermute only.
A program may use at most 64 MiB of HBM per device.

```python
import math
import jax
import jax.numpy as jnp
import numpy as np
from jax import lax

D = 5120
HV = 2560
MB = 2
CAP = 2
SECTIONS = 8
PEERS = 64


def rising(count, factor):
    steps = jnp.arange(count, dtype=jnp.float32) / max(count - 1, 1)
    return factor ** steps


def draw_cotan(key, part):
    key = jax.random.fold_in(key, 11)
    shape = (SECTIONS, PEERS, CAP, MB, D)
    base = jnp.clip(jax.random.normal(key, shape, jnp.float32), -6.0, 6.0)
    factor = 3.0
    scale = rising(SECTIONS, factor)
    return (base * scale[:, None, None, None, None]).astype(jnp.bfloat16)


def draw_w_out(key, part):
    key = jax.random.fold_in(key, 23)
    shape = (SECTIONS, D, HV)
    base = jnp.clip(jax.random.normal(key, shape, jnp.float32), -6.0, 6.0)
    factor = 3.0
    columns = rising(HV, factor)
    columns = columns / jnp.mean(columns)
    return (base * columns[None, None, :] * HV ** (-0.5)).astype(jnp.bfloat16)


def level_of(own_key, shape, shards, low, top_value):
    factor_of = 1.0
    for position, shards_of in shards:
        steps = jax.random.uniform(jax.random.fold_in(jax.random.fold_in(own_key, 6), position), (shards_of,), jnp.float32, low / len(shards), top_value / len(shards))
        factor_of = factor_of * jnp.repeat(jnp.exp(steps), shape[position] // shards_of).reshape((-1,) + (1,) * (len(shape) - 1 - position))
    return factor_of


def assign_block(rng, own, number, rows, amount, top, reach, skew):
    order = jax.random.permutation(rng, amount)
    packed, ordinary = shares(amount, rows * top, reach, skew, True), shares(amount, rows * top, reach, skew, False)
    places = jnp.arange(amount)

    def named(lengths, turn):
        used = int((lengths > 0).sum())
        fixed = max(1, used // 4)
        moved = fixed + (places - fixed + turn * (used - fixed)) % max(1, amount - fixed)
        return jnp.zeros((amount,), jnp.int32).at[order[jnp.where(places < fixed, places, moved)]].set(jnp.asarray(lengths, jnp.int32))

    lengths = jnp.where(number % 4 == 0, named(packed, number // 4), named(ordinary, number - number // 4 - 1))
    mixed = jax.random.permutation(jax.random.fold_in(own, 3), amount)
    source_of, receiver = mixed[0:amount // 2 * 2:2], mixed[1:amount // 2 * 2:2]
    margin = jnp.minimum(lengths[source_of] - 1, reach - lengths[receiver]) // 2
    margin = jnp.where((source_of == order[0]) | (receiver == order[0]) | (lengths[receiver] == 0), 0, jnp.maximum(margin, 0))
    moved = jax.random.randint(jax.random.fold_in(own, 4), (amount // 2,), 0, 1 << 20) % (margin + 1)
    lengths = lengths.at[source_of].add(-moved).at[receiver].add(moved)
    labels = jnp.searchsorted(jnp.cumsum(lengths), jnp.arange(rows * top), side="right").astype(jnp.int32)
    table = labels.reshape(top, rows).T
    table = table[jax.random.permutation(jax.random.fold_in(own, 1), rows)]
    turn = jax.random.randint(jax.random.fold_in(own, 2), (rows, 1), 0, top)
    return jnp.take_along_axis(table, (jnp.arange(top)[None, :] + turn) % top, axis=1)


def shares(count, total, limit, slope, full):
    portions = [(1 << 20) // math.isqrt(rank ** slope) + 1 for rank in range(1, count + 1)]
    largest = limit if full else min(limit, max(-(-total // count), total * portions[0] // sum(portions)))
    least = 1 if total - largest >= count - 1 else 0
    given, surplus = [largest] + [least] * (count - 1), total - largest - least * (count - 1)
    while surplus > 0:
        movable = [i for i in range(1, count) if given[i] < largest] or [i for i in range(1, count) if given[i] < limit]
        mass, budget = sum([portions[i] for i in movable]), surplus
        for i in movable:
            more = min(limit - given[i], max(1, budget * portions[i] // mass), surplus)
            given[i] = given[i] + more
            surplus = surplus - more
    return np.array(given)


def gaussian(key, dims, deviation, reach, pieces=(), held_as=jnp.bfloat16):
    entries = deviation * jax.random.normal(key, dims, jnp.float32)
    if pieces:
        entries = entries * level_of(key, dims, pieces, -0.22, 0.18)
    return jnp.clip(entries, -reach, reach).astype(held_as)


def setup_inputs(seed: int = 0) -> dict:
    splits = jax.random.split(jax.random.key(seed), 9)
    placing_keys = jax.random.split(jax.random.fold_in(splits[0], 1), SECTIONS * PEERS // PEERS)
    placing_turns = jax.random.permutation(jax.random.fold_in(splits[0], 3), SECTIONS * PEERS // PEERS)
    placing = jax.vmap(lambda own, number: assign_block(jax.random.fold_in(splits[0], 2), own, number, PEERS, PEERS, 1, CAP, 2))(placing_keys, placing_turns).reshape((SECTIONS, PEERS, 1))
    acts = gaussian(splits[1], (SECTIONS, PEERS, CAP, MB, D), 1.0, 6.0, ((0, 8), (1, 64)))
    cotan = draw_cotan(jax.random.fold_in(splits[8], 71), 0)
    gain = jnp.clip(1.0 + 0.1 * jax.random.normal(splits[3], (SECTIONS, D), jnp.float32), 0.5, 1.5).astype(jnp.bfloat16)
    w_value = gaussian(splits[4], (SECTIONS, HV, D), D ** -0.5, 0.078125, ((0, 8), (1, 64)))
    w_out = draw_w_out(jax.random.fold_in(splits[8], 71), 0)
    moment_one = gaussian(splits[6], (SECTIONS, HV, D), 0.0001, 0.0006, ((0, 8), (1, 64)), jnp.float32)
    moment_two = jnp.clip(jnp.exp(math.log(9.999999747378752e-06) - 4.6051701 * jax.random.uniform(splits[7], (SECTIONS, HV, D), jnp.float32) ** level_of(splits[7], (SECTIONS, HV, D), ((0, 8), (1, 64)), -0.2, 0.2)), 1.0000000116860974e-07, 9.999999747378752e-06)
    return dict(placing=placing, acts=acts, cotan=cotan, gain=gain, w_value=w_value, w_out=w_out, moment_one=moment_one, moment_two=moment_two)


NORM_EPS = 1e-05
CLIP_NORM = 1.0
LEARN_RATE = 0.001
BETA_ONE = 0.9
BETA_TWO = 0.95
ADAM_EPS = 1e-08
DECAY = 0.1

def slot_ranks(placed):
    micro_ids = jnp.arange(placed.shape[0], dtype=jnp.int32)
    same_place = placed[:, None] == placed[None, :]
    earlier = micro_ids[None, :] < micro_ids[:, None]
    return lax.optimization_barrier(jnp.sum(jnp.where(same_place & earlier, 1, 0), axis=1)).astype(jnp.int32)

def reference(placing, acts, cotan, gain, w_value, w_out, moment_one, moment_two):
    placed = placing[:, :, 0]
    ranks = [slot_ranks(placed[section]) for section in range(SECTIONS)]
    passed = jnp.zeros(acts.shape, jnp.bfloat16)
    returned = jnp.zeros(acts.shape, jnp.bfloat16)
    gradients = []
    for section in range(SECTIONS):
        inputs = acts[section][placed[section], ranks[section]].reshape(PEERS * MB, D).astype(jnp.float32)
        cotangent = cotan[section][placed[section], ranks[section]].reshape(PEERS * MB, D)
        inverse_rms = lax.rsqrt(lax.optimization_barrier(jnp.mean(inputs * inputs, axis=1, keepdims=True)) + NORM_EPS)
        unit = inputs * inverse_rms
        gains = gain[section].astype(jnp.float32)
        normed = (unit * gains).astype(jnp.bfloat16)
        values = jnp.dot(normed, w_value[section].T, preferred_element_type=jnp.float32).astype(jnp.bfloat16)
        mixed = jnp.dot(values, w_out[section].T, preferred_element_type=jnp.float32)
        outputs = (inputs + mixed).astype(jnp.bfloat16)
        value_grads = jnp.dot(cotangent, w_out[section], preferred_element_type=jnp.float32).astype(jnp.bfloat16)
        gradients.append(jnp.dot(value_grads.T, normed, preferred_element_type=jnp.float32))
        norm_grads = jnp.dot(value_grads, w_value[section], preferred_element_type=jnp.float32)
        unit_grads = norm_grads * gains
        inner = lax.optimization_barrier(jnp.mean(unit_grads * unit, axis=1, keepdims=True))
        back = (cotangent.astype(jnp.float32) + inverse_rms * (unit_grads - unit * inner)).astype(jnp.bfloat16)
        after = (section + 1) % SECTIONS
        before = (section + SECTIONS - 1) % SECTIONS
        passed = passed.at[after, placed[after], ranks[after]].set(outputs.reshape(PEERS, MB, D))
        returned = returned.at[before, placed[before], ranks[before]].set(back.reshape(PEERS, MB, D))
    gradient = jnp.stack(gradients)
    totals = jnp.sum(gradient * gradient)
    clip_scale = jnp.minimum(1.0, CLIP_NORM / jnp.sqrt(totals + 1e-06))
    clipped = gradient * clip_scale
    first = BETA_ONE * moment_one + (1.0 - BETA_ONE) * clipped
    second = BETA_TWO * moment_two + (1.0 - BETA_TWO) * clipped * clipped
    weights = w_value.astype(jnp.float32)
    updated = weights - LEARN_RATE * (first / (jnp.sqrt(second) + ADAM_EPS) + DECAY * weights)
    return (passed, returned, updated.astype(jnp.bfloat16), first, second)
```

```python
import jax
import jax.numpy as jnp
from jax import lax
from jax.sharding import Mesh, PartitionSpec as P

NORM_EPS = 1e-05
CLIP_NORM = 1.0
LEARN_RATE = 0.001
BETA_ONE = 0.9
BETA_TWO = 0.95
ADAM_EPS = 1e-08
DECAY = 0.1
PEER = ("chip", "core")
SPARE = 8


def matmul(equation, left, right):
    return jnp.einsum(equation, left, right, preferred_element_type=jnp.float32)


def swap(blocks, axis):
    return lax.all_to_all(blocks, axis, split_axis=0, concat_axis=0, tiled=True)


def moved(block, axis, distance):
    count = lax.axis_size(axis)
    return lax.ppermute(block, axis, [(i, (i + distance) % count) for i in range(count)])


def to_all(block, count):
    return jnp.broadcast_to(block[None], (count,) + block.shape)


def three_parts(values):
    high = lax.reduce_precision(values, 8, 7)
    rest = values - high
    middle = lax.reduce_precision(rest, 8, 7)
    return [part.astype(jnp.bfloat16) for part in (high, middle, rest - middle)]


def selection(placed, capacity, micro_rows):
    count = placed.shape[0]
    ids = jnp.arange(count, dtype=jnp.int32)
    twins = (placed[:, None] == placed[None, :]) & (ids[:, None] < ids[None, :])
    slots = placed * capacity + jnp.sum(twins.astype(jnp.int32), axis=0)
    rows = (slots[:, None] * micro_rows + jnp.arange(micro_rows, dtype=jnp.int32)).reshape(-1)
    every = jnp.arange(count * capacity * micro_rows, dtype=jnp.int32)
    return (every[:, None] == rows[None, :]).astype(jnp.bfloat16)


def body(placing, acts, cotan, gain, w_value, w_out, moment_one, moment_two):
    chips = lax.axis_size("chip")
    peers = 2 * chips
    section_now = lax.axis_index("section")
    peer_now = lax.axis_index(PEER)
    _, _, capacity, micro_rows, model = acts.shape
    slot_rows = capacity * micro_rows
    width = model // peers
    heads = w_value.shape[1]
    rows = peers * micro_rows
    weights, out_weights = w_value[0], w_out[0]

    held = jnp.concatenate(
        [acts[0, 0].reshape(slot_rows, model), cotan[0, 0].reshape(slot_rows, model)]
    )
    cols = swap(held.reshape(2 * slot_rows, peers, width).transpose(1, 0, 2), PEER)
    placed = lax.dynamic_index_in_dim(placing[:, :, 0], section_now, 0, keepdims=False)
    select = selection(placed, capacity, micro_rows)
    gain_col = jnp.broadcast_to(gain[0][:, None], (model, rows))
    cols = cols.reshape(peers, 2, slot_rows, width).transpose(1, 0, 2, 3)
    stacked = matmul("ksf,sr->kfr", cols.reshape(2, peers * slot_rows, width), select)
    stream, cotangent = stacked[0].astype(jnp.bfloat16), stacked[1].astype(jnp.bfloat16)

    grads = matmul("fh,fr->hr", out_weights, cotangent).astype(jnp.bfloat16)
    grads = swap(grads.reshape(chips, 2, heads, rows).transpose(1, 0, 2, 3), "core")
    grads = jnp.sum(grads.astype(jnp.float32), axis=0).astype(jnp.bfloat16)
    first_trip = swap(jnp.concatenate([to_all(stream, chips), grads], axis=1), "chip")
    value_grads = jnp.sum(first_trip[:, width:].astype(jnp.float32), axis=0).astype(jnp.bfloat16)
    streams = lax.all_gather(first_trip[:, :width], "core", axis=1).reshape(model, rows)

    inputs = streams.astype(jnp.float32)
    inverse_rms = lax.rsqrt(jnp.mean(inputs * inputs, axis=0, keepdims=True) + NORM_EPS)
    normed = (inputs * inverse_rms * gain_col.astype(jnp.float32)).astype(jnp.bfloat16)
    values = matmul("hd,dr->hr", weights, normed)
    norm_grads = matmul("hd,hr->dr", weights, value_grads).astype(jnp.bfloat16)
    norm_grads = swap(norm_grads.reshape(chips, 2, width, rows).transpose(1, 0, 2, 3), "core")
    norm_grads = jnp.sum(norm_grads.astype(jnp.float32), axis=0).astype(jnp.bfloat16)
    gradient = matmul("hr,dr->hd", value_grads, normed)

    inner = jnp.sum(value_grads.astype(jnp.float32) * values, axis=0)
    square = jnp.broadcast_to(jnp.sum(gradient * gradient), inner.shape)
    extra = jnp.stack(three_parts(inner) + three_parts(square))
    extra = jnp.pad(extra, ((0, SPARE - extra.shape[0]), (0, 0)))
    own = jnp.concatenate([values.astype(jnp.bfloat16), extra])
    second_trip = swap(jnp.concatenate([norm_grads, to_all(own, chips)], axis=1), "chip")
    norm_grads = jnp.sum(second_trip[:, :width].astype(jnp.float32), axis=0)
    gathered = lax.all_gather(second_trip[:, width:], "core", axis=1)
    extra = jnp.sum(gathered[:, :, heads:].astype(jnp.float32), axis=(0, 1))
    inner = jnp.sum(extra[0:3], axis=0, keepdims=True) / model
    square = jnp.sum(extra[3:6], axis=0)
    squares = swap(jnp.broadcast_to(square, (lax.axis_size("section"), SPARE, rows)), "section")
    totals = jnp.sum(squares[:, 0, 0])

    mixed = matmul("fh,hr->fr", out_weights, gathered[:, :, :heads].reshape(-1, rows))
    outputs = (stream.astype(jnp.float32) + mixed).astype(jnp.bfloat16)
    own_gain = lax.dynamic_slice_in_dim(gain_col, peer_now * width, width, 0).astype(jnp.float32)
    unit = stream.astype(jnp.float32) * inverse_rms
    back = (
        cotangent.astype(jnp.float32) + inverse_rms * (norm_grads * own_gain - unit * inner)
    ).astype(jnp.bfloat16)
    arrived = jnp.stack([moved(outputs, "section", 1), moved(back, "section", -1)])

    spread = matmul("sr,kfr->ksf", select, arrived).astype(jnp.bfloat16)
    spread = spread.reshape(2, peers, slot_rows, width).transpose(1, 0, 2, 3)
    final = swap(spread.reshape(peers, 2 * slot_rows, width), PEER)
    final = final.transpose(1, 0, 2).reshape((2, 1, 1, capacity, micro_rows, model))

    clip_scale = jnp.minimum(1.0, CLIP_NORM / jnp.sqrt(totals + 1e-06))
    clipped = gradient * clip_scale
    first = BETA_ONE * moment_one[0] + (1.0 - BETA_ONE) * clipped
    second = BETA_TWO * moment_two[0] + (1.0 - BETA_TWO) * clipped * clipped
    wide = weights.astype(jnp.float32)
    updated = wide - LEARN_RATE * (first / (jnp.sqrt(second) + ADAM_EPS) + DECAY * wide)
    return final[0], final[1], updated.astype(jnp.bfloat16)[None], first[None], second[None]


def solution(mesh):
    sections, peers = mesh.devices.shape
    fine = Mesh(mesh.devices.reshape(sections, peers // 2, 2), ("section",) + PEER)
    slots = P("section", PEER, None, None, None)
    matrix = P("section", PEER, None)
    return jax.shard_map(
        body,
        mesh=fine,
        in_specs=(P(), slots, slots, P("section", None), matrix, matrix, matrix, matrix),
        out_specs=(slots, slots, matrix, matrix, matrix),
        check_vma=False,
    )
```

```python
import functools

import jax
import jax.numpy as jnp
from jax import lax
from jax.experimental import pallas as pl
from jax.experimental.pallas import tpu as pltpu
from jax.sharding import Mesh, PartitionSpec as P

NORM_EPS = 1e-05
CLIP_NORM = 1.0
LEARN_RATE = 0.001
BETA_ONE = 0.9
BETA_TWO = 0.95
ADAM_EPS = 1e-08
DECAY = 0.1
PEER = ("chip", "core")
SPARE = 8


def matmul(equation, left, right):
    return jnp.einsum(equation, left, right, preferred_element_type=jnp.float32)


def swap(blocks, axis):
    return lax.all_to_all(blocks, axis, split_axis=0, concat_axis=0, tiled=True)


def moved(block, axis, distance):
    count = lax.axis_size(axis)
    return lax.ppermute(block, axis, [(i, (i + distance) % count) for i in range(count)])


def to_all(block, count):
    return jnp.broadcast_to(block[None], (count,) + block.shape)


def selection(placed, capacity, micro_rows):
    count = placed.shape[0]
    ids = jnp.arange(count, dtype=jnp.int32)
    twins = (placed[:, None] == placed[None, :]) & (ids[:, None] < ids[None, :])
    slots = placed * capacity + jnp.sum(twins.astype(jnp.int32), axis=0)
    rows = (slots[:, None] * micro_rows + jnp.arange(micro_rows, dtype=jnp.int32)).reshape(-1)
    every = jnp.arange(count * capacity * micro_rows, dtype=jnp.int32)
    return (every[:, None] == rows[None, :]).astype(jnp.bfloat16)


def on_core(kernel, out_shape, scalars, arrays, scratch=(), flops=0):
    size = sum(a.size * a.dtype.itemsize for a in arrays)
    size += sum(o.size * o.dtype.itemsize for o in out_shape)
    return pl.pallas_call(
        kernel,
        out_shape=out_shape,
        in_specs=[pl.BlockSpec(memory_space=pltpu.SMEM)] * len(scalars)
        + [pl.BlockSpec(memory_space=pltpu.VMEM)] * len(arrays),
        out_specs=[pl.BlockSpec(memory_space=pltpu.VMEM)] * len(out_shape),
        scratch_shapes=list(scratch),
        compiler_params=pltpu.CompilerParams(vmem_limit_bytes=24 * 2**20),
        cost_estimate=pl.CostEstimate(flops=flops, bytes_accessed=size, transcendentals=0),
    )(*scalars, *arrays)


def dnormed_kernel(width, heads, core_ref, trip_ref, weight_ref, grads_ref, mine_ref, other_ref):
    chips = trip_ref.shape[0]
    total = trip_ref[0, width : width + heads, :].astype(jnp.float32)
    for chip in range(1, chips):
        total += trip_ref[chip, width : width + heads, :].astype(jnp.float32)
    grads = total.astype(jnp.bfloat16)
    grads_ref[...] = grads
    first_core = core_ref[0] == 0
    group = 4
    span = group * 2 * width
    for step in range(chips // group):
        part = lax.dot_general(
            weight_ref[:, step * span : (step + 1) * span],
            grads,
            (((0,), (0,)), ((), ())),
            preferred_element_type=jnp.float32,
        )
        for local in range(group):
            low = part[2 * local * width : (2 * local + 1) * width]
            high = part[(2 * local + 1) * width : (2 * local + 2) * width]
            chip = step * group + local
            mine_ref[chip] = jnp.where(first_core, low, high).astype(jnp.bfloat16)
            other_ref[chip] = jnp.where(first_core, high, low).astype(jnp.bfloat16)


def parts_of(values):
    high = values.astype(jnp.bfloat16).astype(jnp.float32)
    middle = (values - high).astype(jnp.bfloat16).astype(jnp.float32)
    return [high, middle, values - high - middle]


def values_kernel(
    width, heads, core_ref, mine_ref, other_ref, gain_ref, weight_ref, grads_ref,
    own_ref, gradient_ref, inverse_ref, normed_ref,
):
    chips = mine_ref.shape[0]
    model = 2 * chips * width
    squares = jnp.zeros((width, mine_ref.shape[2]), jnp.float32)
    for chip in range(chips):
        for ref in (mine_ref, other_ref):
            block = ref[chip, :width, :].astype(jnp.float32)
            squares += block * block
    mean = jnp.sum(squares, axis=0, keepdims=True) / model
    inverse = lax.rsqrt(mean + NORM_EPS)
    inverse_ref[...] = jnp.broadcast_to(inverse, inverse_ref.shape)
    first_core = core_ref[0] == 0
    for chip in range(chips):
        mine, other = mine_ref[chip, :width, :], other_ref[chip, :width, :]
        for core, block in ((0, jnp.where(first_core, mine, other)), (1, jnp.where(first_core, other, mine))):
            at = (2 * chip + core) * width
            unit = block.astype(jnp.float32) * inverse
            scaled = unit * gain_ref[at : at + width, :].astype(jnp.float32)
            normed_ref[at : at + width, :] = scaled.astype(jnp.bfloat16)
    values = jnp.dot(weight_ref[...], normed_ref[...], preferred_element_type=jnp.float32)
    grads = grads_ref[...]
    span = 8 * width
    lanes = mine_ref.shape[2]
    norms = jnp.zeros((heads, lanes), jnp.float32)
    for step in range(model // span):
        block = lax.dot_general(
            grads,
            normed_ref[step * span : (step + 1) * span, :],
            (((1,), (1,)), ((), ())),
            preferred_element_type=jnp.float32,
        )
        gradient_ref[:, step * span : (step + 1) * span] = block
        for lane in range(span // lanes):
            piece = block[:, lane * lanes : (lane + 1) * lanes]
            norms += piece * piece
    inner = jnp.sum(grads.astype(jnp.float32) * values, axis=0, keepdims=True)
    norm = jnp.sum(norms, axis=0, keepdims=True)
    line = lax.broadcasted_iota(jnp.int32, (SPARE, values.shape[1]), 0)
    extra = jnp.zeros((SPARE, values.shape[1]), jnp.float32)
    for index, part in enumerate(parts_of(inner) + parts_of(norm)):
        extra = jnp.where(line == index, part, extra)
    own_ref[...] = jnp.concatenate([values, extra], axis=0).astype(jnp.bfloat16)


def payload_kernel(width, mine_ref, arrived_ref, own_ref, out_ref):
    own = own_ref[...]
    for chip in range(mine_ref.shape[0]):
        block = mine_ref[chip].astype(jnp.float32) + arrived_ref[chip].astype(jnp.float32)
        out_ref[chip, :width, :] = block.astype(jnp.bfloat16)
        out_ref[chip, width:, :] = own


def body(placing, acts, cotan, gain, w_value, w_out, moment_one, moment_two):
    chips = lax.axis_size("chip")
    peers = 2 * chips
    section_now = lax.axis_index("section")
    peer_now = lax.axis_index(PEER)
    _, _, capacity, micro_rows, model = acts.shape
    slot_rows = capacity * micro_rows
    width = model // peers
    heads = w_value.shape[1]
    rows = peers * micro_rows
    weights, out_weights = w_value[0], w_out[0]

    held = jnp.concatenate(
        [acts[0, 0].reshape(slot_rows, model), cotan[0, 0].reshape(slot_rows, model)]
    )
    cols = swap(held.reshape(2 * slot_rows, peers, width).transpose(1, 0, 2), PEER)
    placed = lax.dynamic_index_in_dim(placing[:, :, 0], section_now, 0, keepdims=False)
    select = selection(placed, capacity, micro_rows)
    gain_col = jnp.broadcast_to(gain[0][:, None], (model, rows))
    own_gain = lax.dynamic_slice_in_dim(gain_col, peer_now * width, width, 0)
    cols = cols.reshape(peers, 2, slot_rows, width).transpose(1, 0, 2, 3)
    stacked = matmul("ksf,sr->kfr", cols.reshape(2, peers * slot_rows, width), select)
    stream, cotangent = stacked[0].astype(jnp.bfloat16), stacked[1].astype(jnp.bfloat16)

    grads = matmul("fh,fr->hr", out_weights, cotangent).astype(jnp.bfloat16)
    grads = swap(grads.reshape(chips, 2, heads, rows).transpose(1, 0, 2, 3), "core")
    grads = jnp.sum(grads.astype(jnp.float32), axis=0).astype(jnp.bfloat16)
    first_trip = swap(jnp.concatenate([to_all(stream, chips), grads], axis=1), "chip")
    core = lax.axis_index("core").astype(jnp.int32).reshape(1)
    other_trip = moved(first_trip, "core", 1)
    brief, full = jnp.bfloat16, jnp.float32
    half = jax.ShapeDtypeStruct((chips, width, rows), brief)
    value_grads, mine, other = on_core(
        functools.partial(dnormed_kernel, width, heads),
        [jax.ShapeDtypeStruct((heads, rows), brief), half, half],
        [core],
        [first_trip, weights],
        flops=2 * model * heads * rows,
    )
    arrived = moved(other, "core", 1)
    own, gradient, inverse = on_core(
        functools.partial(values_kernel, width, heads),
        [
            jax.ShapeDtypeStruct((heads + SPARE, rows), brief),
            jax.ShapeDtypeStruct((heads, model), full),
            jax.ShapeDtypeStruct((SPARE, rows), full),
        ],
        [core],
        [first_trip, other_trip, gain_col, weights, value_grads],
        [pltpu.VMEM((model, rows), brief)],
        flops=4 * model * heads * rows,
    )
    (payload,) = on_core(
        functools.partial(payload_kernel, width),
        [jax.ShapeDtypeStruct((chips, width + heads + SPARE, rows), brief)],
        [],
        [mine, arrived, own],
    )
    inverse_rms = inverse[:1]
    payload, own_gain, inverse_rms = lax.optimization_barrier((payload, own_gain, inverse_rms))
    second_trip = swap(payload, "chip")
    norm_grads = jnp.sum(second_trip[:, :width].astype(jnp.float32), axis=0)
    gathered = lax.all_gather(second_trip[:, width:], "core", axis=1)
    extra = jnp.sum(gathered[:, :, heads:].astype(jnp.float32), axis=(0, 1))
    inner = jnp.sum(extra[0:3], axis=0, keepdims=True) / model
    square = jnp.sum(extra[3:6], axis=0, keepdims=True)
    sections = lax.axis_size("section")
    distance = 1
    while distance < sections:
        route = [(i, i ^ distance) for i in range(sections)]
        square = square + lax.ppermute(square, "section", route)
        distance *= 2
    totals = jnp.sum(square)

    mixed = matmul("fh,hr->fr", out_weights, gathered[:, :, :heads].reshape(-1, rows))
    outputs = (stream.astype(jnp.float32) + mixed).astype(jnp.bfloat16)
    unit = stream.astype(jnp.float32) * inverse_rms
    back = (
        cotangent.astype(jnp.float32) + inverse_rms * (norm_grads * own_gain.astype(jnp.float32) - unit * inner)
    ).astype(jnp.bfloat16)
    arrived = jnp.stack([moved(outputs, "section", 1), moved(back, "section", -1)])

    spread = matmul("sr,kfr->ksf", select, arrived).astype(jnp.bfloat16)
    spread = spread.reshape(2, peers, slot_rows, width).transpose(1, 0, 2, 3)
    final = swap(spread.reshape(peers, 2 * slot_rows, width), PEER)
    final = final.transpose(1, 0, 2).reshape((2, 1, 1, capacity, micro_rows, model))

    clip_scale = jnp.minimum(1.0, CLIP_NORM / jnp.sqrt(totals + 1e-06))
    clipped = gradient * clip_scale
    first = BETA_ONE * moment_one[0] + (1.0 - BETA_ONE) * clipped
    second = BETA_TWO * moment_two[0] + (1.0 - BETA_TWO) * clipped * clipped
    wide = weights.astype(jnp.float32)
    updated = wide - LEARN_RATE * (first / (jnp.sqrt(second) + ADAM_EPS) + DECAY * wide)
    return final[0], final[1], updated.astype(jnp.bfloat16)[None], first[None], second[None]


def solution(mesh):
    sections, peers = mesh.devices.shape
    fine = Mesh(mesh.devices.reshape(sections, peers // 2, 2), ("section",) + PEER)
    slots = P("section", PEER, None, None, None)
    matrix = P("section", PEER, None)
    return jax.shard_map(
        body,
        mesh=fine,
        in_specs=(P(), slots, slots, P("section", None), matrix, matrix, matrix, matrix),
        out_specs=(slots, slots, matrix, matrix, matrix),
        check_vma=False,
    )
```

```python
import functools

import jax
import jax.numpy as jnp
from jax import lax
from jax.experimental import pallas as pl
from jax.experimental.pallas import tpu as pltpu
from jax.sharding import Mesh, PartitionSpec as P

NORM_EPS = 1e-05
CLIP_NORM = 1.0
LEARN_RATE = 0.001
BETA_ONE = 0.9
BETA_TWO = 0.95
ADAM_EPS = 1e-08
DECAY = 0.1
PEER = ("chip", "core")
SPARE = 8


def matmul(equation, left, right):
    return jnp.einsum(equation, left, right, preferred_element_type=jnp.float32)


def swap(blocks, axis):
    return lax.all_to_all(blocks, axis, split_axis=0, concat_axis=0, tiled=True)


def moved(block, axis, distance):
    count = lax.axis_size(axis)
    return lax.ppermute(block, axis, [(i, (i + distance) % count) for i in range(count)])


def to_all(block, count):
    return jnp.broadcast_to(block[None], (count,) + block.shape)


def selection(placed, capacity, micro_rows):
    count = placed.shape[0]
    ids = jnp.arange(count, dtype=jnp.int32)
    twins = (placed[:, None] == placed[None, :]) & (ids[:, None] < ids[None, :])
    slots = placed * capacity + jnp.sum(twins.astype(jnp.int32), axis=0)
    rows = (slots[:, None] * micro_rows + jnp.arange(micro_rows, dtype=jnp.int32)).reshape(-1)
    every = jnp.arange(count * capacity * micro_rows, dtype=jnp.int32)
    return (every[:, None] == rows[None, :]).astype(jnp.bfloat16)


def on_core(kernel, out_shape, scalars, arrays, scratch=(), flops=0):
    size = sum(a.size * a.dtype.itemsize for a in arrays)
    size += sum(o.size * o.dtype.itemsize for o in out_shape)
    return pl.pallas_call(
        kernel,
        out_shape=out_shape,
        in_specs=[pl.BlockSpec(memory_space=pltpu.SMEM)] * len(scalars)
        + [pl.BlockSpec(memory_space=pltpu.VMEM)] * len(arrays),
        out_specs=[pl.BlockSpec(memory_space=pltpu.VMEM)] * len(out_shape),
        scratch_shapes=list(scratch),
        compiler_params=pltpu.CompilerParams(vmem_limit_bytes=24 * 2**20),
        cost_estimate=pl.CostEstimate(flops=flops, bytes_accessed=size, transcendentals=0),
    )(*scalars, *arrays)


def dnormed_kernel(width, heads, core_ref, trip_ref, weight_ref, grads_ref, mine_ref, other_ref):
    chips = trip_ref.shape[0]
    total = trip_ref[0, width : width + heads, :].astype(jnp.float32)
    for chip in range(1, chips):
        total += trip_ref[chip, width : width + heads, :].astype(jnp.float32)
    grads = total.astype(jnp.bfloat16)
    grads_ref[...] = grads
    first_core = core_ref[0] == 0
    group = 4
    span = group * 2 * width
    for step in range(chips // group):
        part = lax.dot_general(
            weight_ref[:, step * span : (step + 1) * span],
            grads,
            (((0,), (0,)), ((), ())),
            preferred_element_type=jnp.float32,
        )
        for local in range(group):
            low = part[2 * local * width : (2 * local + 1) * width]
            high = part[(2 * local + 1) * width : (2 * local + 2) * width]
            chip = step * group + local
            mine_ref[chip] = jnp.where(first_core, low, high).astype(jnp.bfloat16)
            other_ref[chip] = jnp.where(first_core, high, low).astype(jnp.bfloat16)


def split_kernel(acts_ref, cotan_ref, out_ref):
    peers, _, width = out_ref.shape
    _, _, capacity, _, _ = acts_ref.shape
    held = [ref[0, 0, slot] for ref in (acts_ref, cotan_ref) for slot in range(capacity)]
    held = jnp.concatenate([rows.astype(jnp.float32) for rows in held], axis=0)
    for peer in range(peers):
        out_ref[peer] = held[:, peer * width : (peer + 1) * width].astype(jnp.bfloat16)


def join_kernel(trip_ref, passed_ref, returned_ref, rows_ref):
    peers, _, width = trip_ref.shape
    _, _, capacity, micro_rows, _ = passed_ref.shape
    for peer in range(peers):
        rows_ref[:, peer * width : (peer + 1) * width] = trip_ref[peer].astype(jnp.float32)
    at = 0
    for ref in (passed_ref, returned_ref):
        for slot in range(capacity):
            ref[0, 0, slot] = rows_ref[at : at + micro_rows, :].astype(jnp.bfloat16)
            at += micro_rows


def parts_of(values):
    high = lax.reduce_precision(values, 8, 7)
    middle = lax.reduce_precision(values - high, 8, 7)
    return [high, middle, values - high - middle]


def values_kernel(
    width, heads, core_ref, mine_ref, other_ref, gain_ref, weight_ref, grads_ref,
    own_ref, gradient_ref, inverse_ref, normed_ref,
):
    chips = mine_ref.shape[0]
    model = 2 * chips * width
    squares = jnp.zeros((width, mine_ref.shape[2]), jnp.float32)
    for chip in range(chips):
        for ref in (mine_ref, other_ref):
            block = ref[chip, :width, :].astype(jnp.float32)
            squares += block * block
    mean = jnp.sum(squares, axis=0, keepdims=True) / model
    inverse = lax.rsqrt(mean + NORM_EPS)
    inverse_ref[...] = jnp.broadcast_to(inverse, inverse_ref.shape)
    first_core = core_ref[0] == 0
    for chip in range(chips):
        mine, other = mine_ref[chip, :width, :], other_ref[chip, :width, :]
        for core, block in ((0, jnp.where(first_core, mine, other)), (1, jnp.where(first_core, other, mine))):
            at = (2 * chip + core) * width
            unit = block.astype(jnp.float32) * inverse
            scaled = unit * gain_ref[at : at + width, :].astype(jnp.float32)
            normed_ref[at : at + width, :] = scaled.astype(jnp.bfloat16)
    values = jnp.dot(weight_ref[...], normed_ref[...], preferred_element_type=jnp.float32)
    grads = grads_ref[...]
    span = 8 * width
    lanes = mine_ref.shape[2]
    norms = jnp.zeros((heads, lanes), jnp.float32)
    for step in range(model // span):
        block = lax.dot_general(
            grads,
            normed_ref[step * span : (step + 1) * span, :],
            (((1,), (1,)), ((), ())),
            preferred_element_type=jnp.float32,
        )
        gradient_ref[:, step * span : (step + 1) * span] = block
        for lane in range(span // lanes):
            piece = block[:, lane * lanes : (lane + 1) * lanes]
            norms += piece * piece
    inner = jnp.sum(grads.astype(jnp.float32) * values, axis=0, keepdims=True)
    norm = jnp.sum(norms, axis=0, keepdims=True)
    line = lax.broadcasted_iota(jnp.int32, (SPARE, values.shape[1]), 0)
    extra = jnp.zeros((SPARE, values.shape[1]), jnp.float32)
    for index, part in enumerate(parts_of(inner) + parts_of(norm)):
        extra = jnp.where(line == index, part, extra)
    own_ref[...] = jnp.concatenate([values, extra], axis=0).astype(jnp.bfloat16)


def payload_kernel(width, mine_ref, arrived_ref, own_ref, out_ref):
    own = own_ref[...]
    for chip in range(mine_ref.shape[0]):
        block = mine_ref[chip].astype(jnp.float32) + arrived_ref[chip].astype(jnp.float32)
        out_ref[chip, :width, :] = block.astype(jnp.bfloat16)
        out_ref[chip, width:, :] = own


def body(placing, acts, cotan, gain, w_value, w_out, moment_one, moment_two):
    chips = lax.axis_size("chip")
    peers = 2 * chips
    section_now = lax.axis_index("section")
    peer_now = lax.axis_index(PEER)
    _, _, capacity, micro_rows, model = acts.shape
    slot_rows = capacity * micro_rows
    width = model // peers
    heads = w_value.shape[1]
    rows = peers * micro_rows
    weights, out_weights = w_value[0], w_out[0]

    (held,) = on_core(
        split_kernel,
        [jax.ShapeDtypeStruct((peers, 2 * slot_rows, width), jnp.bfloat16)],
        [],
        [acts, cotan],
    )
    cols = swap(held, PEER)
    placed = lax.dynamic_index_in_dim(placing[:, :, 0], section_now, 0, keepdims=False)
    select = selection(placed, capacity, micro_rows)
    gain_col = jnp.broadcast_to(gain[0][:, None], (model, rows))
    own_gain = lax.dynamic_slice_in_dim(gain_col, peer_now * width, width, 0)
    cols, gain_col, own_gain = lax.optimization_barrier((cols, gain_col, own_gain))
    cols = cols.reshape(peers, 2, slot_rows, width).transpose(1, 0, 2, 3)
    stacked = matmul("ksf,sr->kfr", cols.reshape(2, peers * slot_rows, width), select)
    stream, cotangent = stacked[0].astype(jnp.bfloat16), stacked[1].astype(jnp.bfloat16)

    grads = matmul("fh,fr->hr", out_weights, cotangent).astype(jnp.bfloat16)
    grads = swap(grads.reshape(chips, 2, heads, rows).transpose(1, 0, 2, 3), "core")
    grads = jnp.sum(grads.astype(jnp.float32), axis=0).astype(jnp.bfloat16)
    first_trip = swap(jnp.concatenate([to_all(stream, chips), grads], axis=1), "chip")
    core = lax.axis_index("core").astype(jnp.int32).reshape(1)
    other_trip = moved(first_trip, "core", 1)
    brief, full = jnp.bfloat16, jnp.float32
    half = jax.ShapeDtypeStruct((chips, width, rows), brief)
    value_grads, mine, other = on_core(
        functools.partial(dnormed_kernel, width, heads),
        [jax.ShapeDtypeStruct((heads, rows), brief), half, half],
        [core],
        [first_trip, weights],
        flops=2 * model * heads * rows,
    )
    arrived = moved(other, "core", 1)
    own, gradient, inverse = on_core(
        functools.partial(values_kernel, width, heads),
        [
            jax.ShapeDtypeStruct((heads + SPARE, rows), brief),
            jax.ShapeDtypeStruct((heads, model), full),
            jax.ShapeDtypeStruct((SPARE, rows), full),
        ],
        [core],
        [first_trip, other_trip, gain_col, weights, value_grads],
        [pltpu.VMEM((model, rows), brief)],
        flops=4 * model * heads * rows,
    )
    (payload,) = on_core(
        functools.partial(payload_kernel, width),
        [jax.ShapeDtypeStruct((chips, width + heads + SPARE, rows), brief)],
        [],
        [mine, arrived, own],
    )
    inverse_rms = inverse[:1]
    second_trip = swap(payload, "chip")
    norm_grads = jnp.sum(second_trip[:, :width].astype(jnp.float32), axis=0)
    gathered = lax.all_gather(second_trip[:, width:], "core", axis=1)
    extra = jnp.sum(gathered[:, :, heads:].astype(jnp.float32), axis=(0, 1))
    inner = jnp.sum(extra[0:3], axis=0, keepdims=True) / model
    square = jnp.sum(extra[3:6], axis=0, keepdims=True)
    mixed = matmul("fh,hr->fr", out_weights, gathered[:, :, :heads].reshape(-1, rows))
    outputs = (stream.astype(jnp.float32) + mixed).astype(jnp.bfloat16)
    unit = stream.astype(jnp.float32) * inverse_rms
    back = (
        cotangent.astype(jnp.float32) + inverse_rms * (norm_grads * own_gain.astype(jnp.float32) - unit * inner)
    ).astype(jnp.bfloat16)

    sections = lax.axis_size("section")
    parts = jnp.concatenate(parts_of(square)).astype(jnp.bfloat16)
    parts = jnp.pad(parts, ((0, SPARE - parts.shape[0]), (0, 0)))
    ahead = jnp.arange(sections)[:, None, None] == (section_now + 1) % sections
    both = jnp.where(ahead, jnp.concatenate([outputs, parts]), jnp.concatenate([back, parts]))
    third_trip = swap(both, "section")
    totals = jnp.sum(third_trip[:, width : width + 3].astype(jnp.float32))
    behind = [(section_now + sections - 1) % sections, (section_now + 1) % sections]
    arrived = jnp.stack(
        [lax.dynamic_index_in_dim(third_trip, at, 0, keepdims=False)[:width] for at in behind]
    )

    spread = matmul("sr,kfr->ksf", select, arrived).astype(jnp.bfloat16)
    spread = spread.reshape(2, peers, slot_rows, width).transpose(1, 0, 2, 3)
    final = swap(spread.reshape(peers, 2 * slot_rows, width), PEER)
    passed, returned = on_core(
        join_kernel,
        [jax.ShapeDtypeStruct(acts.shape, brief)] * 2,
        [],
        [final],
        [pltpu.VMEM((2 * slot_rows, model), full)],
    )

    clip_scale = jnp.minimum(1.0, CLIP_NORM / jnp.sqrt(totals + 1e-06))
    clipped = gradient * clip_scale
    first = BETA_ONE * moment_one[0] + (1.0 - BETA_ONE) * clipped
    second = BETA_TWO * moment_two[0] + (1.0 - BETA_TWO) * clipped * clipped
    wide = weights.astype(jnp.float32)
    updated = wide - LEARN_RATE * (first / (jnp.sqrt(second) + ADAM_EPS) + DECAY * wide)
    return passed, returned, updated.astype(jnp.bfloat16)[None], first[None], second[None]


def solution(mesh):
    sections, peers = mesh.devices.shape
    fine = Mesh(mesh.devices.reshape(sections, peers // 2, 2), ("section",) + PEER)
    slots = P("section", PEER, None, None, None)
    matrix = P("section", PEER, None)
    return jax.shard_map(
        body,
        mesh=fine,
        in_specs=(P(), slots, slots, P("section", None), matrix, matrix, matrix, matrix),
        out_specs=(slots, slots, matrix, matrix, matrix),
        check_vma=False,
    )
```

```python
import functools

import jax
import jax.numpy as jnp
from jax import lax
from jax.experimental import pallas as pl
from jax.experimental.pallas import tpu as pltpu
from jax.sharding import Mesh, PartitionSpec as P

NORM_EPS = 1e-05
CLIP_NORM = 1.0
LEARN_RATE = 0.001
BETA_ONE = 0.9
BETA_TWO = 0.95
ADAM_EPS = 1e-08
DECAY = 0.1
PEER = ("chip", "core")
SPARE = 8


def matmul(equation, left, right):
    return jnp.einsum(equation, left, right, preferred_element_type=jnp.float32)


def swap(blocks, axis):
    return lax.all_to_all(blocks, axis, split_axis=0, concat_axis=0, tiled=True)


def moved(block, axis, distance):
    count = lax.axis_size(axis)
    return lax.ppermute(block, axis, [(i, (i + distance) % count) for i in range(count)])


def to_all(block, count):
    return jnp.broadcast_to(block[None], (count,) + block.shape)


def slot_rows_of(placed, capacity, micro_rows):
    ids = jnp.arange(placed.shape[0], dtype=jnp.int32)
    twins = (placed[:, None] == placed[None, :]) & (ids[:, None] < ids[None, :])
    slots = placed * capacity + jnp.sum(twins.astype(jnp.int32), axis=0)
    return (slots[:, None] * micro_rows + jnp.arange(micro_rows, dtype=jnp.int32)).reshape(-1)


def on_core(kernel, out_shape, scalars, arrays, scratch=(), flops=0, held_in=pltpu.VMEM):
    size = sum(a.size * a.dtype.itemsize for a in arrays)
    size += sum(o.size * o.dtype.itemsize for o in out_shape)
    return pl.pallas_call(
        kernel,
        out_shape=out_shape,
        in_specs=[pl.BlockSpec(memory_space=pltpu.SMEM)] * len(scalars)
        + [pl.BlockSpec(memory_space=held_in)] * len(arrays),
        out_specs=[pl.BlockSpec(memory_space=pltpu.VMEM)] * len(out_shape),
        scratch_shapes=list(scratch),
        compiler_params=pltpu.CompilerParams(vmem_limit_bytes=24 * 2**20),
        cost_estimate=pl.CostEstimate(flops=flops, bytes_accessed=size, transcendentals=0),
    )(*scalars, *arrays)


def dnormed_kernel(width, heads, core_ref, trip_ref, weight_ref, grads_ref, mine_ref, other_ref):
    chips = trip_ref.shape[0]
    total = trip_ref[0, width : width + heads, :].astype(jnp.float32)
    for chip in range(1, chips):
        total += trip_ref[chip, width : width + heads, :].astype(jnp.float32)
    grads = total.astype(jnp.bfloat16)
    grads_ref[...] = grads
    first_core = core_ref[0] == 0
    group = 4
    span = group * 2 * width
    for step in range(chips // group):
        part = lax.dot_general(
            weight_ref[:, step * span : (step + 1) * span],
            grads,
            (((0,), (0,)), ((), ())),
            preferred_element_type=jnp.float32,
        )
        for local in range(group):
            low = part[2 * local * width : (2 * local + 1) * width]
            high = part[(2 * local + 1) * width : (2 * local + 2) * width]
            chip = step * group + local
            mine_ref[chip] = jnp.where(first_core, low, high).astype(jnp.bfloat16)
            other_ref[chip] = jnp.where(first_core, high, low).astype(jnp.bfloat16)


def split_kernel(acts_ref, cotan_ref, out_ref, acts_here, cotan_here, arrived):
    chips, _, width = out_ref.shape
    pairs = ((acts_ref, acts_here), (cotan_ref, cotan_here))
    copies = [pltpu.make_async_copy(a, b, arrived.at[n]) for n, (a, b) in enumerate(pairs)]
    for copy in copies:
        copy.start()
    for copy in copies:
        copy.wait()
    capacity = acts_here.shape[2]
    held = [ref[0, 0, slot] for ref in (acts_here, cotan_here) for slot in range(capacity)]
    held = jnp.concatenate([rows.astype(jnp.float32) for rows in held], axis=0)
    for chip in range(chips):
        out_ref[chip] = held[:, chip * width : (chip + 1) * width].astype(jnp.bfloat16)


def features_kernel(
    heads, core_ref, cols_ref, at_ref, weight_ref, other_weight_ref,
    out_ref, stream_ref, cotangent_ref,
):
    chips = out_ref.shape[0]
    width, rows = stream_ref.shape
    slot_rows = cols_ref.shape[0] // (4 * chips)
    first_core = core_ref[0] == 0
    line = lax.broadcasted_iota(jnp.int32, (cols_ref.shape[0], rows), 0)
    cols = cols_ref[...]

    def picked(first):
        select = (line == at_ref[...] + first).astype(jnp.float32).astype(jnp.bfloat16)
        both = lax.dot_general(
            cols, select, (((0,), (0,)), ((), ())), preferred_element_type=jnp.float32
        )
        low, high = both[:width], both[width:]
        own = jnp.where(first_core, low, high).astype(jnp.bfloat16)
        return own, jnp.where(first_core, high, low).astype(jnp.bfloat16)

    stream, _ = picked(0)
    cotangent, other_cotangent = picked(slot_rows)
    stream_ref[...] = stream
    cotangent_ref[...] = cotangent
    group = min(8, chips)
    span = group * 2 * heads
    for step in range(chips // group):
        part = sum(
            lax.dot_general(
                ref[:, step * span : (step + 1) * span],
                block,
                (((0,), (0,)), ((), ())),
                preferred_element_type=jnp.float32,
            )
            for ref, block in ((weight_ref, cotangent), (other_weight_ref, other_cotangent))
        )
        for local in range(group):
            low = part[2 * local * heads : (2 * local + 1) * heads]
            high = part[(2 * local + 1) * heads : (2 * local + 2) * heads]
            chip = step * group + local
            mine = jnp.where(first_core, low, high).astype(jnp.bfloat16)
            out_ref[chip] = jnp.concatenate([stream, mine], axis=0)


def join_kernel(trip_ref, passed_ref, returned_ref, rows_ref):
    peers, _, width = trip_ref.shape
    _, _, capacity, micro_rows, _ = passed_ref.shape
    for peer in range(peers):
        rows_ref[:, peer * width : (peer + 1) * width] = trip_ref[peer].astype(jnp.float32)
    at = 0
    for ref in (passed_ref, returned_ref):
        for slot in range(capacity):
            ref[0, 0, slot] = rows_ref[at : at + micro_rows, :].astype(jnp.bfloat16)
            at += micro_rows


def parts_of(values):
    high = lax.reduce_precision(values, 8, 7)
    middle = lax.reduce_precision(values - high, 8, 7)
    return [high, middle, values - high - middle]


def values_kernel(
    width, heads, core_ref, mine_ref, other_ref, gain_ref, weight_ref, grads_ref,
    own_ref, gradient_ref, inverse_ref, normed_ref,
):
    chips = mine_ref.shape[0]
    model = 2 * chips * width
    squares = jnp.zeros((width, mine_ref.shape[2]), jnp.float32)
    for chip in range(chips):
        for ref in (mine_ref, other_ref):
            block = ref[chip, :width, :].astype(jnp.float32)
            squares += block * block
    mean = jnp.sum(squares, axis=0, keepdims=True) / model
    inverse = lax.rsqrt(mean + NORM_EPS)
    inverse_ref[...] = jnp.broadcast_to(inverse, inverse_ref.shape)
    first_core = core_ref[0] == 0
    lanes = mine_ref.shape[2]
    one = (lax.broadcasted_iota(jnp.int32, (16, lanes), 0) == 0).astype(jnp.float32)
    group = 4
    span = group * 2 * width
    for step in range(chips // group):
        gains = jnp.broadcast_to(gain_ref[:, step * span : (step + 1) * span], (16, span))
        gains = lax.dot_general(
            gains,
            one.astype(jnp.bfloat16),
            (((0,), (0,)), ((), ())),
            preferred_element_type=jnp.float32,
        )
        for local in range(group):
            mine, other = (ref[step * group + local, :width, :] for ref in (mine_ref, other_ref))
            low, high = jnp.where(first_core, mine, other), jnp.where(first_core, other, mine)
            for core, block in ((0, low), (1, high)):
                at = (2 * local + core) * width
                scaled = block.astype(jnp.float32) * inverse * gains[at : at + width]
                normed_ref[pl.ds(step * span + at, width), :] = scaled.astype(jnp.bfloat16)
    values = jnp.dot(weight_ref[...], normed_ref[...], preferred_element_type=jnp.float32)
    grads = grads_ref[...]
    span = 8 * width
    norms = jnp.zeros((heads, lanes), jnp.float32)
    for step in range(model // span):
        block = lax.dot_general(
            grads,
            normed_ref[step * span : (step + 1) * span, :],
            (((1,), (1,)), ((), ())),
            preferred_element_type=jnp.float32,
        )
        gradient_ref[:, step * span : (step + 1) * span] = block
        for lane in range(span // lanes):
            piece = block[:, lane * lanes : (lane + 1) * lanes]
            norms += piece * piece
    inner = jnp.sum(grads.astype(jnp.float32) * values, axis=0, keepdims=True)
    norm = jnp.sum(norms, axis=0, keepdims=True)
    line = lax.broadcasted_iota(jnp.int32, (SPARE, values.shape[1]), 0)
    extra = jnp.zeros((SPARE, values.shape[1]), jnp.float32)
    for index, part in enumerate(parts_of(inner) + parts_of(norm)):
        extra = jnp.where(line == index, part, extra)
    own_ref[...] = jnp.concatenate([values, extra], axis=0).astype(jnp.bfloat16)


def payload_kernel(width, mine_ref, arrived_ref, own_ref, out_ref):
    own = own_ref[...]
    for chip in range(mine_ref.shape[0]):
        block = mine_ref[chip].astype(jnp.float32) + arrived_ref[chip].astype(jnp.float32)
        out_ref[chip, :width, :] = block.astype(jnp.bfloat16)
        out_ref[chip, width:, :] = own


def body(placing, acts, cotan, gain, w_value, w_out, moment_one, moment_two):
    chips = lax.axis_size("chip")
    peers = 2 * chips
    section_now = lax.axis_index("section")
    peer_now = lax.axis_index(PEER)
    _, _, capacity, micro_rows, model = acts.shape
    slot_rows = capacity * micro_rows
    width = model // peers
    heads = w_value.shape[1]
    rows = peers * micro_rows
    weights, out_weights = w_value[0], w_out[0]

    core = lax.axis_index("core").astype(jnp.int32).reshape(1)
    brief, full = jnp.bfloat16, jnp.float32
    (held,) = on_core(
        split_kernel,
        [jax.ShapeDtypeStruct((chips, 2 * slot_rows, 2 * width), brief)],
        [],
        [acts, cotan],
        [pltpu.VMEM(acts.shape, brief), pltpu.VMEM(cotan.shape, brief), pltpu.SemaphoreType.DMA((2,))],
        held_in=pltpu.HBM,
    )
    other_out_weights = moved(out_weights, "core", 1)
    cols = swap(held, "chip")
    placed = lax.dynamic_index_in_dim(placing[:, :, 0], section_now, 0, keepdims=False)
    slots = slot_rows_of(placed, capacity, micro_rows)
    holder = slots // slot_rows
    at = ((holder % 2) * chips + holder // 2) * (2 * slot_rows) + slots % slot_rows
    own_gain = lax.dynamic_slice_in_dim(gain[0], peer_now * width, width, 0).astype(full)
    own_gain = jnp.broadcast_to(own_gain[:, None], (width, rows))
    cols, at, slots, own_gain = lax.optimization_barrier((cols, at, slots, own_gain))
    cols = lax.all_gather(cols, "core", axis=0).reshape(peers * 2 * slot_rows, 2 * width)

    payload, stream, cotangent = on_core(
        functools.partial(features_kernel, heads),
        [
            jax.ShapeDtypeStruct((chips, width + heads, rows), brief),
            jax.ShapeDtypeStruct((width, rows), brief),
            jax.ShapeDtypeStruct((width, rows), brief),
        ],
        [core],
        [cols, at[None], out_weights, other_out_weights],
        flops=4 * heads * peers * width * rows,
    )
    first_trip = swap(payload, "chip")
    other_trip = moved(first_trip, "core", 1)
    half = jax.ShapeDtypeStruct((chips, width, rows), brief)
    value_grads, mine, other = on_core(
        functools.partial(dnormed_kernel, width, heads),
        [jax.ShapeDtypeStruct((heads, rows), brief), half, half],
        [core],
        [first_trip, weights],
        flops=2 * model * heads * rows,
    )
    arrived = moved(other, "core", 1)
    own, gradient, inverse = on_core(
        functools.partial(values_kernel, width, heads),
        [
            jax.ShapeDtypeStruct((heads + SPARE, rows), brief),
            jax.ShapeDtypeStruct((heads, model), full),
            jax.ShapeDtypeStruct((SPARE, rows), full),
        ],
        [core],
        [first_trip, other_trip, gain, weights, value_grads],
        [pltpu.VMEM((model, rows), brief)],
        flops=4 * model * heads * rows,
    )
    (payload,) = on_core(
        functools.partial(payload_kernel, width),
        [jax.ShapeDtypeStruct((chips, width + heads + SPARE, rows), brief)],
        [],
        [mine, arrived, own],
    )
    inverse_rms = inverse[:1]
    second_trip = swap(payload, "chip")
    kept = (gradient, inverse_rms, stream, cotangent, own_gain, slots, w_value, moment_one, moment_two)
    second_trip, kept = lax.optimization_barrier((second_trip, kept))
    gradient, inverse_rms, stream, cotangent, own_gain, slots, w_value, moment_one, moment_two = kept
    norm_grads = jnp.sum(second_trip[:, :width].astype(jnp.float32), axis=0)
    gathered = lax.all_gather(second_trip[:, width:], "core", axis=1)
    extra = jnp.sum(gathered[:, :, heads:].astype(jnp.float32), axis=(0, 1))
    inner = jnp.sum(extra[0:3], axis=0, keepdims=True) / model
    square = jnp.sum(extra[3:6], axis=0, keepdims=True)
    mixed = matmul("fh,hr->fr", out_weights, gathered[:, :, :heads].reshape(-1, rows))
    outputs = (stream.astype(jnp.float32) + mixed).astype(jnp.bfloat16)
    unit = stream.astype(jnp.float32) * inverse_rms
    back = (
        cotangent.astype(jnp.float32) + inverse_rms * (norm_grads * own_gain - unit * inner)
    ).astype(jnp.bfloat16)

    sections = lax.axis_size("section")
    parts = jnp.concatenate(parts_of(square)).astype(jnp.bfloat16)
    parts = jnp.pad(parts, ((0, SPARE - parts.shape[0]), (0, 0)))
    ahead = jnp.arange(sections)[:, None, None] == (section_now + 1) % sections
    both = jnp.where(ahead, jnp.concatenate([outputs, parts]), jnp.concatenate([back, parts]))
    third_trip = swap(both, "section")
    behind = [(section_now + sections - 1) % sections, (section_now + 1) % sections]
    arrived = jnp.stack(
        [lax.dynamic_index_in_dim(third_trip, at, 0, keepdims=False)[:width] for at in behind]
    )

    every = jnp.arange(peers * slot_rows, dtype=jnp.int32)
    select = (every[:, None] == slots[None, :]).astype(brief)
    spread = matmul("sr,kfr->ksf", select, arrived).astype(brief)
    spread = spread.reshape(2, peers, slot_rows, width).transpose(1, 0, 2, 3)
    spread = spread.reshape(peers, 2 * slot_rows, width)
    spread, third_trip = lax.optimization_barrier((spread, third_trip))
    final = swap(spread, PEER)
    totals = jnp.sum(third_trip[:, width : width + 3].astype(full))
    passed, returned = on_core(
        join_kernel,
        [jax.ShapeDtypeStruct(acts.shape, brief)] * 2,
        [],
        [final],
        [pltpu.VMEM((2 * slot_rows, model), full)],
    )

    clip_scale = jnp.minimum(1.0, CLIP_NORM / jnp.sqrt(totals + 1e-06))
    clipped = gradient * clip_scale
    first = BETA_ONE * moment_one[0] + (1.0 - BETA_ONE) * clipped
    second = BETA_TWO * moment_two[0] + (1.0 - BETA_TWO) * clipped * clipped
    wide = w_value[0].astype(jnp.float32)
    updated = wide - LEARN_RATE * (first / (jnp.sqrt(second) + ADAM_EPS) + DECAY * wide)
    return passed, returned, updated.astype(jnp.bfloat16)[None], first[None], second[None]


def solution(mesh):
    sections, peers = mesh.devices.shape
    fine = Mesh(mesh.devices.reshape(sections, peers // 2, 2), ("section",) + PEER)
    slots = P("section", PEER, None, None, None)
    matrix = P("section", PEER, None)
    return jax.shard_map(
        body,
        mesh=fine,
        in_specs=(P(), slots, slots, P("section", None), matrix, matrix, matrix, matrix),
        out_specs=(slots, slots, matrix, matrix, matrix),
        check_vma=False,
    )
```

```python
import functools

import jax
import jax.numpy as jnp
from jax import lax
from jax.experimental import pallas as pl
from jax.experimental.pallas import tpu as pltpu
from jax.sharding import Mesh, PartitionSpec as P

NORM_EPS = 1e-05
CLIP_NORM = 1.0
LEARN_RATE = 0.001
BETA_ONE = 0.9
BETA_TWO = 0.95
ADAM_EPS = 1e-08
DECAY = 0.1
PEER = ("chip", "core")
SPARE = 8


def matmul(equation, left, right):
    return jnp.einsum(equation, left, right, preferred_element_type=jnp.float32)


def swap(blocks, axis):
    return lax.all_to_all(blocks, axis, split_axis=0, concat_axis=0, tiled=True)


def moved(block, axis, distance):
    count = lax.axis_size(axis)
    return lax.ppermute(block, axis, [(i, (i + distance) % count) for i in range(count)])


def to_all(block, count):
    return jnp.broadcast_to(block[None], (count,) + block.shape)


def slot_rows_of(placed, capacity, micro_rows):
    ids = jnp.arange(placed.shape[0], dtype=jnp.int32)
    twins = (placed[:, None] == placed[None, :]) & (ids[:, None] < ids[None, :])
    slots = placed * capacity + jnp.sum(twins.astype(jnp.int32), axis=0)
    return (slots[:, None] * micro_rows + jnp.arange(micro_rows, dtype=jnp.int32)).reshape(-1)


def on_core(kernel, out_shape, scalars, arrays, scratch=(), flops=0, held_in=pltpu.VMEM, limit=24 * 2**20):
    size = sum(a.size * a.dtype.itemsize for a in arrays)
    size += sum(o.size * o.dtype.itemsize for o in out_shape)
    return pl.pallas_call(
        kernel,
        out_shape=out_shape,
        in_specs=[pl.BlockSpec(memory_space=pltpu.SMEM)] * len(scalars)
        + [pl.BlockSpec(memory_space=held_in)] * len(arrays),
        out_specs=[pl.BlockSpec(memory_space=pltpu.VMEM)] * len(out_shape),
        scratch_shapes=list(scratch),
        compiler_params=pltpu.CompilerParams(vmem_limit_bytes=limit),
        cost_estimate=pl.CostEstimate(flops=flops, bytes_accessed=size, transcendentals=0),
    )(*scalars, *arrays)


def dnormed_kernel(width, heads, core_ref, trip_ref, weight_ref, grads_ref, mine_ref, other_ref):
    chips = trip_ref.shape[0]
    total = trip_ref[0, width : width + heads, :].astype(jnp.float32)
    for chip in range(1, chips):
        total += trip_ref[chip, width : width + heads, :].astype(jnp.float32)
    grads = total.astype(jnp.bfloat16)
    grads_ref[...] = grads
    first_core = core_ref[0] == 0
    group = 4
    span = group * 2 * width
    for step in range(chips // group):
        part = lax.dot_general(
            weight_ref[:, step * span : (step + 1) * span],
            grads,
            (((0,), (0,)), ((), ())),
            preferred_element_type=jnp.float32,
        )
        for local in range(group):
            low = part[2 * local * width : (2 * local + 1) * width]
            high = part[(2 * local + 1) * width : (2 * local + 2) * width]
            chip = step * group + local
            mine_ref[chip] = jnp.where(first_core, low, high).astype(jnp.bfloat16)
            other_ref[chip] = jnp.where(first_core, high, low).astype(jnp.bfloat16)


def split_kernel(acts_ref, cotan_ref, out_ref, acts_here, cotan_here, arrived):
    chips, _, width = out_ref.shape
    pairs = ((acts_ref, acts_here), (cotan_ref, cotan_here))
    copies = [pltpu.make_async_copy(a, b, arrived.at[n]) for n, (a, b) in enumerate(pairs)]
    for copy in copies:
        copy.start()
    for copy in copies:
        copy.wait()
    capacity = acts_here.shape[2]
    held = [ref[0, 0, slot] for ref in (acts_here, cotan_here) for slot in range(capacity)]
    held = jnp.concatenate([rows.astype(jnp.float32) for rows in held], axis=0)
    for chip in range(chips):
        out_ref[chip] = held[:, chip * width : (chip + 1) * width].astype(jnp.bfloat16)


def features_kernel(
    heads, core_ref, cols_ref, at_ref, weight_ref, other_weight_ref,
    out_ref, stream_ref, cotangent_ref,
):
    chips = out_ref.shape[0]
    width, rows = stream_ref.shape
    slot_rows = cols_ref.shape[0] // (4 * chips)
    first_core = core_ref[0] == 0
    line = lax.broadcasted_iota(jnp.int32, (cols_ref.shape[0], rows), 0)
    cols = cols_ref[...]

    def picked(first):
        select = (line == at_ref[...] + first).astype(jnp.float32).astype(jnp.bfloat16)
        both = lax.dot_general(
            cols, select, (((0,), (0,)), ((), ())), preferred_element_type=jnp.float32
        )
        low, high = both[:width], both[width:]
        own = jnp.where(first_core, low, high).astype(jnp.bfloat16)
        return own, jnp.where(first_core, high, low).astype(jnp.bfloat16)

    stream, _ = picked(0)
    cotangent, other_cotangent = picked(slot_rows)
    stream_ref[...] = stream
    cotangent_ref[...] = cotangent
    group = min(8, chips)
    span = group * 2 * heads
    for step in range(chips // group):
        part = sum(
            lax.dot_general(
                ref[:, step * span : (step + 1) * span],
                block,
                (((0,), (0,)), ((), ())),
                preferred_element_type=jnp.float32,
            )
            for ref, block in ((weight_ref, cotangent), (other_weight_ref, other_cotangent))
        )
        for local in range(group):
            low = part[2 * local * heads : (2 * local + 1) * heads]
            high = part[(2 * local + 1) * heads : (2 * local + 2) * heads]
            chip = step * group + local
            mine = jnp.where(first_core, low, high).astype(jnp.bfloat16)
            out_ref[chip] = jnp.concatenate([stream, mine], axis=0)


def join_kernel(trip_ref, passed_ref, returned_ref, rows_ref):
    peers, _, width = trip_ref.shape
    _, _, capacity, micro_rows, _ = passed_ref.shape
    for peer in range(peers):
        rows_ref[:, peer * width : (peer + 1) * width] = trip_ref[peer].astype(jnp.float32)
    at = 0
    for ref in (passed_ref, returned_ref):
        for slot in range(capacity):
            ref[0, 0, slot] = rows_ref[at : at + micro_rows, :].astype(jnp.bfloat16)
            at += micro_rows


def parts_of(values):
    high = lax.reduce_precision(values, 8, 7)
    middle = lax.reduce_precision(values - high, 8, 7)
    return [high, middle, values - high - middle]


def values_kernel(
    width, heads, core_ref, mine_ref, other_ref, gain_ref, weight_ref, grads_ref,
    own_ref, gradient_ref, inverse_ref, normed_ref,
):
    chips = mine_ref.shape[0]
    model = 2 * chips * width
    squares = jnp.zeros((width, mine_ref.shape[2]), jnp.float32)
    for chip in range(chips):
        for ref in (mine_ref, other_ref):
            block = ref[chip, :width, :].astype(jnp.float32)
            squares += block * block
    mean = jnp.sum(squares, axis=0, keepdims=True) / model
    inverse = lax.rsqrt(mean + NORM_EPS)
    inverse_ref[...] = jnp.broadcast_to(inverse, inverse_ref.shape)
    first_core = core_ref[0] == 0
    lanes = mine_ref.shape[2]
    one = (lax.broadcasted_iota(jnp.int32, (16, lanes), 0) == 0).astype(jnp.float32)
    group = 4
    span = group * 2 * width
    for step in range(chips // group):
        gains = jnp.broadcast_to(gain_ref[:, step * span : (step + 1) * span], (16, span))
        gains = lax.dot_general(
            gains,
            one.astype(jnp.bfloat16),
            (((0,), (0,)), ((), ())),
            preferred_element_type=jnp.float32,
        )
        for local in range(group):
            mine, other = (ref[step * group + local, :width, :] for ref in (mine_ref, other_ref))
            low, high = jnp.where(first_core, mine, other), jnp.where(first_core, other, mine)
            for core, block in ((0, low), (1, high)):
                at = (2 * local + core) * width
                scaled = block.astype(jnp.float32) * inverse * gains[at : at + width]
                normed_ref[pl.ds(step * span + at, width), :] = scaled.astype(jnp.bfloat16)
    values = jnp.dot(weight_ref[...], normed_ref[...], preferred_element_type=jnp.float32)
    grads = grads_ref[...]
    span = 8 * width
    norms = jnp.zeros((heads, lanes), jnp.float32)
    for step in range(model // span):
        block = lax.dot_general(
            grads,
            normed_ref[step * span : (step + 1) * span, :],
            (((1,), (1,)), ((), ())),
            preferred_element_type=jnp.float32,
        )
        gradient_ref[:, step * span : (step + 1) * span] = block
        for lane in range(span // lanes):
            piece = block[:, lane * lanes : (lane + 1) * lanes]
            norms += piece * piece
    inner = jnp.sum(grads.astype(jnp.float32) * values, axis=0, keepdims=True)
    norm = jnp.sum(norms, axis=0, keepdims=True)
    line = lax.broadcasted_iota(jnp.int32, (SPARE, values.shape[1]), 0)
    extra = jnp.zeros((SPARE, values.shape[1]), jnp.float32)
    for index, part in enumerate(parts_of(inner) + parts_of(norm)):
        extra = jnp.where(line == index, part, extra)
    own_ref[...] = jnp.concatenate([values, extra], axis=0).astype(jnp.bfloat16)


def payload_kernel(width, mine_ref, arrived_ref, own_ref, out_ref):
    own = own_ref[...]
    for chip in range(mine_ref.shape[0]):
        block = mine_ref[chip].astype(jnp.float32) + arrived_ref[chip].astype(jnp.float32)
        out_ref[chip, :width, :] = block.astype(jnp.bfloat16)
        out_ref[chip, width:, :] = own


def body(placing, acts, cotan, gain, w_value, w_out, moment_one, moment_two):
    chips = lax.axis_size("chip")
    peers = 2 * chips
    section_now = lax.axis_index("section")
    peer_now = lax.axis_index(PEER)
    _, _, capacity, micro_rows, model = acts.shape
    slot_rows = capacity * micro_rows
    width = model // peers
    heads = w_value.shape[1]
    rows = peers * micro_rows
    weights, out_weights = w_value[0], w_out[0]

    core = lax.axis_index("core").astype(jnp.int32).reshape(1)
    brief, full = jnp.bfloat16, jnp.float32
    (held,) = on_core(
        split_kernel,
        [jax.ShapeDtypeStruct((chips, 2 * slot_rows, 2 * width), brief)],
        [],
        [acts, cotan],
        [pltpu.VMEM(acts.shape, brief), pltpu.VMEM(cotan.shape, brief), pltpu.SemaphoreType.DMA((2,))],
        held_in=pl.ANY,
        limit=None,
    )
    other_out_weights = moved(out_weights, "core", 1)
    cols = swap(held, "chip")
    placed = lax.dynamic_index_in_dim(placing[:, :, 0], section_now, 0, keepdims=False)
    slots = slot_rows_of(placed, capacity, micro_rows)
    holder = slots // slot_rows
    at = ((holder % 2) * chips + holder // 2) * (2 * slot_rows) + slots % slot_rows
    own_gain = lax.dynamic_slice_in_dim(gain[0], peer_now * width, width, 0).astype(full)
    own_gain = jnp.broadcast_to(own_gain[:, None], (width, rows))
    cols, at, slots, own_gain = lax.optimization_barrier((cols, at, slots, own_gain))
    cols = lax.all_gather(cols, "core", axis=0).reshape(peers * 2 * slot_rows, 2 * width)

    payload, stream, cotangent = on_core(
        functools.partial(features_kernel, heads),
        [
            jax.ShapeDtypeStruct((chips, width + heads, rows), brief),
            jax.ShapeDtypeStruct((width, rows), brief),
            jax.ShapeDtypeStruct((width, rows), brief),
        ],
        [core],
        [cols, at[None], out_weights, other_out_weights],
        flops=4 * heads * peers * width * rows,
    )
    first_trip = swap(payload, "chip")
    other_trip = moved(first_trip, "core", 1)
    half = jax.ShapeDtypeStruct((chips, width, rows), brief)
    value_grads, mine, other = on_core(
        functools.partial(dnormed_kernel, width, heads),
        [jax.ShapeDtypeStruct((heads, rows), brief), half, half],
        [core],
        [first_trip, weights],
        flops=2 * model * heads * rows,
    )
    arrived = moved(other, "core", 1)
    own, gradient, inverse = on_core(
        functools.partial(values_kernel, width, heads),
        [
            jax.ShapeDtypeStruct((heads + SPARE, rows), brief),
            jax.ShapeDtypeStruct((heads, model), full),
            jax.ShapeDtypeStruct((SPARE, rows), full),
        ],
        [core],
        [first_trip, other_trip, gain, weights, value_grads],
        [pltpu.VMEM((model, rows), brief)],
        flops=4 * model * heads * rows,
    )
    (payload,) = on_core(
        functools.partial(payload_kernel, width),
        [jax.ShapeDtypeStruct((chips, width + heads + SPARE, rows), brief)],
        [],
        [mine, arrived, own],
    )
    second_trip = swap(payload, "chip")
    kept = (gradient, inverse, stream, cotangent, own_gain, slots, section_now, w_value)
    kept = kept + (moment_one, moment_two)
    second_trip, kept = lax.optimization_barrier((second_trip, kept))
    gradient, inverse, stream, cotangent, own_gain, slots, section_now, w_value = kept[:8]
    moment_one, moment_two = kept[8:]
    inverse_rms = inverse[:1]
    norm_grads = jnp.sum(second_trip[:, :width].astype(jnp.float32), axis=0)
    gathered = lax.all_gather(second_trip[:, width:], "core", axis=1)
    extra = jnp.sum(gathered[:, :, heads:].astype(jnp.float32), axis=(0, 1))
    inner = jnp.sum(extra[0:3], axis=0, keepdims=True) / model
    square = jnp.sum(extra[3:6], axis=0, keepdims=True)
    mixed = matmul("fh,hr->fr", out_weights, gathered[:, :, :heads].reshape(-1, rows))
    outputs = (stream.astype(jnp.float32) + mixed).astype(jnp.bfloat16)
    unit = stream.astype(jnp.float32) * inverse_rms
    back = (
        cotangent.astype(jnp.float32) + inverse_rms * (norm_grads * own_gain - unit * inner)
    ).astype(jnp.bfloat16)

    sections = lax.axis_size("section")
    parts = jnp.concatenate(parts_of(square)).astype(jnp.bfloat16)
    parts = jnp.pad(parts, ((0, SPARE - parts.shape[0]), (0, 0)))
    both = jnp.broadcast_to(jnp.concatenate([back, parts])[None], (sections, width + SPARE, rows))
    ahead = jnp.concatenate([outputs, parts])
    both = lax.dynamic_update_index_in_dim(both, ahead, (section_now + 1) % sections, 0)
    third_trip = swap(both, "section")
    kept = (third_trip, section_now, slots, gradient, w_value, moment_one, moment_two)
    third_trip, section_now, slots, gradient, w_value, moment_one, moment_two = (
        lax.optimization_barrier(kept)
    )
    behind = [(section_now + sections - 1) % sections, (section_now + 1) % sections]
    arrived = jnp.concatenate(
        [lax.dynamic_index_in_dim(third_trip, at, 0, keepdims=False)[:width] for at in behind],
        axis=1,
    )

    at = slots // slot_rows * (2 * slot_rows) + slots % slot_rows
    at = jnp.concatenate([at, at + slot_rows])
    every = jnp.arange(peers * 2 * slot_rows, dtype=jnp.int32)
    select = (every[:, None] == at[None, :]).astype(brief)
    spread = matmul("sr,fr->sf", select, arrived).astype(brief)
    spread = spread.reshape(peers, 2 * slot_rows, width)
    spread, third_trip = lax.optimization_barrier((spread, third_trip))
    final = swap(spread, PEER)
    totals = jnp.sum(third_trip[:, width : width + 3].astype(full))
    passed, returned = on_core(
        join_kernel,
        [jax.ShapeDtypeStruct(acts.shape, brief)] * 2,
        [],
        [final],
        [pltpu.VMEM((2 * slot_rows, model), full)],
    )

    clip_scale = jnp.minimum(1.0, CLIP_NORM / jnp.sqrt(totals + 1e-06))
    clipped = gradient * clip_scale
    first = BETA_ONE * moment_one[0] + (1.0 - BETA_ONE) * clipped
    second = BETA_TWO * moment_two[0] + (1.0 - BETA_TWO) * clipped * clipped
    wide = w_value[0].astype(jnp.float32)
    updated = wide - LEARN_RATE * (first / (jnp.sqrt(second) + ADAM_EPS) + DECAY * wide)
    return passed, returned, updated.astype(jnp.bfloat16)[None], first[None], second[None]


def solution(mesh):
    sections, peers = mesh.devices.shape
    fine = Mesh(mesh.devices.reshape(sections, peers // 2, 2), ("section",) + PEER)
    slots = P("section", PEER, None, None, None)
    matrix = P("section", PEER, None)
    return jax.shard_map(
        body,
        mesh=fine,
        in_specs=(P(), slots, slots, P("section", None), matrix, matrix, matrix, matrix),
        out_specs=(slots, slots, matrix, matrix, matrix),
        check_vma=False,
    )
```

```python
import functools

import jax
import jax.numpy as jnp
from jax import lax
from jax.experimental import pallas as pl
from jax.experimental.pallas import tpu as pltpu
from jax.sharding import Mesh, PartitionSpec as P

NORM_EPS = 1e-05
CLIP_NORM = 1.0
LEARN_RATE = 0.001
BETA_ONE = 0.9
BETA_TWO = 0.95
ADAM_EPS = 1e-08
DECAY = 0.1
CHIP = ("far", "pair", "line")
PEER = CHIP + ("core",)
TEAM = ("far", "line")
SPARE = 8
LANES = 128


def swap(blocks, axis):
    return lax.all_to_all(blocks, axis, split_axis=0, concat_axis=0, tiled=True)


def moved(block, axis):
    return lax.ppermute(block, axis, [(0, 1), (1, 0)])


def product(left, right, contract):
    dims = (((contract[0],), (contract[1],)), ((), ()))
    return lax.dot_general(left, right, dims, preferred_element_type=jnp.float32)


def turned(values):
    return pltpu.roll(values, values.shape[1] // 2, 1)


def in_low(shape):
    return lax.broadcasted_iota(jnp.int32, shape, 1) < shape[1] // 2


def pieces_apart(packed, first_pair):
    low, other = in_low(packed.shape), turned(packed)
    ahead, behind = jnp.where(first_pair, packed, other), jnp.where(first_pair, other, packed)
    zero = jnp.zeros_like(packed)
    own = jnp.where(low, ahead, zero), jnp.where(low, zero, behind)
    partner = jnp.where(low, behind, zero), jnp.where(low, zero, ahead)
    return own, partner


def by_pieces(weight_refs, packed_ref, first_pair):
    span = packed_ref.shape[0] // 2
    results = []
    for ref in weight_refs:
        low, high = (
            sum(
                product(
                    ref[:, (2 * far + piece) * span : (2 * far + piece + 1) * span],
                    packed_ref[far * span : (far + 1) * span, :],
                    (1, 0),
                )
                for far in range(2)
            )
            for piece in range(2)
        )
        joined = jnp.where(in_low(low.shape), low, high)
        results.append(joined + turned(joined))
    own, partner = results
    low = in_low(own.shape)
    ahead, behind = jnp.where(first_pair, own, partner), jnp.where(first_pair, partner, own)
    return jnp.where(low, ahead, behind)


def parts_of(values):
    high = lax.reduce_precision(values, 8, 7)
    middle = lax.reduce_precision(values - high, 8, 7)
    return [high, middle, values - high - middle]


def as_rows(parts, shape):
    line = lax.broadcasted_iota(jnp.int32, shape, 0)
    rows = jnp.zeros(shape, jnp.float32)
    for index, part in enumerate(parts):
        rows = jnp.where(line == index, part, rows)
    return rows


def split_kernel(acts_ref, cotan_ref, out_ref, acts_here, cotan_here, arrived):
    chips, _, width = out_ref.shape
    pairs = ((acts_ref, acts_here), (cotan_ref, cotan_here))
    copies = [pltpu.make_async_copy(a, b, arrived.at[n]) for n, (a, b) in enumerate(pairs)]
    for copy in copies:
        copy.start()
    for copy in copies:
        copy.wait()
    capacity = acts_here.shape[2]
    held = [ref[0, 0, slot] for ref in (acts_here, cotan_here) for slot in range(capacity)]
    held = jnp.concatenate([rows.astype(jnp.float32) for rows in held], axis=0)
    half, lines = width // 2, chips // 4
    for far in range(2):
        for line in range(lines):
            at = [((2 * far + piece) * lines + line) * half for piece in range(2)]
            both = jnp.concatenate([held[:, a : a + half] for a in at], axis=1).astype(jnp.bfloat16)
            for pair in range(2):
                out_ref[(2 * far + pair) * lines + line] = both


def store_by_core(part, first_core, chip, width, mine_ref, other_ref):
    for local in range(part.shape[0] // (2 * width)):
        low = part[2 * local * width : (2 * local + 1) * width]
        high = part[(2 * local + 1) * width : (2 * local + 2) * width]
        mine_ref[chip + local] = jnp.where(first_core, low, high).astype(jnp.bfloat16)
        other_ref[chip + local] = jnp.where(first_core, high, low).astype(jnp.bfloat16)


def partial_sums(weight_refs, packed, first_core, first_pair, width, mine_ref, other_ref):
    own, partner = pieces_apart(packed, first_pair)
    own, partner = ([half.astype(jnp.bfloat16) for half in halves] for halves in (own, partner))
    span = weight_refs[0].shape[1] // 4
    for far in range(2):
        part = 0.0
        for piece in range(2):
            at = (2 * far + piece) * span
            for ref, halves in zip(weight_refs, (own, partner)):
                part = part + product(ref[:, at : at + span], halves[piece], (0, 0))
        chip = far * (mine_ref.shape[0] // 2)
        store_by_core(part, first_core, chip, width, mine_ref, other_ref)


def features_kernel(
    heads, core_ref, pair_ref, cols_ref, at_ref, weight_ref, partner_ref,
    mine_ref, other_ref, stream_ref, cotangent_ref,
):
    width, rows = stream_ref.shape
    slot_rows = cols_ref.shape[0] // (8 * mine_ref.shape[0])
    first_core, first_pair = core_ref[0] == 0, pair_ref[0] == 0
    line = lax.broadcasted_iota(jnp.int32, (cols_ref.shape[0], rows), 0)
    cols = cols_ref[...]

    def picked(first):
        total = 0.0
        for piece in range(2):
            select = (line == at_ref[piece : piece + 1, :] + first).astype(jnp.float32)
            both = product(cols, select.astype(jnp.bfloat16), (0, 0))
            total = total + both[2 * piece * width : 2 * (piece + 1) * width]
        return jnp.where(first_core, total[:width], total[width:])

    stream, cotangent = picked(0), picked(slot_rows)
    stream_ref[...] = stream.astype(jnp.bfloat16)
    cotangent_ref[...] = cotangent.astype(jnp.bfloat16)
    refs = (weight_ref, partner_ref)
    partial_sums(refs, cotangent, first_core, first_pair, heads, mine_ref, other_ref)


def payload_kernel(sums_at, own_at, mine_ref, arrived_ref, own_ref, out_ref):
    own = own_ref[...]
    count = mine_ref.shape[1]
    for chip in range(mine_ref.shape[0]):
        block = mine_ref[chip].astype(jnp.float32) + arrived_ref[chip].astype(jnp.float32)
        out_ref[chip, sums_at : sums_at + count, :] = block.astype(jnp.bfloat16)
        out_ref[chip, own_at : own_at + own.shape[0], :] = own


def dnormed_kernel(
    width, heads, core_ref, pair_ref, trip_ref, weight_ref, partner_ref,
    grads_ref, mine_ref, other_ref,
):
    total = trip_ref[0, width : width + heads, :].astype(jnp.float32)
    for chip in range(1, trip_ref.shape[0]):
        total += trip_ref[chip, width : width + heads, :].astype(jnp.float32)
    grads = total.astype(jnp.bfloat16)
    grads_ref[...] = grads
    first_core, first_pair = core_ref[0] == 0, pair_ref[0] == 0
    refs = (weight_ref, partner_ref)
    grads = grads.astype(jnp.float32)
    partial_sums(refs, grads, first_core, first_pair, width, mine_ref, other_ref)


def values_kernel(
    width, heads, core_ref, pair_ref, mine_ref, other_ref, gain_ref, weight_ref, partner_ref,
    grads_ref, own_ref, gradient_ref, partner_gradient_ref, inverse_ref, normed_ref,
):
    chips, _, lanes = mine_ref.shape
    first_core, first_pair = core_ref[0] == 0, pair_ref[0] == 0
    squares = jnp.zeros((width, lanes), jnp.float32)
    for chip in range(chips):
        for ref in (mine_ref, other_ref):
            block = ref[chip, :width, :].astype(jnp.float32)
            squares += block * block
    total = jnp.broadcast_to(jnp.sum(squares, axis=0, keepdims=True), (SPARE, lanes))
    inverses = lax.rsqrt((total + turned(total)) / gain_ref.shape[1] + NORM_EPS)
    inverse_ref[...] = inverses
    inverse = inverses[0:1]
    span = gain_ref.shape[1] // 4
    lines = chips // 2
    top = lax.broadcasted_iota(jnp.int32, (16, lanes), 0) == 0
    low = in_low((16, lanes))
    ones = [jnp.where(top & (low == (piece == 0)), 1.0, 0.0).astype(jnp.bfloat16) for piece in range(2)]
    for far in range(2):
        gains = 0.0
        for piece in range(2):
            at = (2 * far + piece) * span
            rows = jnp.broadcast_to(gain_ref[:, at : at + span], (16, span))
            gains = gains + product(rows, ones[piece], (0, 0))
        for line in range(lines):
            mine, other = (ref[far * lines + line, :width, :] for ref in (mine_ref, other_ref))
            near, beyond = jnp.where(first_core, mine, other), jnp.where(first_core, other, mine)
            for core, block in ((0, near), (1, beyond)):
                at = (2 * line + core) * width
                scaled = block.astype(jnp.float32) * inverse * gains[at : at + width]
                normed_ref[pl.ds(far * span + at, width), :] = scaled.astype(jnp.bfloat16)
    values = by_pieces((weight_ref, partner_ref), normed_ref, first_pair)
    grads = grads_ref[...].astype(jnp.float32)
    own, partner = pieces_apart(grads, first_pair)
    for piece in range(2):
        both = jnp.concatenate([own[piece], partner[piece]], axis=0).astype(jnp.bfloat16)
        for far in range(2):
            block = product(both, normed_ref[far * span : (far + 1) * span, :], (1, 1))
            at = (2 * far + piece) * span
            gradient_ref[:, at : at + span] = block[:heads]
            partner_gradient_ref[:, at : at + span] = block[heads:].astype(jnp.bfloat16)
    inner = jnp.broadcast_to(jnp.sum(grads * values, axis=0, keepdims=True), (SPARE, lanes))
    inner = inner + turned(inner)
    extra = as_rows(parts_of(inner), (SPARE, lanes))
    own_ref[...] = jnp.concatenate([values, extra], axis=0).astype(jnp.bfloat16)


def gradient_kernel(mine_ref, arrived_ref, gradient_ref, norms_ref):
    lanes = norms_ref.shape[1]
    norms = jnp.zeros((mine_ref.shape[0], lanes), jnp.float32)
    for at in range(0, mine_ref.shape[1], lanes):
        block = mine_ref[:, at : at + lanes] + arrived_ref[:, at : at + lanes].astype(jnp.float32)
        gradient_ref[:, at : at + lanes] = block
        norms += block * block
    norms_ref[...] = jnp.broadcast_to(jnp.sum(norms, axis=0, keepdims=True), norms_ref.shape)


def finish_kernel(
    model, pair_ref, ahead_ref, trip_ref, values_ref, extra_ref, weight_ref, partner_ref, stream_ref,
    cotangent_ref, gain_ref, inverse_ref, norms_ref, out_ref,
):
    width, lanes = stream_ref.shape
    first_pair = pair_ref[0] == 0
    norm_grads = trip_ref[0, :width, :].astype(jnp.float32)
    for chip in range(1, trip_ref.shape[0]):
        norm_grads += trip_ref[chip, :width, :].astype(jnp.float32)
    inner = (extra_ref[0:1] + extra_ref[1:2] + extra_ref[2:3]) / model
    inverse = inverse_ref[0:1]
    stream = stream_ref[...].astype(jnp.float32)
    outputs = stream + by_pieces((weight_ref, partner_ref), values_ref, first_pair)
    units = stream * inverse
    back = cotangent_ref[...].astype(jnp.float32)
    back = back + inverse * (norm_grads * gain_ref[...] - units * inner)
    extra = as_rows(parts_of(norms_ref[0:1]), (SPARE, lanes))
    outputs, back = (
        jnp.concatenate([block, extra], axis=0).astype(jnp.bfloat16) for block in (outputs, back)
    )
    for section in range(out_ref.shape[0]):
        out_ref[section] = jnp.where(ahead_ref[0] == section, outputs, back)


def spread_kernel(width, from_ref, trip_ref, code_ref, out_ref):
    rows = trip_ref.shape[2]
    blocks = [trip_ref[from_ref[index], :width, :] for index in range(2)]
    blocks = jnp.concatenate(blocks, axis=1)
    blocks = jnp.concatenate([blocks, jnp.zeros((LANES - width, 2 * rows), jnp.bfloat16)], axis=0)
    line = lax.broadcasted_iota(jnp.int32, (out_ref.shape[0], 2 * rows), 0)
    select = (line == code_ref[...]).astype(jnp.float32).astype(jnp.bfloat16)
    spread = product(select, blocks, (1, 1))
    total = jnp.zeros((SPARE, rows), jnp.float32)
    for section in range(trip_ref.shape[0]):
        total += trip_ref[section, width:, :].astype(jnp.float32)
    total = jnp.sum(jnp.sum(total, axis=0, keepdims=True), axis=1, keepdims=True)
    lane = lax.broadcasted_iota(jnp.int32, (1, LANES), 1)
    for index, part in enumerate(parts_of(total)):
        spread = spread + jnp.where(lane == width + index, part, 0.0)
    out_ref[...] = spread.astype(jnp.bfloat16)


def join_kernel(width, trip_ref, passed_ref, returned_ref, total_ref, rows_ref):
    _, _, capacity, micro_rows, model = passed_ref.shape
    lines = trip_ref.shape[0] // 8
    slots = 2 * capacity * micro_rows
    norms = jnp.zeros((1, LANES), jnp.float32)
    for far in range(2):
        for at in range(2 * lines):
            peers = [(2 * far + pair) * 2 * lines + at for pair in range(2)]
            block = trip_ref[peers[0]].astype(jnp.float32) + trip_ref[peers[1]].astype(jnp.float32)
            norms += block[0:1]
            for piece in range(2):
                first = ((2 * far + piece) * 2 * lines + at) * width
                rows_ref[:, first : first + width] = block[piece * slots : (piece + 1) * slots, :width]
    lane = lax.broadcasted_iota(jnp.int32, (1, LANES), 1)
    inside = (lane >= width) & (lane < width + 3)
    total = jnp.sum(jnp.where(inside, norms, 0.0), axis=1, keepdims=True)
    total_ref[...] = jnp.broadcast_to(total, total_ref.shape)
    at = 0
    for ref in (passed_ref, returned_ref):
        for slot in range(capacity):
            ref[0, 0, slot] = rows_ref[at : at + micro_rows, :].astype(jnp.bfloat16)
            at += micro_rows


def slot_rows_of(placed, capacity, micro_rows):
    ids = jnp.arange(placed.shape[0], dtype=jnp.int32)
    twins = (placed[:, None] == placed[None, :]) & (ids[:, None] < ids[None, :])
    slots = placed * capacity + jnp.sum(twins.astype(jnp.int32), axis=0)
    return (slots[:, None] * micro_rows + jnp.arange(micro_rows, dtype=jnp.int32)).reshape(-1)


def on_core(kernel, out_shape, scalars, arrays, scratch=(), held_in=pltpu.VMEM, limit=24 * 2**20):
    size = sum(a.size * a.dtype.itemsize for a in arrays)
    size += sum(o.size * o.dtype.itemsize for o in out_shape)
    return pl.pallas_call(
        kernel,
        out_shape=out_shape,
        in_specs=[pl.BlockSpec(memory_space=pltpu.SMEM)] * len(scalars)
        + [pl.BlockSpec(memory_space=held_in)] * len(arrays),
        out_specs=[pl.BlockSpec(memory_space=pltpu.VMEM)] * len(out_shape),
        scratch_shapes=list(scratch),
        compiler_params=pltpu.CompilerParams(vmem_limit_bytes=limit),
        cost_estimate=pl.CostEstimate(flops=0, bytes_accessed=size, transcendentals=0),
    )(*scalars, *arrays)


def body(placing, acts, cotan, gain, w_value, w_out, moment_one, moment_two):
    lines = lax.axis_size("line")
    chips, team = 4 * lines, 2 * lines
    peers = 2 * chips
    sections = lax.axis_size("section")
    section_now, pair_now = lax.axis_index("section"), lax.axis_index("pair")
    far_now, line_now = lax.axis_index("far"), lax.axis_index("line")
    _, _, capacity, micro_rows, model = acts.shape
    slot_rows = capacity * micro_rows
    width = model // peers
    heads = w_value.shape[1]
    rows = peers * micro_rows
    half = rows // 2
    weights, out_weights = w_value[0], w_out[0]
    brief, full = jnp.bfloat16, jnp.float32
    core = lax.axis_index("core").astype(jnp.int32).reshape(1)
    pair = pair_now.astype(jnp.int32).reshape(1)

    def shape(dims, kind=brief):
        return jax.ShapeDtypeStruct(dims, kind)

    (held,) = on_core(
        split_kernel,
        [shape((chips, 2 * slot_rows, 4 * width))],
        [],
        [acts, cotan],
        [pltpu.VMEM(acts.shape, brief), pltpu.VMEM(cotan.shape, brief), pltpu.SemaphoreType.DMA((2,))],
        held_in=pl.ANY,
        limit=None,
    )
    pair_out_weights, pair_weights = moved(out_weights, "pair"), moved(weights, "pair")
    cols = swap(held, CHIP)
    placed = lax.dynamic_index_in_dim(placing[:, :, 0], section_now, 0, keepdims=False)
    slots = slot_rows_of(placed, capacity, micro_rows)
    slots = lax.dynamic_slice_in_dim(slots, pair_now * half, half, 0)
    holder, place = slots // slot_rows, slots % slot_rows
    at = ((holder % 2) * chips + holder // 2) * (2 * slot_rows) + place
    none = jnp.full_like(at, -(2**20))
    at = jnp.stack([jnp.concatenate([at, none]), jnp.concatenate([none, at])])
    code = holder * (4 * slot_rows) + place
    code = [code + kind * slot_rows + piece * 2 * slot_rows for kind in range(2) for piece in range(2)]
    code = jnp.concatenate(code)[None]
    own_gain = [
        lax.dynamic_slice_in_dim(
            gain[0], ((2 * far_now + piece) * lines + line_now) * 2 * width + core[0] * width, width, 0
        )
        for piece in range(2)
    ]
    own_gain = jnp.concatenate(
        [jnp.broadcast_to(part.astype(full)[:, None], (width, half)) for part in own_gain], axis=1
    )
    cols, at, code, own_gain = lax.optimization_barrier((cols, at, code, own_gain))
    cols = lax.all_gather(cols, "core", axis=0).reshape(peers * 2 * slot_rows, 4 * width)

    mine, other, stream, cotangent = on_core(
        functools.partial(features_kernel, heads),
        [shape((team, heads, rows))] * 2 + [shape((width, rows))] * 2,
        [core, pair],
        [cols, at, out_weights, pair_out_weights],
    )
    arrived = moved(other, "core")
    (payload,) = on_core(
        functools.partial(payload_kernel, width, 0),
        [shape((team, width + heads, rows))],
        [],
        [mine, arrived, stream],
    )
    first_trip = swap(payload, TEAM)
    other_trip = moved(first_trip, "core")
    value_grads, mine, other = on_core(
        functools.partial(dnormed_kernel, width, heads),
        [shape((heads, rows))] + [shape((team, width, rows))] * 2,
        [core, pair],
        [first_trip, weights, pair_weights],
    )
    arrived = moved(other, "core")
    own, gradient, pair_gradient, inverse = on_core(
        functools.partial(values_kernel, width, heads),
        [
            shape((heads + SPARE, rows)),
            shape((heads, model), full),
            shape((heads, model)),
            shape((SPARE, rows), full),
        ],
        [core, pair],
        [first_trip, other_trip, gain, weights, pair_weights, value_grads],
        [pltpu.VMEM((model // 2, rows), brief)],
    )
    (payload,) = on_core(
        functools.partial(payload_kernel, 0, width),
        [shape((team, width + heads + SPARE, rows))],
        [],
        [mine, arrived, own],
    )
    payload, pair_gradient = lax.optimization_barrier((payload, pair_gradient))
    second_trip = swap(payload, TEAM)
    gradient, norms = on_core(
        gradient_kernel,
        [shape((heads, model), full), shape((SPARE, rows), full)],
        [],
        [gradient, moved(pair_gradient, "pair")],
    )
    gathered = lax.all_gather(second_trip[:, width:], "core", axis=1)
    extra = jnp.sum(gathered[:, :, heads:].astype(full), axis=(0, 1))

    ahead = ((section_now + 1) % sections).astype(jnp.int32).reshape(1)
    (both,) = on_core(
        functools.partial(finish_kernel, model),
        [shape((sections, width + SPARE, rows))],
        [pair, ahead],
        [
            second_trip,
            gathered[:, :, :heads].reshape(-1, rows),
            extra,
            out_weights,
            pair_out_weights,
            stream,
            cotangent,
            own_gain,
            inverse,
            norms,
        ],
    )
    third_trip = swap(both, "section")
    behind = jnp.stack([(section_now + sections - 1) % sections, (section_now + 1) % sections])

    (spread,) = on_core(
        functools.partial(spread_kernel, width),
        [shape((peers * 4 * slot_rows, LANES))],
        [behind.astype(jnp.int32)],
        [third_trip, code],
    )
    final = swap(spread.reshape(peers, 4 * slot_rows, LANES), PEER)
    passed, returned, totals = on_core(
        functools.partial(join_kernel, width),
        [shape(acts.shape)] * 2 + [shape((SPARE, LANES), full)],
        [],
        [final],
        [pltpu.VMEM((2 * slot_rows, model), full)],
    )

    clip_scale = jnp.minimum(1.0, CLIP_NORM / jnp.sqrt(totals[0, 0] + 1e-06))
    clipped = gradient * clip_scale
    first = BETA_ONE * moment_one[0] + (1.0 - BETA_ONE) * clipped
    second = BETA_TWO * moment_two[0] + (1.0 - BETA_TWO) * clipped * clipped
    wide = weights.astype(full)
    updated = wide - LEARN_RATE * (first / (jnp.sqrt(second) + ADAM_EPS) + DECAY * wide)
    return passed, returned, updated.astype(brief)[None], first[None], second[None]


def solution(mesh):
    sections, peers = mesh.devices.shape
    fine = Mesh(mesh.devices.reshape(sections, 2, 2, peers // 8, 2), ("section",) + PEER)
    slots = P("section", PEER, None, None, None)
    matrix = P("section", PEER, None)
    return jax.shard_map(
        body,
        mesh=fine,
        in_specs=(P(), slots, slots, P("section", None), matrix, matrix, matrix, matrix),
        out_specs=(slots, slots, matrix, matrix, matrix),
        check_vma=False,
    )
```

```python
import functools

import jax
import jax.numpy as jnp
from jax import lax
from jax.experimental import pallas as pl
from jax.experimental.pallas import tpu as pltpu
from jax.sharding import Mesh, PartitionSpec as P

NORM_EPS = 1e-05
CLIP_NORM = 1.0
LEARN_RATE = 0.001
BETA_ONE = 0.9
BETA_TWO = 0.95
ADAM_EPS = 1e-08
DECAY = 0.1
CHIP = ("team", "pair")
PEER = CHIP + ("core",)
TEAM = "team"
SPARE = 8
LANES = 128


def swap(blocks, axis):
    return lax.all_to_all(blocks, axis, split_axis=0, concat_axis=0, tiled=True)


def moved(block, axis):
    return lax.ppermute(block, axis, [(0, 1), (1, 0)])


def product(left, right, contract):
    dims = (((contract[0],), (contract[1],)), ((), ()))
    return lax.dot_general(left, right, dims, preferred_element_type=jnp.float32)


def turned(values):
    return pltpu.roll(values, values.shape[1] // 2, 1)


def in_low(shape):
    return lax.broadcasted_iota(jnp.int32, shape, 1) < shape[1] // 2


def pieces_apart(packed, first_pair):
    low, other = in_low(packed.shape), turned(packed)
    first, second = jnp.where(low, packed, other), jnp.where(low, other, packed)
    return jnp.where(first_pair, first, second), jnp.where(first_pair, second, first)


def by_pieces(weight_refs, features, first_pair):
    results = []
    for ref in weight_refs:
        both = product(ref[...], features, (1, 0))
        results.append(both + turned(both))
    own, partner = results
    low = in_low(own.shape)
    ahead, behind = jnp.where(first_pair, own, partner), jnp.where(first_pair, partner, own)
    return jnp.where(low, ahead, behind)


def parts_of(values):
    high = lax.reduce_precision(values, 8, 7)
    middle = lax.reduce_precision(values - high, 8, 7)
    return [high, middle, values - high - middle]


def as_rows(parts, shape):
    line = lax.broadcasted_iota(jnp.int32, shape, 0)
    rows = jnp.zeros(shape, jnp.float32)
    for index, part in enumerate(parts):
        rows = jnp.where(line == index, part, rows)
    return rows


def split_kernel(acts_ref, cotan_ref, out_ref, acts_here, cotan_here, arrived):
    chips, _, width = out_ref.shape
    pairs = ((acts_ref, acts_here), (cotan_ref, cotan_here))
    copies = [pltpu.make_async_copy(a, b, arrived.at[n]) for n, (a, b) in enumerate(pairs)]
    for copy in copies:
        copy.start()
    for copy in copies:
        copy.wait()
    capacity = acts_here.shape[2]
    held = [ref[0, 0, slot] for ref in (acts_here, cotan_here) for slot in range(capacity)]
    held = jnp.concatenate([rows.astype(jnp.float32) for rows in held], axis=0)
    for chip in range(chips):
        at = chip // 2 * width
        out_ref[chip] = held[:, at : at + width].astype(jnp.bfloat16)


def partial_sums(weight_refs, packed, first_core, first_pair, width, mine_ref, other_ref):
    pieces = [piece.astype(jnp.bfloat16) for piece in pieces_apart(packed, first_pair)]
    team, span = mine_ref.shape[0], 4 * width
    group = min(team, 640 // span)
    low = in_low((width, packed.shape[1]))
    for first in range(0, team, group):
        columns = slice(first * span, (first + group) * span)
        part = sum(product(ref[:, columns], p, (0, 0)) for ref, p in zip(weight_refs, pieces))
        for local in range(group):
            parts = [part[local * span + n * width : local * span + (n + 1) * width] for n in range(4)]
            near, beyond = jnp.where(low, parts[0], parts[2]), jnp.where(low, parts[1], parts[3])
            mine, other = jnp.where(first_core, near, beyond), jnp.where(first_core, beyond, near)
            mine_ref[first + local] = mine.astype(jnp.bfloat16)
            other_ref[first + local] = other.astype(jnp.bfloat16)


def features_kernel(
    heads, core_ref, pair_ref, cols_ref, at_ref, weight_ref, partner_ref,
    mine_ref, other_ref, stream_ref, cotangent_ref,
):
    width, rows = stream_ref.shape
    slot_rows = cols_ref.shape[0] // (8 * mine_ref.shape[0])
    first_core, first_pair = core_ref[0] == 0, pair_ref[0] == 0
    line = lax.broadcasted_iota(jnp.int32, (cols_ref.shape[0], rows), 0)
    cols = cols_ref[...]

    def picked(first):
        total = 0.0
        for piece in range(2):
            select = (line == at_ref[piece : piece + 1, :] + first).astype(jnp.float32)
            both = product(cols, select.astype(jnp.bfloat16), (0, 0))
            total = total + both[2 * piece * width : 2 * (piece + 1) * width]
        return jnp.where(first_core, total[:width], total[width:])

    stream, cotangent = picked(0), picked(slot_rows)
    stream_ref[...] = stream.astype(jnp.bfloat16)
    cotangent_ref[...] = cotangent.astype(jnp.bfloat16)
    refs = (weight_ref, partner_ref)
    partial_sums(refs, cotangent, first_core, first_pair, heads, mine_ref, other_ref)


def payload_kernel(sums_at, own_at, mine_ref, arrived_ref, own_ref, out_ref):
    own = own_ref[...]
    count = mine_ref.shape[1]
    for chip in range(mine_ref.shape[0]):
        block = mine_ref[chip].astype(jnp.float32) + arrived_ref[chip].astype(jnp.float32)
        out_ref[chip, sums_at : sums_at + count, :] = block.astype(jnp.bfloat16)
        out_ref[chip, own_at : own_at + own.shape[0], :] = own


def dnormed_kernel(
    width, heads, core_ref, pair_ref, trip_ref, weight_ref, partner_ref,
    grads_ref, mine_ref, other_ref,
):
    total = trip_ref[0, width : width + heads, :].astype(jnp.float32)
    for chip in range(1, trip_ref.shape[0]):
        total += trip_ref[chip, width : width + heads, :].astype(jnp.float32)
    grads = total.astype(jnp.bfloat16)
    grads_ref[...] = grads
    first_core, first_pair = core_ref[0] == 0, pair_ref[0] == 0
    refs = (weight_ref, partner_ref)
    grads = grads.astype(jnp.float32)
    partial_sums(refs, grads, first_core, first_pair, width, mine_ref, other_ref)


def values_kernel(
    width, heads, core_ref, pair_ref, mine_ref, other_ref, gain_ref, weight_ref, partner_ref,
    grads_ref, own_ref, gradient_ref, partner_gradient_ref, inverse_ref, normed_ref,
):
    chips, _, lanes = mine_ref.shape
    first_core, first_pair = core_ref[0] == 0, pair_ref[0] == 0
    squares = jnp.zeros((width, lanes), jnp.float32)
    for chip in range(chips):
        for ref in (mine_ref, other_ref):
            block = ref[chip, :width, :].astype(jnp.float32)
            squares += block * block
    total = jnp.broadcast_to(jnp.sum(squares, axis=0, keepdims=True), (SPARE, lanes))
    inverses = lax.rsqrt((total + turned(total)) / gain_ref.shape[1] + NORM_EPS)
    inverse_ref[...] = inverses
    inverse = inverses[0:1]
    top = lax.broadcasted_iota(jnp.int32, (16, lanes), 0) == 0
    one = top.astype(jnp.float32).astype(jnp.bfloat16)
    low = in_low((width, lanes))
    span = 8 * width
    for first in range(0, chips, 2):
        at = first // 2 * span
        gains = jnp.broadcast_to(gain_ref[:, at : at + span], (16, span))
        gains = product(gains, one, (0, 0))
        for local in range(2):
            mine, other = (ref[first + local, :width, :] for ref in (mine_ref, other_ref))
            near, beyond = jnp.where(first_core, mine, other), jnp.where(first_core, other, mine)
            for core, block in ((0, near), (1, beyond)):
                units = block.astype(jnp.float32) * inverse
                for piece in range(2):
                    line = ((local * 2 + piece) * 2 + core) * width
                    scaled = units * gains[line : line + width]
                    scaled = jnp.where(low == (piece == 0), scaled, 0.0)
                    normed_ref[pl.ds(at + line, width), :] = scaled.astype(jnp.bfloat16)
    values = by_pieces((weight_ref, partner_ref), normed_ref[...], first_pair)
    grads = grads_ref[...].astype(jnp.float32)
    both = jnp.concatenate(pieces_apart(grads, first_pair), axis=0).astype(jnp.bfloat16)
    for at in range(0, gain_ref.shape[1], span):
        block = product(both, normed_ref[at : at + span, :], (1, 1))
        gradient_ref[:, at : at + span] = block[:heads]
        partner_gradient_ref[:, at : at + span] = block[heads:].astype(jnp.bfloat16)
    inner = jnp.broadcast_to(jnp.sum(grads * values, axis=0, keepdims=True), (SPARE, lanes))
    inner = inner + turned(inner)
    extra = as_rows(parts_of(inner), (SPARE, lanes))
    own_ref[...] = jnp.concatenate([values, extra], axis=0).astype(jnp.bfloat16)


def gradient_kernel(mine_ref, arrived_ref, gradient_ref, norms_ref):
    lanes = norms_ref.shape[1]
    norms = jnp.zeros((mine_ref.shape[0], lanes), jnp.float32)
    for at in range(0, mine_ref.shape[1], lanes):
        block = mine_ref[:, at : at + lanes] + arrived_ref[:, at : at + lanes].astype(jnp.float32)
        gradient_ref[:, at : at + lanes] = block
        norms += block * block
    norms_ref[...] = jnp.broadcast_to(jnp.sum(norms, axis=0, keepdims=True), norms_ref.shape)


def finish_kernel(
    model, pair_ref, ahead_ref, trip_ref, values_ref, extra_ref, weight_ref, partner_ref, stream_ref,
    cotangent_ref, gain_ref, inverse_ref, norms_ref, out_ref, features_ref,
):
    width, lanes = stream_ref.shape
    first_pair = pair_ref[0] == 0
    norm_grads = trip_ref[0, :width, :].astype(jnp.float32)
    for chip in range(1, trip_ref.shape[0]):
        norm_grads += trip_ref[chip, :width, :].astype(jnp.float32)
    inner = (extra_ref[0:1] + extra_ref[1:2] + extra_ref[2:3]) / model
    inverse = inverse_ref[0:1]
    stream = stream_ref[...].astype(jnp.float32)
    heads = values_ref.shape[2] - SPARE
    low = in_low((heads, lanes))
    for chip in range(values_ref.shape[0]):
        for core in range(2):
            block = values_ref[chip, core].astype(jnp.float32)[:heads]
            for piece in range(2):
                at = ((chip * 2 + piece) * 2 + core) * heads
                features_ref[at : at + heads, :] = jnp.where(low == (piece == 0), block, 0.0)
    features = features_ref[...].astype(jnp.bfloat16)
    outputs = stream + by_pieces((weight_ref, partner_ref), features, first_pair)
    units = stream * inverse
    back = cotangent_ref[...].astype(jnp.float32)
    back = back + inverse * (norm_grads * gain_ref[...] - units * inner)
    extra = as_rows(parts_of(norms_ref[0:1]), (SPARE, lanes))
    outputs, back = (
        jnp.concatenate([block, extra], axis=0).astype(jnp.bfloat16) for block in (outputs, back)
    )
    for section in range(out_ref.shape[0]):
        out_ref[section] = jnp.where(ahead_ref[0] == section, outputs, back)


def spread_kernel(width, from_ref, trip_ref, code_ref, out_ref):
    rows = trip_ref.shape[2]
    blocks = [trip_ref[from_ref[index], :width, :] for index in range(2)]
    blocks = jnp.concatenate(blocks, axis=1)
    blocks = jnp.concatenate([blocks, jnp.zeros((LANES - width, 2 * rows), jnp.bfloat16)], axis=0)
    line = lax.broadcasted_iota(jnp.int32, (out_ref.shape[0], 2 * rows), 0)
    select = (line == code_ref[...]).astype(jnp.float32).astype(jnp.bfloat16)
    spread = product(select, blocks, (1, 1))
    total = jnp.zeros((SPARE, rows), jnp.float32)
    for section in range(trip_ref.shape[0]):
        total += trip_ref[section, width:, :].astype(jnp.float32)
    total = jnp.sum(jnp.sum(total, axis=0, keepdims=True), axis=1, keepdims=True)
    lane = lax.broadcasted_iota(jnp.int32, (1, LANES), 1)
    for index, part in enumerate(parts_of(total)):
        spread = spread + jnp.where(lane == width + index, part, 0.0)
    out_ref[...] = spread.astype(jnp.bfloat16)


def join_kernel(
    width, trip_ref, gradient_ref, weight_ref, first_ref, second_ref,
    passed_ref, returned_ref, new_weight_ref, new_first_ref, new_second_ref, rows_ref,
):
    _, _, capacity, micro_rows, _ = passed_ref.shape
    slots = 2 * capacity * micro_rows
    norms = jnp.zeros((1, LANES), jnp.float32)
    for chip in range(trip_ref.shape[0] // 4):
        for core in range(2):
            peers = [(chip * 2 + pair) * 2 + core for pair in range(2)]
            block = trip_ref[peers[0]].astype(jnp.float32) + trip_ref[peers[1]].astype(jnp.float32)
            norms += block[0:1]
            for piece in range(2):
                at = peers[piece] * width
                rows_ref[:, at : at + width] = block[piece * slots : (piece + 1) * slots, :width]
    at = 0
    for ref in (passed_ref, returned_ref):
        for slot in range(capacity):
            ref[0, 0, slot] = rows_ref[at : at + micro_rows, :].astype(jnp.bfloat16)
            at += micro_rows
    lane = lax.broadcasted_iota(jnp.int32, (1, LANES), 1)
    inside = (lane >= width) & (lane < width + 3)
    total = jnp.sum(jnp.where(inside, norms, 0.0), axis=1, keepdims=True)
    scale = jnp.minimum(1.0, CLIP_NORM / jnp.sqrt(total + 1e-06))
    span = 8 * width
    for at in range(0, gradient_ref.shape[1], span):
        here = slice(at, at + span)
        clipped = gradient_ref[:, here] * scale
        first = BETA_ONE * first_ref[0, :, here] + (1.0 - BETA_ONE) * clipped
        second = BETA_TWO * second_ref[0, :, here] + (1.0 - BETA_TWO) * clipped * clipped
        wide = weight_ref[0, :, here].astype(jnp.float32)
        updated = wide - LEARN_RATE * (first / (jnp.sqrt(second) + ADAM_EPS) + DECAY * wide)
        new_weight_ref[0, :, here] = updated.astype(jnp.bfloat16)
        new_first_ref[0, :, here] = first
        new_second_ref[0, :, here] = second


def slot_rows_of(placed, capacity, micro_rows):
    ids = jnp.arange(placed.shape[0], dtype=jnp.int32)
    twins = (placed[:, None] == placed[None, :]) & (ids[:, None] < ids[None, :])
    slots = placed * capacity + jnp.sum(twins.astype(jnp.int32), axis=0)
    return (slots[:, None] * micro_rows + jnp.arange(micro_rows, dtype=jnp.int32)).reshape(-1)


def on_core(kernel, out_shape, scalars, arrays, scratch=(), held_in=pltpu.VMEM, limit=24 * 2**20):
    size = sum(a.size * a.dtype.itemsize for a in arrays)
    size += sum(o.size * o.dtype.itemsize for o in out_shape)
    return pl.pallas_call(
        kernel,
        out_shape=out_shape,
        in_specs=[pl.BlockSpec(memory_space=pltpu.SMEM)] * len(scalars)
        + [pl.BlockSpec(memory_space=held_in)] * len(arrays),
        out_specs=[pl.BlockSpec(memory_space=pltpu.VMEM)] * len(out_shape),
        scratch_shapes=list(scratch),
        compiler_params=pltpu.CompilerParams(vmem_limit_bytes=limit),
        cost_estimate=pl.CostEstimate(flops=0, bytes_accessed=size, transcendentals=0),
    )(*scalars, *arrays)


def body(placing, acts, cotan, gain, w_value, w_out, moment_one, moment_two):
    team = lax.axis_size("team")
    chips = 2 * team
    peers = 2 * chips
    sections = lax.axis_size("section")
    section_now, pair_now = lax.axis_index("section"), lax.axis_index("pair")
    team_now = lax.axis_index("team")
    _, _, capacity, micro_rows, model = acts.shape
    slot_rows = capacity * micro_rows
    width = model // peers
    heads = w_value.shape[1]
    rows = peers * micro_rows
    half = rows // 2
    weights, out_weights = w_value[0], w_out[0]
    brief, full = jnp.bfloat16, jnp.float32
    core = lax.axis_index("core").astype(jnp.int32).reshape(1)
    pair = pair_now.astype(jnp.int32).reshape(1)

    def shape(dims, kind=brief):
        return jax.ShapeDtypeStruct(dims, kind)

    (held,) = on_core(
        split_kernel,
        [shape((chips, 2 * slot_rows, 4 * width))],
        [],
        [acts, cotan],
        [pltpu.VMEM(acts.shape, brief), pltpu.VMEM(cotan.shape, brief), pltpu.SemaphoreType.DMA((2,))],
        held_in=pl.ANY,
        limit=None,
    )
    pair_out_weights, pair_weights = moved(out_weights, "pair"), moved(weights, "pair")
    cols = swap(held, CHIP)
    placed = lax.dynamic_index_in_dim(placing[:, :, 0], section_now, 0, keepdims=False)
    slots = slot_rows_of(placed, capacity, micro_rows)
    slots = lax.dynamic_slice_in_dim(slots, pair_now * half, half, 0)
    holder, place = slots // slot_rows, slots % slot_rows
    at = ((holder % 2) * chips + holder // 2) * (2 * slot_rows) + place
    none = jnp.full_like(at, -(2**20))
    at = jnp.stack([jnp.concatenate([at, none]), jnp.concatenate([none, at])])
    code = holder * (4 * slot_rows) + place
    code = [code + kind * slot_rows + piece * 2 * slot_rows for kind in range(2) for piece in range(2)]
    code = jnp.concatenate(code)[None]
    own_gain = [
        lax.dynamic_slice_in_dim(
            gain[0], ((2 * team_now + piece) * 2 + core[0]) * width, width, 0
        )
        for piece in range(2)
    ]
    own_gain = jnp.concatenate(
        [jnp.broadcast_to(part.astype(full)[:, None], (width, half)) for part in own_gain], axis=1
    )
    cols, at, code, own_gain = lax.optimization_barrier((cols, at, code, own_gain))
    cols = lax.all_gather(cols, "core", axis=0).reshape(peers * 2 * slot_rows, 4 * width)

    mine, other, stream, cotangent = on_core(
        functools.partial(features_kernel, heads),
        [shape((team, heads, rows))] * 2 + [shape((width, rows))] * 2,
        [core, pair],
        [cols, at, out_weights, pair_out_weights],
    )
    arrived = moved(other, "core")
    (payload,) = on_core(
        functools.partial(payload_kernel, width, 0),
        [shape((team, width + heads, rows))],
        [],
        [mine, arrived, stream],
    )
    payload, pair_weights = lax.optimization_barrier((payload, pair_weights))
    first_trip = swap(payload, TEAM)
    other_trip = moved(first_trip, "core")
    value_grads, mine, other = on_core(
        functools.partial(dnormed_kernel, width, heads),
        [shape((heads, rows))] + [shape((team, width, rows))] * 2,
        [core, pair],
        [first_trip, weights, pair_weights],
    )
    arrived = moved(other, "core")
    own, gradient, pair_gradient, inverse = on_core(
        functools.partial(values_kernel, width, heads),
        [
            shape((heads + SPARE, rows)),
            shape((heads, model), full),
            shape((heads, model)),
            shape((SPARE, rows), full),
        ],
        [core, pair],
        [first_trip, other_trip, gain, weights, pair_weights, value_grads],
        [pltpu.VMEM((model, rows), brief)],
    )
    (payload,) = on_core(
        functools.partial(payload_kernel, 0, width),
        [shape((team, width + heads + SPARE, rows))],
        [],
        [mine, arrived, own],
    )
    payload, pair_gradient = lax.optimization_barrier((payload, pair_gradient))
    second_trip = swap(payload, TEAM)
    gradient, norms = on_core(
        gradient_kernel,
        [shape((heads, model), full), shape((SPARE, rows), full)],
        [],
        [gradient, moved(pair_gradient, "pair")],
    )
    gathered = lax.all_gather(second_trip[:, width:], "core", axis=1)
    extra = jnp.sum(gathered[:, :, heads:].astype(full), axis=(0, 1))

    ahead = ((section_now + 1) % sections).astype(jnp.int32).reshape(1)
    (both,) = on_core(
        functools.partial(finish_kernel, model),
        [shape((sections, width + SPARE, rows))],
        [pair, ahead],
        [
            second_trip,
            gathered,
            extra,
            out_weights,
            pair_out_weights,
            stream,
            cotangent,
            own_gain,
            inverse,
            norms,
        ],
        [pltpu.VMEM((model // 2, rows), full)],
    )
    third_trip = swap(both, "section")
    behind = jnp.stack([(section_now + sections - 1) % sections, (section_now + 1) % sections])

    (spread,) = on_core(
        functools.partial(spread_kernel, width),
        [shape((peers * 4 * slot_rows, LANES))],
        [behind.astype(jnp.int32)],
        [third_trip, code],
    )
    final = swap(spread.reshape(peers, 4 * slot_rows, LANES), PEER)
    return on_core(
        functools.partial(join_kernel, width),
        [shape(acts.shape)] * 2
        + [shape(w_value.shape), shape(moment_one.shape, full), shape(moment_two.shape, full)],
        [],
        [final, gradient, w_value, moment_one, moment_two],
        [pltpu.VMEM((2 * slot_rows, model), full)],
    )


def solution(mesh):
    sections, peers = mesh.devices.shape
    fine = Mesh(mesh.devices.reshape(sections, peers // 4, 2, 2), ("section",) + PEER)
    slots = P("section", PEER, None, None, None)
    matrix = P("section", PEER, None)
    return jax.shard_map(
        body,
        mesh=fine,
        in_specs=(P(), slots, slots, P("section", None), matrix, matrix, matrix, matrix),
        out_specs=(slots, slots, matrix, matrix, matrix),
        check_vma=False,
    )
```

```python
import functools

import jax
import jax.numpy as jnp
from jax import lax
from jax.experimental import pallas as pl
from jax.experimental.pallas import tpu as pltpu
from jax.sharding import Mesh, PartitionSpec as P

NORM_EPS = 1e-05
CLIP_NORM = 1.0
LEARN_RATE = 0.001
BETA_ONE = 0.9
BETA_TWO = 0.95
ADAM_EPS = 1e-08
DECAY = 0.1
CHIP = ("team", "pair")
PEER = CHIP + ("core",)
TEAM = "team"
SPARE = 8
LANES = 128


def swap(blocks, axis):
    return lax.all_to_all(blocks, axis, split_axis=0, concat_axis=0, tiled=True)


def moved(block, axis):
    return lax.ppermute(block, axis, [(0, 1), (1, 0)])


def product(left, right, contract):
    dims = (((contract[0],), (contract[1],)), ((), ()))
    return lax.dot_general(left, right, dims, preferred_element_type=jnp.float32)


def turned(values):
    return pltpu.roll(values, values.shape[1] // 2, 1)


def in_low(shape):
    return lax.broadcasted_iota(jnp.int32, shape, 1) < shape[1] // 2


def pieces_apart(packed, first_pair):
    low, other = in_low(packed.shape), turned(packed)
    first, second = jnp.where(low, packed, other), jnp.where(low, other, packed)
    return jnp.where(first_pair, first, second), jnp.where(first_pair, second, first)


def by_pieces(weight_refs, features, first_pair):
    results = []
    for ref in weight_refs:
        both = product(ref[...], features, (1, 0))
        results.append(both + turned(both))
    own, partner = results
    low = in_low(own.shape)
    ahead, behind = jnp.where(first_pair, own, partner), jnp.where(first_pair, partner, own)
    return jnp.where(low, ahead, behind)


def parts_of(values):
    high = lax.reduce_precision(values, 8, 7)
    middle = lax.reduce_precision(values - high, 8, 7)
    return [high, middle, values - high - middle]


def as_rows(parts, shape):
    line = lax.broadcasted_iota(jnp.int32, shape, 0)
    rows = jnp.zeros(shape, jnp.float32)
    for index, part in enumerate(parts):
        rows = jnp.where(line == index, part, rows)
    return rows


def split_kernel(acts_ref, cotan_ref, out_ref, acts_here, cotan_here, arrived):
    chips, _, width = out_ref.shape
    pairs = ((acts_ref, acts_here), (cotan_ref, cotan_here))
    copies = [pltpu.make_async_copy(a, b, arrived.at[n]) for n, (a, b) in enumerate(pairs)]
    for copy in copies:
        copy.start()
    for copy in copies:
        copy.wait()
    capacity = acts_here.shape[2]
    held = [ref[0, 0, slot] for ref in (acts_here, cotan_here) for slot in range(capacity)]
    held = jnp.concatenate([rows.astype(jnp.float32) for rows in held], axis=0)
    for chip in range(chips):
        at = chip // 2 * width
        out_ref[chip] = held[:, at : at + width].astype(jnp.bfloat16)


def partial_sums(weight_refs, packed, first_core, first_pair, width, mine_ref, other_ref):
    pieces = [piece.astype(jnp.bfloat16) for piece in pieces_apart(packed, first_pair)]
    team, span = mine_ref.shape[0], 4 * width
    group = min(team, 640 // span)
    low = in_low((width, packed.shape[1]))
    for first in range(0, team, group):
        columns = slice(first * span, (first + group) * span)
        part = sum(product(ref[:, columns], p, (0, 0)) for ref, p in zip(weight_refs, pieces))
        for local in range(group):
            parts = [part[local * span + n * width : local * span + (n + 1) * width] for n in range(4)]
            near, beyond = jnp.where(low, parts[0], parts[2]), jnp.where(low, parts[1], parts[3])
            mine, other = jnp.where(first_core, near, beyond), jnp.where(first_core, beyond, near)
            mine_ref[first + local] = mine.astype(jnp.bfloat16)
            other_ref[first + local] = other.astype(jnp.bfloat16)


def features_kernel(
    heads, core_ref, pair_ref, cols_ref, at_ref, weight_ref, partner_ref,
    mine_ref, other_ref, stream_ref, cotangent_ref,
):
    width, rows = stream_ref.shape
    slot_rows = cols_ref.shape[0] // (8 * mine_ref.shape[0])
    first_core, first_pair = core_ref[0] == 0, pair_ref[0] == 0
    line = lax.broadcasted_iota(jnp.int32, (cols_ref.shape[0], rows), 0)
    cols = cols_ref[...]

    def picked(first):
        total = 0.0
        for piece in range(2):
            select = (line == at_ref[piece : piece + 1, :] + first).astype(jnp.float32)
            both = product(cols, select.astype(jnp.bfloat16), (0, 0))
            total = total + both[2 * piece * width : 2 * (piece + 1) * width]
        return jnp.where(first_core, total[:width], total[width:])

    stream, cotangent = picked(0), picked(slot_rows)
    stream_ref[...] = stream.astype(jnp.bfloat16)
    cotangent_ref[...] = cotangent.astype(jnp.bfloat16)
    refs = (weight_ref, partner_ref)
    partial_sums(refs, cotangent, first_core, first_pair, heads, mine_ref, other_ref)


def payload_kernel(sums_at, own_at, mine_ref, arrived_ref, own_ref, out_ref):
    own = own_ref[...]
    count = mine_ref.shape[1]
    for chip in range(mine_ref.shape[0]):
        block = mine_ref[chip].astype(jnp.float32) + arrived_ref[chip].astype(jnp.float32)
        out_ref[chip, sums_at : sums_at + count, :] = block.astype(jnp.bfloat16)
        out_ref[chip, own_at : own_at + own.shape[0], :] = own


def dnormed_kernel(
    width, heads, core_ref, pair_ref, trip_ref, weight_ref, partner_ref,
    grads_ref, mine_ref, other_ref,
):
    total = trip_ref[0, width : width + heads, :].astype(jnp.float32)
    for chip in range(1, trip_ref.shape[0]):
        total += trip_ref[chip, width : width + heads, :].astype(jnp.float32)
    grads = total.astype(jnp.bfloat16)
    grads_ref[...] = grads
    first_core, first_pair = core_ref[0] == 0, pair_ref[0] == 0
    refs = (weight_ref, partner_ref)
    grads = grads.astype(jnp.float32)
    partial_sums(refs, grads, first_core, first_pair, width, mine_ref, other_ref)


def normalise(width, first_core, mine_ref, other_ref, gain_ref, normed_ref):
    chips, _, lanes = mine_ref.shape
    squares = jnp.zeros((width, lanes), jnp.float32)
    for chip in range(chips):
        for ref in (mine_ref, other_ref):
            block = ref[chip, :width, :].astype(jnp.float32)
            squares += block * block
    total = jnp.broadcast_to(jnp.sum(squares, axis=0, keepdims=True), (SPARE, lanes))
    inverses = lax.rsqrt((total + turned(total)) / gain_ref.shape[1] + NORM_EPS)
    inverse = inverses[0:1]
    top = lax.broadcasted_iota(jnp.int32, (16, lanes), 0) == 0
    one = top.astype(jnp.float32).astype(jnp.bfloat16)
    low = in_low((width, lanes))
    span = 8 * width
    for first in range(0, chips, 2):
        at = first // 2 * span
        gains = jnp.broadcast_to(gain_ref[:, at : at + span], (16, span))
        gains = product(gains, one, (0, 0))
        for local in range(2):
            mine, other = (ref[first + local, :width, :] for ref in (mine_ref, other_ref))
            near, beyond = jnp.where(first_core, mine, other), jnp.where(first_core, other, mine)
            for core, block in ((0, near), (1, beyond)):
                units = block.astype(jnp.float32) * inverse
                for piece in range(2):
                    line = ((local * 2 + piece) * 2 + core) * width
                    scaled = units * gains[line : line + width]
                    scaled = jnp.where(low == (piece == 0), scaled, 0.0)
                    normed_ref[pl.ds(at + line, width), :] = scaled.astype(jnp.bfloat16)
    return inverses


def values_kernel(
    width, heads, core_ref, pair_ref, mine_ref, other_ref, gain_ref, weight_ref, partner_ref,
    grads_ref, own_ref, gradient_ref, inverse_ref, normed_ref,
):
    lanes = mine_ref.shape[2]
    first_core, first_pair = core_ref[0] == 0, pair_ref[0] == 0
    inverse_ref[...] = normalise(width, first_core, mine_ref, other_ref, gain_ref, normed_ref)
    values = by_pieces((weight_ref, partner_ref), normed_ref[...], first_pair)
    grads = grads_ref[...].astype(jnp.float32)
    own = pieces_apart(grads, first_pair)[0].astype(jnp.bfloat16)
    span = 8 * width
    for at in range(0, gain_ref.shape[1], span):
        gradient_ref[:, at : at + span] = product(own, normed_ref[at : at + span, :], (1, 1))
    inner = jnp.broadcast_to(jnp.sum(grads * values, axis=0, keepdims=True), (SPARE, lanes))
    inner = inner + turned(inner)
    extra = as_rows(parts_of(inner), (SPARE, lanes))
    own_ref[...] = jnp.concatenate([values, extra], axis=0).astype(jnp.bfloat16)


def gradient_kernel(
    width, core_ref, pair_ref, mine_ref, other_ref, gain_ref, grads_ref, half_ref,
    gradient_ref, norms_ref, normed_ref,
):
    lanes = norms_ref.shape[1]
    first_core, first_pair = core_ref[0] == 0, pair_ref[0] == 0
    normalise(width, first_core, mine_ref, other_ref, gain_ref, normed_ref)
    grads = grads_ref[...].astype(jnp.float32)
    own = pieces_apart(grads, first_pair)[0].astype(jnp.bfloat16)
    norms = jnp.zeros((half_ref.shape[0], lanes), jnp.float32)
    span = 8 * width
    for at in range(0, gain_ref.shape[1], span):
        block = product(own, normed_ref[at : at + span, :], (1, 1)) + half_ref[:, at : at + span]
        gradient_ref[:, at : at + span] = block
        for lane in range(0, span, lanes):
            norms += block[:, lane : lane + lanes] * block[:, lane : lane + lanes]
    norms_ref[...] = jnp.broadcast_to(jnp.sum(norms, axis=0, keepdims=True), norms_ref.shape)


def finish_kernel(
    model, pair_ref, ahead_ref, trip_ref, values_ref, extra_ref, weight_ref, partner_ref, stream_ref,
    cotangent_ref, gain_ref, inverse_ref, norms_ref, out_ref, features_ref,
):
    width, lanes = stream_ref.shape
    first_pair = pair_ref[0] == 0
    norm_grads = trip_ref[0, :width, :].astype(jnp.float32)
    for chip in range(1, trip_ref.shape[0]):
        norm_grads += trip_ref[chip, :width, :].astype(jnp.float32)
    inner = (extra_ref[0:1] + extra_ref[1:2] + extra_ref[2:3]) / model
    inverse = inverse_ref[0:1]
    stream = stream_ref[...].astype(jnp.float32)
    heads = values_ref.shape[2] - SPARE
    low = in_low((heads, lanes))
    for chip in range(values_ref.shape[0]):
        for core in range(2):
            block = values_ref[chip, core].astype(jnp.float32)[:heads]
            for piece in range(2):
                at = ((chip * 2 + piece) * 2 + core) * heads
                features_ref[at : at + heads, :] = jnp.where(low == (piece == 0), block, 0.0)
    features = features_ref[...].astype(jnp.bfloat16)
    outputs = stream + by_pieces((weight_ref, partner_ref), features, first_pair)
    units = stream * inverse
    back = cotangent_ref[...].astype(jnp.float32)
    back = back + inverse * (norm_grads * gain_ref[...] - units * inner)
    extra = as_rows(parts_of(norms_ref[0:1]), (SPARE, lanes))
    outputs, back = (
        jnp.concatenate([block, extra], axis=0).astype(jnp.bfloat16) for block in (outputs, back)
    )
    for section in range(out_ref.shape[0]):
        out_ref[section] = jnp.where(ahead_ref[0] == section, outputs, back)


def spread_kernel(width, from_ref, trip_ref, code_ref, out_ref):
    rows = trip_ref.shape[2]
    blocks = [trip_ref[from_ref[index], :width, :] for index in range(2)]
    blocks = jnp.concatenate(blocks, axis=1)
    blocks = jnp.concatenate([blocks, jnp.zeros((LANES - width, 2 * rows), jnp.bfloat16)], axis=0)
    line = lax.broadcasted_iota(jnp.int32, (out_ref.shape[0], 2 * rows), 0)
    select = (line == code_ref[...]).astype(jnp.float32).astype(jnp.bfloat16)
    spread = product(select, blocks, (1, 1))
    total = jnp.zeros((SPARE, rows), jnp.float32)
    for section in range(trip_ref.shape[0]):
        total += trip_ref[section, width:, :].astype(jnp.float32)
    total = jnp.sum(jnp.sum(total, axis=0, keepdims=True), axis=1, keepdims=True)
    lane = lax.broadcasted_iota(jnp.int32, (1, LANES), 1)
    for index, part in enumerate(parts_of(total)):
        spread = spread + jnp.where(lane == width + index, part, 0.0)
    out_ref[...] = spread.astype(jnp.bfloat16)


def join_kernel(
    width, trip_ref, gradient_ref, weight_ref, first_ref, second_ref,
    passed_ref, returned_ref, new_weight_ref, new_first_ref, new_second_ref, rows_ref,
):
    _, _, capacity, micro_rows, _ = passed_ref.shape
    slots = 2 * capacity * micro_rows
    norms = jnp.zeros((1, LANES), jnp.float32)
    for chip in range(trip_ref.shape[0] // 4):
        for core in range(2):
            peers = [(chip * 2 + pair) * 2 + core for pair in range(2)]
            block = trip_ref[peers[0]].astype(jnp.float32) + trip_ref[peers[1]].astype(jnp.float32)
            norms += block[0:1]
            for piece in range(2):
                at = peers[piece] * width
                rows_ref[:, at : at + width] = block[piece * slots : (piece + 1) * slots, :width]
    at = 0
    for ref in (passed_ref, returned_ref):
        for slot in range(capacity):
            ref[0, 0, slot] = rows_ref[at : at + micro_rows, :].astype(jnp.bfloat16)
            at += micro_rows
    lane = lax.broadcasted_iota(jnp.int32, (1, LANES), 1)
    inside = (lane >= width) & (lane < width + 3)
    total = jnp.sum(jnp.where(inside, norms, 0.0), axis=1, keepdims=True)
    scale = jnp.minimum(1.0, CLIP_NORM / jnp.sqrt(total + 1e-06))
    span = 8 * width
    for at in range(0, gradient_ref.shape[1], span):
        here = slice(at, at + span)
        clipped = gradient_ref[:, here] * scale
        first = BETA_ONE * first_ref[0, :, here] + (1.0 - BETA_ONE) * clipped
        second = BETA_TWO * second_ref[0, :, here] + (1.0 - BETA_TWO) * clipped * clipped
        wide = weight_ref[0, :, here].astype(jnp.float32)
        updated = wide - LEARN_RATE * (first / (jnp.sqrt(second) + ADAM_EPS) + DECAY * wide)
        new_weight_ref[0, :, here] = updated.astype(jnp.bfloat16)
        new_first_ref[0, :, here] = first
        new_second_ref[0, :, here] = second


def slot_rows_of(placed, capacity, micro_rows):
    ids = jnp.arange(placed.shape[0], dtype=jnp.int32)
    twins = (placed[:, None] == placed[None, :]) & (ids[:, None] < ids[None, :])
    slots = placed * capacity + jnp.sum(twins.astype(jnp.int32), axis=0)
    return (slots[:, None] * micro_rows + jnp.arange(micro_rows, dtype=jnp.int32)).reshape(-1)


def on_core(kernel, out_shape, scalars, arrays, scratch=(), held_in=pltpu.VMEM, limit=24 * 2**20):
    size = sum(a.size * a.dtype.itemsize for a in arrays)
    size += sum(o.size * o.dtype.itemsize for o in out_shape)
    return pl.pallas_call(
        kernel,
        out_shape=out_shape,
        in_specs=[pl.BlockSpec(memory_space=pltpu.SMEM)] * len(scalars)
        + [pl.BlockSpec(memory_space=held_in)] * len(arrays),
        out_specs=[pl.BlockSpec(memory_space=pltpu.VMEM)] * len(out_shape),
        scratch_shapes=list(scratch),
        compiler_params=pltpu.CompilerParams(vmem_limit_bytes=limit),
        cost_estimate=pl.CostEstimate(flops=0, bytes_accessed=size, transcendentals=0),
    )(*scalars, *arrays)


def body(placing, acts, cotan, gain, w_value, w_out, moment_one, moment_two):
    team = lax.axis_size("team")
    chips = 2 * team
    peers = 2 * chips
    sections = lax.axis_size("section")
    section_now, pair_now = lax.axis_index("section"), lax.axis_index("pair")
    team_now = lax.axis_index("team")
    _, _, capacity, micro_rows, model = acts.shape
    slot_rows = capacity * micro_rows
    width = model // peers
    heads = w_value.shape[1]
    rows = peers * micro_rows
    half = rows // 2
    weights, out_weights = w_value[0], w_out[0]
    brief, full = jnp.bfloat16, jnp.float32
    core = lax.axis_index("core").astype(jnp.int32).reshape(1)
    pair = pair_now.astype(jnp.int32).reshape(1)

    def shape(dims, kind=brief):
        return jax.ShapeDtypeStruct(dims, kind)

    (held,) = on_core(
        split_kernel,
        [shape((chips, 2 * slot_rows, 4 * width))],
        [],
        [acts, cotan],
        [pltpu.VMEM(acts.shape, brief), pltpu.VMEM(cotan.shape, brief), pltpu.SemaphoreType.DMA((2,))],
        held_in=pl.ANY,
        limit=None,
    )
    pair_out_weights, pair_weights = moved(out_weights, "pair"), moved(weights, "pair")
    cols = swap(held, CHIP)
    placed = lax.dynamic_index_in_dim(placing[:, :, 0], section_now, 0, keepdims=False)
    slots = slot_rows_of(placed, capacity, micro_rows)
    slots = lax.dynamic_slice_in_dim(slots, pair_now * half, half, 0)
    holder, place = slots // slot_rows, slots % slot_rows
    at = ((holder % 2) * chips + holder // 2) * (2 * slot_rows) + place
    none = jnp.full_like(at, -(2**20))
    at = jnp.stack([jnp.concatenate([at, none]), jnp.concatenate([none, at])])
    code = holder * (4 * slot_rows) + place
    code = [code + kind * slot_rows + piece * 2 * slot_rows for kind in range(2) for piece in range(2)]
    code = jnp.concatenate(code)[None]
    own_gain = [
        lax.dynamic_slice_in_dim(
            gain[0], ((2 * team_now + piece) * 2 + core[0]) * width, width, 0
        )
        for piece in range(2)
    ]
    own_gain = jnp.concatenate(
        [jnp.broadcast_to(part.astype(full)[:, None], (width, half)) for part in own_gain], axis=1
    )
    cols, at, code, own_gain = lax.optimization_barrier((cols, at, code, own_gain))
    cols = lax.all_gather(cols, "core", axis=0).reshape(peers * 2 * slot_rows, 4 * width)

    mine, other, stream, cotangent = on_core(
        functools.partial(features_kernel, heads),
        [shape((team, heads, rows))] * 2 + [shape((width, rows))] * 2,
        [core, pair],
        [cols, at, out_weights, pair_out_weights],
    )
    arrived = moved(other, "core")
    (payload,) = on_core(
        functools.partial(payload_kernel, width, 0),
        [shape((team, width + heads, rows))],
        [],
        [mine, arrived, stream],
    )
    payload, pair_weights = lax.optimization_barrier((payload, pair_weights))
    first_trip = swap(payload, TEAM)
    other_trip = moved(first_trip, "core")
    pair_mine = moved(first_trip[:, :width], "pair")
    value_grads, mine, other = on_core(
        functools.partial(dnormed_kernel, width, heads),
        [shape((heads, rows))] + [shape((team, width, rows))] * 2,
        [core, pair],
        [first_trip, weights, pair_weights],
    )
    arrived = moved(other, "core")
    own, half_gradient, inverse = on_core(
        functools.partial(values_kernel, width, heads),
        [
            shape((heads + SPARE, rows)),
            shape((heads, model), full),
            shape((SPARE, rows), full),
        ],
        [core, pair],
        [first_trip, other_trip, gain, weights, pair_weights, value_grads],
        [pltpu.VMEM((model, rows), brief)],
    )
    (payload,) = on_core(
        functools.partial(payload_kernel, 0, width),
        [shape((team, width + heads + SPARE, rows))],
        [],
        [mine, arrived, own],
    )
    payload, pair_mine, pair_grads = lax.optimization_barrier((payload, pair_mine, value_grads))
    second_trip = swap(payload, TEAM)
    gradient, norms = on_core(
        functools.partial(gradient_kernel, width),
        [shape((heads, model), full), shape((SPARE, rows), full)],
        [core, pair],
        [pair_mine, moved(pair_mine, "core"), gain, moved(pair_grads, "pair"), half_gradient],
        [pltpu.VMEM((model, rows), brief)],
    )
    gathered = lax.all_gather(second_trip[:, width:], "core", axis=1)
    extra = jnp.sum(gathered[:, :, heads:].astype(full), axis=(0, 1))

    ahead = ((section_now + 1) % sections).astype(jnp.int32).reshape(1)
    (both,) = on_core(
        functools.partial(finish_kernel, model),
        [shape((sections, width + SPARE, rows))],
        [pair, ahead],
        [
            second_trip,
            gathered,
            extra,
            out_weights,
            pair_out_weights,
            stream,
            cotangent,
            own_gain,
            inverse,
            norms,
        ],
        [pltpu.VMEM((model // 2, rows), full)],
    )
    third_trip = swap(both, "section")
    behind = jnp.stack([(section_now + sections - 1) % sections, (section_now + 1) % sections])

    (spread,) = on_core(
        functools.partial(spread_kernel, width),
        [shape((peers * 4 * slot_rows, LANES))],
        [behind.astype(jnp.int32)],
        [third_trip, code],
    )
    final = swap(spread.reshape(peers, 4 * slot_rows, LANES), PEER)
    return on_core(
        functools.partial(join_kernel, width),
        [shape(acts.shape)] * 2
        + [shape(w_value.shape), shape(moment_one.shape, full), shape(moment_two.shape, full)],
        [],
        [final, gradient, w_value, moment_one, moment_two],
        [pltpu.VMEM((2 * slot_rows, model), full)],
    )


def solution(mesh):
    sections, peers = mesh.devices.shape
    fine = Mesh(mesh.devices.reshape(sections, peers // 4, 2, 2), ("section",) + PEER)
    slots = P("section", PEER, None, None, None)
    matrix = P("section", PEER, None)
    return jax.shard_map(
        body,
        mesh=fine,
        in_specs=(P(), slots, slots, P("section", None), matrix, matrix, matrix, matrix),
        out_specs=(slots, slots, matrix, matrix, matrix),
        check_vma=False,
    )
```

```python
import functools

import jax
import jax.numpy as jnp
from jax import lax
from jax.experimental import pallas as pl
from jax.experimental.pallas import tpu as pltpu
from jax.sharding import Mesh, PartitionSpec as P

NORM_EPS = 1e-05
CLIP_NORM = 1.0
LEARN_RATE = 0.001
BETA_ONE = 0.9
BETA_TWO = 0.95
ADAM_EPS = 1e-08
DECAY = 0.1
CHIP = ("team", "pair")
PEER = CHIP + ("core",)
TEAM = "team"
SPARE = 8
LANES = 128


def swap(blocks, axis):
    return lax.all_to_all(blocks, axis, split_axis=0, concat_axis=0, tiled=True)


def moved(block, axis):
    return lax.ppermute(block, axis, [(0, 1), (1, 0)])


def product(left, right, contract):
    dims = (((contract[0],), (contract[1],)), ((), ()))
    return lax.dot_general(left, right, dims, preferred_element_type=jnp.float32)


def turned(values):
    return pltpu.roll(values, values.shape[1] // 2, 1)


def in_low(shape):
    return lax.broadcasted_iota(jnp.int32, shape, 1) < shape[1] // 2


def pieces_apart(packed, first_pair):
    low, other = in_low(packed.shape), turned(packed)
    first, second = jnp.where(low, packed, other), jnp.where(low, other, packed)
    return jnp.where(first_pair, first, second), jnp.where(first_pair, second, first)


def by_pieces(weight_refs, features, first_pair):
    results = []
    for ref in weight_refs:
        both = product(ref[...], features, (1, 0))
        results.append(both + turned(both))
    own, partner = results
    low = in_low(own.shape)
    ahead, behind = jnp.where(first_pair, own, partner), jnp.where(first_pair, partner, own)
    return jnp.where(low, ahead, behind)


def parts_of(values):
    high = lax.reduce_precision(values, 8, 7)
    middle = lax.reduce_precision(values - high, 8, 7)
    return [high, middle, values - high - middle]


def as_rows(parts, shape):
    line = lax.broadcasted_iota(jnp.int32, shape, 0)
    rows = jnp.zeros(shape, jnp.float32)
    for index, part in enumerate(parts):
        rows = jnp.where(line == index, part, rows)
    return rows


def split_kernel(acts_ref, cotan_ref, out_ref, acts_here, cotan_here, arrived):
    chips, _, width = out_ref.shape
    pairs = ((acts_ref, acts_here), (cotan_ref, cotan_here))
    copies = [pltpu.make_async_copy(a, b, arrived.at[n]) for n, (a, b) in enumerate(pairs)]
    for copy in copies:
        copy.start()
    for copy in copies:
        copy.wait()
    capacity = acts_here.shape[2]
    held = [ref[0, 0, slot] for ref in (acts_here, cotan_here) for slot in range(capacity)]
    held = jnp.concatenate([rows.astype(jnp.float32) for rows in held], axis=0)
    for chip in range(chips):
        at = chip // 2 * width
        out_ref[chip] = held[:, at : at + width].astype(jnp.bfloat16)


def partial_sums(weight_refs, packed, first_core, first_pair, width, mine_ref, other_ref):
    pieces = [piece.astype(jnp.bfloat16) for piece in pieces_apart(packed, first_pair)]
    team, span = mine_ref.shape[0], 4 * width
    group = min(team, 640 // span)
    low = in_low((width, packed.shape[1]))
    for first in range(0, team, group):
        columns = slice(first * span, (first + group) * span)
        part = sum(product(ref[:, columns], p, (0, 0)) for ref, p in zip(weight_refs, pieces))
        for local in range(group):
            parts = [part[local * span + n * width : local * span + (n + 1) * width] for n in range(4)]
            near, beyond = jnp.where(low, parts[0], parts[2]), jnp.where(low, parts[1], parts[3])
            mine, other = jnp.where(first_core, near, beyond), jnp.where(first_core, beyond, near)
            mine_ref[first + local] = mine.astype(jnp.bfloat16)
            other_ref[first + local] = other.astype(jnp.bfloat16)


def features_kernel(
    heads, core_ref, pair_ref, cols_ref, at_ref, weight_ref, partner_ref,
    mine_ref, other_ref, stream_ref, cotangent_ref,
):
    width, rows = stream_ref.shape
    slot_rows = cols_ref.shape[0] // (8 * mine_ref.shape[0])
    first_core, first_pair = core_ref[0] == 0, pair_ref[0] == 0
    line = lax.broadcasted_iota(jnp.int32, (cols_ref.shape[0], rows), 0)
    cols = cols_ref[...]

    def picked(first):
        total = 0.0
        for piece in range(2):
            select = (line == at_ref[piece : piece + 1, :] + first).astype(jnp.float32)
            both = product(cols, select.astype(jnp.bfloat16), (0, 0))
            total = total + both[2 * piece * width : 2 * (piece + 1) * width]
        return jnp.where(first_core, total[:width], total[width:])

    stream, cotangent = picked(0), picked(slot_rows)
    stream_ref[...] = stream.astype(jnp.bfloat16)
    cotangent_ref[...] = cotangent.astype(jnp.bfloat16)
    refs = (weight_ref, partner_ref)
    partial_sums(refs, cotangent, first_core, first_pair, heads, mine_ref, other_ref)


def payload_kernel(sums_at, own_at, mine_ref, arrived_ref, own_ref, out_ref):
    own = own_ref[...]
    count = mine_ref.shape[1]
    for chip in range(mine_ref.shape[0]):
        block = mine_ref[chip].astype(jnp.float32) + arrived_ref[chip].astype(jnp.float32)
        out_ref[chip, sums_at : sums_at + count, :] = block.astype(jnp.bfloat16)
        out_ref[chip, own_at : own_at + own.shape[0], :] = own


def summed_grads(width, trip_ref):
    total = trip_ref[0, width:, :].astype(jnp.float32)
    for chip in range(1, trip_ref.shape[0]):
        total += trip_ref[chip, width:, :].astype(jnp.float32)
    return total.astype(jnp.bfloat16)


def dnormed_kernel(
    width, core_ref, pair_ref, trip_ref, weight_ref, partner_ref,
    grads_ref, mine_ref, other_ref,
):
    grads = summed_grads(width, trip_ref)
    grads_ref[...] = grads
    first_core, first_pair = core_ref[0] == 0, pair_ref[0] == 0
    refs = (weight_ref, partner_ref)
    grads = grads.astype(jnp.float32)
    partial_sums(refs, grads, first_core, first_pair, width, mine_ref, other_ref)


def normalise(width, first_core, mine_ref, other_ref, gain_ref, normed_ref):
    chips, _, lanes = mine_ref.shape
    squares = jnp.zeros((width, lanes), jnp.float32)
    for chip in range(chips):
        for ref in (mine_ref, other_ref):
            block = ref[chip, :width, :].astype(jnp.float32)
            squares += block * block
    total = jnp.broadcast_to(jnp.sum(squares, axis=0, keepdims=True), (SPARE, lanes))
    inverses = lax.rsqrt((total + turned(total)) / gain_ref.shape[1] + NORM_EPS)
    inverse = inverses[0:1]
    top = lax.broadcasted_iota(jnp.int32, (16, lanes), 0) == 0
    one = top.astype(jnp.float32).astype(jnp.bfloat16)
    low = in_low((width, lanes))
    span = 8 * width
    for first in range(0, chips, 2):
        at = first // 2 * span
        gains = jnp.broadcast_to(gain_ref[:, at : at + span], (16, span))
        gains = product(gains, one, (0, 0))
        for local in range(2):
            mine, other = (ref[first + local, :width, :] for ref in (mine_ref, other_ref))
            near, beyond = jnp.where(first_core, mine, other), jnp.where(first_core, other, mine)
            for core, block in ((0, near), (1, beyond)):
                units = block.astype(jnp.float32) * inverse
                for piece in range(2):
                    line = ((local * 2 + piece) * 2 + core) * width
                    scaled = units * gains[line : line + width]
                    scaled = jnp.where(low == (piece == 0), scaled, 0.0)
                    normed_ref[pl.ds(at + line, width), :] = scaled.astype(jnp.bfloat16)
    return inverses


def values_kernel(
    width, heads, core_ref, pair_ref, mine_ref, other_ref, gain_ref, weight_ref, partner_ref,
    grads_ref, own_ref, gradient_ref, inverse_ref, normed_ref,
):
    lanes = mine_ref.shape[2]
    first_core, first_pair = core_ref[0] == 0, pair_ref[0] == 0
    inverse_ref[...] = normalise(width, first_core, mine_ref, other_ref, gain_ref, normed_ref)
    values = by_pieces((weight_ref, partner_ref), normed_ref[...], first_pair)
    grads = grads_ref[...].astype(jnp.float32)
    own = pieces_apart(grads, first_pair)[0].astype(jnp.bfloat16)
    span = 8 * width
    for at in range(0, gain_ref.shape[1], span):
        gradient_ref[:, at : at + span] = product(own, normed_ref[at : at + span, :], (1, 1))
    inner = jnp.broadcast_to(jnp.sum(grads * values, axis=0, keepdims=True), (SPARE, lanes))
    inner = inner + turned(inner)
    extra = as_rows(parts_of(inner), (SPARE, lanes))
    own_ref[...] = jnp.concatenate([values, extra], axis=0).astype(jnp.bfloat16)


def gradient_kernel(
    width, core_ref, pair_ref, mine_ref, other_ref, gain_ref, half_ref,
    gradient_ref, norms_ref, normed_ref,
):
    lanes = norms_ref.shape[1]
    first_core, first_pair = core_ref[0] == 0, pair_ref[0] == 0
    normalise(width, first_core, mine_ref, other_ref, gain_ref, normed_ref)
    grads = summed_grads(width, mine_ref).astype(jnp.float32)
    own = pieces_apart(grads, first_pair)[0].astype(jnp.bfloat16)
    norms = jnp.zeros((half_ref.shape[0], lanes), jnp.float32)
    span = 8 * width
    for at in range(0, gain_ref.shape[1], span):
        block = product(own, normed_ref[at : at + span, :], (1, 1)) + half_ref[:, at : at + span]
        gradient_ref[:, at : at + span] = block
        for lane in range(0, span, lanes):
            norms += block[:, lane : lane + lanes] * block[:, lane : lane + lanes]
    norms_ref[...] = jnp.broadcast_to(jnp.sum(norms, axis=0, keepdims=True), norms_ref.shape)


def finish_kernel(
    model, pair_ref, ahead_ref, trip_ref, values_ref, extra_ref, weight_ref, partner_ref, stream_ref,
    cotangent_ref, gain_ref, inverse_ref, norms_ref, out_ref, features_ref,
):
    width, lanes = stream_ref.shape
    first_pair = pair_ref[0] == 0
    norm_grads = trip_ref[0, :width, :].astype(jnp.float32)
    for chip in range(1, trip_ref.shape[0]):
        norm_grads += trip_ref[chip, :width, :].astype(jnp.float32)
    inner = (extra_ref[0:1] + extra_ref[1:2] + extra_ref[2:3]) / model
    inverse = inverse_ref[0:1]
    stream = stream_ref[...].astype(jnp.float32)
    heads = values_ref.shape[2] - SPARE
    low = in_low((heads, lanes))
    for chip in range(values_ref.shape[0]):
        for core in range(2):
            block = values_ref[chip, core].astype(jnp.float32)[:heads]
            for piece in range(2):
                at = ((chip * 2 + piece) * 2 + core) * heads
                features_ref[at : at + heads, :] = jnp.where(low == (piece == 0), block, 0.0)
    features = features_ref[...].astype(jnp.bfloat16)
    outputs = stream + by_pieces((weight_ref, partner_ref), features, first_pair)
    units = stream * inverse
    back = cotangent_ref[...].astype(jnp.float32)
    back = back + inverse * (norm_grads * gain_ref[...] - units * inner)
    extra = as_rows(parts_of(norms_ref[0:1]), (SPARE, lanes))
    outputs, back = (
        jnp.concatenate([block, extra], axis=0).astype(jnp.bfloat16) for block in (outputs, back)
    )
    for section in range(out_ref.shape[0]):
        out_ref[section] = jnp.where(ahead_ref[0] == section, outputs, back)


def spread_kernel(width, from_ref, trip_ref, code_ref, out_ref):
    rows = trip_ref.shape[2]
    blocks = [trip_ref[from_ref[index], :width, :] for index in range(2)]
    blocks = jnp.concatenate(blocks, axis=1)
    blocks = jnp.concatenate([blocks, jnp.zeros((LANES - width, 2 * rows), jnp.bfloat16)], axis=0)
    line = lax.broadcasted_iota(jnp.int32, (out_ref.shape[0], 2 * rows), 0)
    select = (line == code_ref[...]).astype(jnp.float32).astype(jnp.bfloat16)
    spread = product(select, blocks, (1, 1))
    total = jnp.zeros((SPARE, rows), jnp.float32)
    for section in range(trip_ref.shape[0]):
        total += trip_ref[section, width:, :].astype(jnp.float32)
    total = jnp.sum(jnp.sum(total, axis=0, keepdims=True), axis=1, keepdims=True)
    lane = lax.broadcasted_iota(jnp.int32, (1, LANES), 1)
    for index, part in enumerate(parts_of(total)):
        spread = spread + jnp.where(lane == width + index, part, 0.0)
    out_ref[...] = spread.astype(jnp.bfloat16)


def join_kernel(
    width, trip_ref, gradient_ref, weight_ref, first_ref, second_ref,
    passed_ref, returned_ref, new_weight_ref, new_first_ref, new_second_ref, rows_ref,
):
    _, _, capacity, micro_rows, _ = passed_ref.shape
    slots = 2 * capacity * micro_rows
    norms = jnp.zeros((1, LANES), jnp.float32)
    for chip in range(trip_ref.shape[0] // 4):
        for core in range(2):
            peers = [(chip * 2 + pair) * 2 + core for pair in range(2)]
            block = trip_ref[peers[0]].astype(jnp.float32) + trip_ref[peers[1]].astype(jnp.float32)
            norms += block[0:1]
            for piece in range(2):
                at = peers[piece] * width
                rows_ref[:, at : at + width] = block[piece * slots : (piece + 1) * slots, :width]
    at = 0
    for ref in (passed_ref, returned_ref):
        for slot in range(capacity):
            ref[0, 0, slot] = rows_ref[at : at + micro_rows, :].astype(jnp.bfloat16)
            at += micro_rows
    lane = lax.broadcasted_iota(jnp.int32, (1, LANES), 1)
    inside = (lane >= width) & (lane < width + 3)
    total = jnp.sum(jnp.where(inside, norms, 0.0), axis=1, keepdims=True)
    scale = jnp.minimum(1.0, CLIP_NORM / jnp.sqrt(total + 1e-06))
    span = 8 * width
    for at in range(0, gradient_ref.shape[1], span):
        here = slice(at, at + span)
        clipped = gradient_ref[:, here] * scale
        first = BETA_ONE * first_ref[0, :, here] + (1.0 - BETA_ONE) * clipped
        second = BETA_TWO * second_ref[0, :, here] + (1.0 - BETA_TWO) * clipped * clipped
        wide = weight_ref[0, :, here].astype(jnp.float32)
        updated = wide - LEARN_RATE * (first / (jnp.sqrt(second) + ADAM_EPS) + DECAY * wide)
        new_weight_ref[0, :, here] = updated.astype(jnp.bfloat16)
        new_first_ref[0, :, here] = first
        new_second_ref[0, :, here] = second


def slot_rows_of(placed, capacity, micro_rows):
    ids = jnp.arange(placed.shape[0], dtype=jnp.int32)
    twins = (placed[:, None] == placed[None, :]) & (ids[:, None] < ids[None, :])
    slots = placed * capacity + jnp.sum(twins.astype(jnp.int32), axis=0)
    return (slots[:, None] * micro_rows + jnp.arange(micro_rows, dtype=jnp.int32)).reshape(-1)


def on_core(kernel, out_shape, scalars, arrays, scratch=(), held_in=pltpu.VMEM, limit=24 * 2**20):
    size = sum(a.size * a.dtype.itemsize for a in arrays)
    size += sum(o.size * o.dtype.itemsize for o in out_shape)
    return pl.pallas_call(
        kernel,
        out_shape=out_shape,
        in_specs=[pl.BlockSpec(memory_space=pltpu.SMEM)] * len(scalars)
        + [pl.BlockSpec(memory_space=held_in)] * len(arrays),
        out_specs=[pl.BlockSpec(memory_space=pltpu.VMEM)] * len(out_shape),
        scratch_shapes=list(scratch),
        compiler_params=pltpu.CompilerParams(vmem_limit_bytes=limit),
        cost_estimate=pl.CostEstimate(flops=0, bytes_accessed=size, transcendentals=0),
    )(*scalars, *arrays)


def body(placing, acts, cotan, gain, w_value, w_out, moment_one, moment_two):
    team = lax.axis_size("team")
    chips = 2 * team
    peers = 2 * chips
    sections = lax.axis_size("section")
    section_now, pair_now = lax.axis_index("section"), lax.axis_index("pair")
    team_now = lax.axis_index("team")
    _, _, capacity, micro_rows, model = acts.shape
    slot_rows = capacity * micro_rows
    width = model // peers
    heads = w_value.shape[1]
    rows = peers * micro_rows
    half = rows // 2
    weights, out_weights = w_value[0], w_out[0]
    brief, full = jnp.bfloat16, jnp.float32
    core = lax.axis_index("core").astype(jnp.int32).reshape(1)
    pair = pair_now.astype(jnp.int32).reshape(1)

    def shape(dims, kind=brief):
        return jax.ShapeDtypeStruct(dims, kind)

    (held,) = on_core(
        split_kernel,
        [shape((chips, 2 * slot_rows, 4 * width))],
        [],
        [acts, cotan],
        [pltpu.VMEM(acts.shape, brief), pltpu.VMEM(cotan.shape, brief), pltpu.SemaphoreType.DMA((2,))],
        held_in=pl.ANY,
        limit=None,
    )
    pair_out_weights, pair_weights = moved(out_weights, "pair"), moved(weights, "pair")
    cols = swap(held, CHIP)
    placed = lax.dynamic_index_in_dim(placing[:, :, 0], section_now, 0, keepdims=False)
    slots = slot_rows_of(placed, capacity, micro_rows)
    slots = lax.dynamic_slice_in_dim(slots, pair_now * half, half, 0)
    holder, place = slots // slot_rows, slots % slot_rows
    at = ((holder % 2) * chips + holder // 2) * (2 * slot_rows) + place
    none = jnp.full_like(at, -(2**20))
    at = jnp.stack([jnp.concatenate([at, none]), jnp.concatenate([none, at])])
    code = holder * (4 * slot_rows) + place
    code = [code + kind * slot_rows + piece * 2 * slot_rows for kind in range(2) for piece in range(2)]
    code = jnp.concatenate(code)[None]
    own_gain = [
        lax.dynamic_slice_in_dim(
            gain[0], ((2 * team_now + piece) * 2 + core[0]) * width, width, 0
        )
        for piece in range(2)
    ]
    own_gain = jnp.concatenate(
        [jnp.broadcast_to(part.astype(full)[:, None], (width, half)) for part in own_gain], axis=1
    )
    cols, at, code, own_gain = lax.optimization_barrier((cols, at, code, own_gain))
    cols = lax.all_gather(cols, "core", axis=0).reshape(peers * 2 * slot_rows, 4 * width)

    mine, other, stream, cotangent = on_core(
        functools.partial(features_kernel, heads),
        [shape((team, heads, rows))] * 2 + [shape((width, rows))] * 2,
        [core, pair],
        [cols, at, out_weights, pair_out_weights],
    )
    arrived = moved(other, "core")
    (payload,) = on_core(
        functools.partial(payload_kernel, width, 0),
        [shape((team, width + heads, rows))],
        [],
        [mine, arrived, stream],
    )
    first_trip = swap(payload, TEAM)
    other_trip = moved(first_trip, "core")
    pair_trip = moved(first_trip, "pair")
    value_grads, mine, other = on_core(
        functools.partial(dnormed_kernel, width),
        [shape((heads, rows))] + [shape((team, width, rows))] * 2,
        [core, pair],
        [first_trip, weights, pair_weights],
    )
    arrived = moved(other, "core")
    own, half_gradient, inverse = on_core(
        functools.partial(values_kernel, width, heads),
        [
            shape((heads + SPARE, rows)),
            shape((heads, model), full),
            shape((SPARE, rows), full),
        ],
        [core, pair],
        [first_trip, other_trip, gain, weights, pair_weights, value_grads],
        [pltpu.VMEM((model, rows), brief)],
    )
    (payload,) = on_core(
        functools.partial(payload_kernel, 0, width),
        [shape((team, width + heads + SPARE, rows))],
        [],
        [mine, arrived, own],
    )
    second_trip = swap(payload, TEAM)
    gradient, norms = on_core(
        functools.partial(gradient_kernel, width),
        [shape((heads, model), full), shape((SPARE, rows), full)],
        [core, pair],
        [pair_trip, moved(pair_trip, "core"), gain, half_gradient],
        [pltpu.VMEM((model, rows), brief)],
    )
    gathered = lax.all_gather(second_trip[:, width:], "core", axis=1)
    extra = jnp.sum(gathered[:, :, heads:].astype(full), axis=(0, 1))

    ahead = ((section_now + 1) % sections).astype(jnp.int32).reshape(1)
    (both,) = on_core(
        functools.partial(finish_kernel, model),
        [shape((sections, width + SPARE, rows))],
        [pair, ahead],
        [
            second_trip,
            gathered,
            extra,
            out_weights,
            pair_out_weights,
            stream,
            cotangent,
            own_gain,
            inverse,
            norms,
        ],
        [pltpu.VMEM((model // 2, rows), full)],
    )
    third_trip = swap(both, "section")
    behind = jnp.stack([(section_now + sections - 1) % sections, (section_now + 1) % sections])

    (spread,) = on_core(
        functools.partial(spread_kernel, width),
        [shape((peers * 4 * slot_rows, LANES))],
        [behind.astype(jnp.int32)],
        [third_trip, code],
    )
    final = swap(spread.reshape(peers, 4 * slot_rows, LANES), PEER)
    return on_core(
        functools.partial(join_kernel, width),
        [shape(acts.shape)] * 2
        + [shape(w_value.shape), shape(moment_one.shape, full), shape(moment_two.shape, full)],
        [],
        [final, gradient, w_value, moment_one, moment_two],
        [pltpu.VMEM((2 * slot_rows, model), full)],
    )


def solution(mesh):
    sections, peers = mesh.devices.shape
    fine = Mesh(mesh.devices.reshape(sections, peers // 4, 2, 2), ("section",) + PEER)
    slots = P("section", PEER, None, None, None)
    matrix = P("section", PEER, None)
    return jax.shard_map(
        body,
        mesh=fine,
        in_specs=(P(), slots, slots, P("section", None), matrix, matrix, matrix, matrix),
        out_specs=(slots, slots, matrix, matrix, matrix),
        check_vma=False,
    )
```

```python
import functools

import jax
import jax.numpy as jnp
from jax import lax
from jax.experimental import pallas as pl
from jax.experimental.pallas import tpu as pltpu
from jax.sharding import Mesh, PartitionSpec as P

NORM_EPS = 1e-05
CLIP_NORM = 1.0
LEARN_RATE = 0.001
BETA_ONE = 0.9
BETA_TWO = 0.95
ADAM_EPS = 1e-08
DECAY = 0.1
CHIP = ("team", "pair")
PEER = CHIP + ("core",)
TEAM = "team"
SPARE = 8
LANES = 128


def swap(blocks, axis):
    return lax.all_to_all(blocks, axis, split_axis=0, concat_axis=0, tiled=True)


def moved(block, axis):
    return lax.ppermute(block, axis, [(0, 1), (1, 0)])


def product(left, right, contract):
    dims = (((contract[0],), (contract[1],)), ((), ()))
    return lax.dot_general(left, right, dims, preferred_element_type=jnp.float32)


def turned(values):
    return pltpu.roll(values, values.shape[1] // 2, 1)


def in_low(shape):
    return lax.broadcasted_iota(jnp.int32, shape, 1) < shape[1] // 2


def pieces_apart(packed, first_pair):
    low, other = in_low(packed.shape), turned(packed)
    first, second = jnp.where(low, packed, other), jnp.where(low, other, packed)
    return jnp.where(first_pair, first, second), jnp.where(first_pair, second, first)


def by_pieces(weight_refs, features, first_pair):
    results = []
    for ref in weight_refs:
        both = product(ref[...], features, (1, 0))
        results.append(both + turned(both))
    own, partner = results
    low = in_low(own.shape)
    ahead, behind = jnp.where(first_pair, own, partner), jnp.where(first_pair, partner, own)
    return jnp.where(low, ahead, behind)


def parts_of(values):
    high = lax.reduce_precision(values, 8, 7)
    middle = lax.reduce_precision(values - high, 8, 7)
    return [high, middle, values - high - middle]


def as_rows(parts, shape):
    line = lax.broadcasted_iota(jnp.int32, shape, 0)
    rows = jnp.zeros(shape, jnp.float32)
    for index, part in enumerate(parts):
        rows = jnp.where(line == index, part, rows)
    return rows


def split_kernel(acts_ref, cotan_ref, out_ref, acts_here, cotan_here, arrived):
    chips, _, width = out_ref.shape
    pairs = ((acts_ref, acts_here), (cotan_ref, cotan_here))
    copies = [pltpu.make_async_copy(a, b, arrived.at[n]) for n, (a, b) in enumerate(pairs)]
    for copy in copies:
        copy.start()
    for copy in copies:
        copy.wait()
    capacity = acts_here.shape[2]
    held = [ref[0, 0, slot] for ref in (acts_here, cotan_here) for slot in range(capacity)]
    held = jnp.concatenate([rows.astype(jnp.float32) for rows in held], axis=0)
    for chip in range(chips):
        at = chip // 2 * width
        out_ref[chip] = held[:, at : at + width].astype(jnp.bfloat16)


def partial_sums(weight_refs, packed, first_core, first_pair, width, mine_ref, other_ref):
    pieces = [piece.astype(jnp.bfloat16) for piece in pieces_apart(packed, first_pair)]
    team, span = mine_ref.shape[0], 4 * width
    group = min(team, 640 // span)
    low = in_low((width, packed.shape[1]))
    for first in range(0, team, group):
        columns = slice(first * span, (first + group) * span)
        part = sum(product(ref[:, columns], p, (0, 0)) for ref, p in zip(weight_refs, pieces))
        for local in range(group):
            parts = [part[local * span + n * width : local * span + (n + 1) * width] for n in range(4)]
            near, beyond = jnp.where(low, parts[0], parts[2]), jnp.where(low, parts[1], parts[3])
            mine, other = jnp.where(first_core, near, beyond), jnp.where(first_core, beyond, near)
            mine_ref[first + local] = mine.astype(jnp.bfloat16)
            other_ref[first + local] = other.astype(jnp.bfloat16)


def features_kernel(
    heads, core_ref, pair_ref, cols_ref, at_ref, weight_ref, partner_ref,
    mine_ref, other_ref, stream_ref, cotangent_ref,
):
    width, rows = stream_ref.shape
    slot_rows = cols_ref.shape[0] // (8 * mine_ref.shape[0])
    first_core, first_pair = core_ref[0] == 0, pair_ref[0] == 0
    line = lax.broadcasted_iota(jnp.int32, (cols_ref.shape[0], rows), 0)
    cols = cols_ref[...]

    def picked(first):
        total = 0.0
        for piece in range(2):
            select = (line == at_ref[piece : piece + 1, :] + first).astype(jnp.float32)
            both = product(cols, select.astype(jnp.bfloat16), (0, 0))
            total = total + both[2 * piece * width : 2 * (piece + 1) * width]
        return jnp.where(first_core, total[:width], total[width:])

    stream, cotangent = picked(0), picked(slot_rows)
    stream_ref[...] = stream.astype(jnp.bfloat16)
    cotangent_ref[...] = cotangent.astype(jnp.bfloat16)
    refs = (weight_ref, partner_ref)
    partial_sums(refs, cotangent, first_core, first_pair, heads, mine_ref, other_ref)


def payload_kernel(sums_at, own_at, mine_ref, arrived_ref, own_ref, out_ref):
    own = own_ref[...]
    count = mine_ref.shape[1]
    for chip in range(mine_ref.shape[0]):
        block = mine_ref[chip].astype(jnp.float32) + arrived_ref[chip].astype(jnp.float32)
        out_ref[chip, sums_at : sums_at + count, :] = block.astype(jnp.bfloat16)
        out_ref[chip, own_at : own_at + own.shape[0], :] = own


def dnormed_kernel(
    width, core_ref, pair_ref, trip_ref, weight_ref, partner_ref,
    grads_ref, mine_ref, other_ref, sent_ref,
):
    chips, heads = trip_ref.shape[0], grads_ref.shape[0]
    total = trip_ref[0, width:, :].astype(jnp.float32)
    for chip in range(1, chips):
        total += trip_ref[chip, width:, :].astype(jnp.float32)
    grads = total.astype(jnp.bfloat16)
    grads_ref[...] = grads
    for chip in range(chips):
        sent_ref[chip] = trip_ref[chip, :width, :]
    rest = jnp.zeros((width - heads, total.shape[1]), jnp.float32)
    sent_ref[chips] = jnp.concatenate([total, rest], axis=0).astype(jnp.bfloat16)
    first_core, first_pair = core_ref[0] == 0, pair_ref[0] == 0
    refs = (weight_ref, partner_ref)
    grads = grads.astype(jnp.float32)
    partial_sums(refs, grads, first_core, first_pair, width, mine_ref, other_ref)


def normalise(width, first_core, mine_ref, other_ref, gain_ref, normed_ref):
    chips, lanes = gain_ref.shape[1] // (4 * width), mine_ref.shape[2]
    squares = jnp.zeros((width, lanes), jnp.float32)
    for chip in range(chips):
        for ref in (mine_ref, other_ref):
            block = ref[chip, :width, :].astype(jnp.float32)
            squares += block * block
    total = jnp.broadcast_to(jnp.sum(squares, axis=0, keepdims=True), (SPARE, lanes))
    inverses = lax.rsqrt((total + turned(total)) / gain_ref.shape[1] + NORM_EPS)
    inverse = inverses[0:1]
    top = lax.broadcasted_iota(jnp.int32, (16, lanes), 0) == 0
    one = top.astype(jnp.float32).astype(jnp.bfloat16)
    low = in_low((width, lanes))
    span = 8 * width
    for first in range(0, chips, 2):
        at = first // 2 * span
        gains = jnp.broadcast_to(gain_ref[:, at : at + span], (16, span))
        gains = product(gains, one, (0, 0))
        for local in range(2):
            mine, other = (ref[first + local, :width, :] for ref in (mine_ref, other_ref))
            near, beyond = jnp.where(first_core, mine, other), jnp.where(first_core, other, mine)
            for core, block in ((0, near), (1, beyond)):
                units = block.astype(jnp.float32) * inverse
                for piece in range(2):
                    line = ((local * 2 + piece) * 2 + core) * width
                    scaled = units * gains[line : line + width]
                    scaled = jnp.where(low == (piece == 0), scaled, 0.0)
                    normed_ref[pl.ds(at + line, width), :] = scaled.astype(jnp.bfloat16)
    return inverses


def values_kernel(
    width, heads, core_ref, pair_ref, mine_ref, other_ref, gain_ref, weight_ref, partner_ref,
    grads_ref, own_ref, gradient_ref, inverse_ref, normed_ref,
):
    lanes = mine_ref.shape[2]
    first_core, first_pair = core_ref[0] == 0, pair_ref[0] == 0
    inverse_ref[...] = normalise(width, first_core, mine_ref, other_ref, gain_ref, normed_ref)
    values = by_pieces((weight_ref, partner_ref), normed_ref[...], first_pair)
    grads = grads_ref[...].astype(jnp.float32)
    own = pieces_apart(grads, first_pair)[0].astype(jnp.bfloat16)
    span = 8 * width
    for at in range(0, gain_ref.shape[1], span):
        gradient_ref[:, at : at + span] = product(own, normed_ref[at : at + span, :], (1, 1))
    inner = jnp.broadcast_to(jnp.sum(grads * values, axis=0, keepdims=True), (SPARE, lanes))
    inner = inner + turned(inner)
    extra = as_rows(parts_of(inner), (SPARE, lanes))
    own_ref[...] = jnp.concatenate([values, extra], axis=0).astype(jnp.bfloat16)


def gradient_kernel(
    width, core_ref, pair_ref, mine_ref, other_ref, gain_ref, half_ref,
    gradient_ref, norms_ref, normed_ref,
):
    lanes = norms_ref.shape[1]
    first_core, first_pair = core_ref[0] == 0, pair_ref[0] == 0
    normalise(width, first_core, mine_ref, other_ref, gain_ref, normed_ref)
    chips, heads = mine_ref.shape[0] - 1, half_ref.shape[0]
    grads = mine_ref[chips].astype(jnp.float32)[:heads]
    own = pieces_apart(grads, first_pair)[0].astype(jnp.bfloat16)
    norms = jnp.zeros((half_ref.shape[0], lanes), jnp.float32)
    span = 8 * width
    for at in range(0, gain_ref.shape[1], span):
        block = product(own, normed_ref[at : at + span, :], (1, 1)) + half_ref[:, at : at + span]
        gradient_ref[:, at : at + span] = block
        for lane in range(0, span, lanes):
            norms += block[:, lane : lane + lanes] * block[:, lane : lane + lanes]
    norms_ref[...] = jnp.broadcast_to(jnp.sum(norms, axis=0, keepdims=True), norms_ref.shape)


def finish_kernel(
    model, pair_ref, ahead_ref, trip_ref, values_ref, extra_ref, weight_ref, partner_ref, stream_ref,
    cotangent_ref, gain_ref, inverse_ref, norms_ref, out_ref, features_ref,
):
    width, lanes = stream_ref.shape
    first_pair = pair_ref[0] == 0
    norm_grads = trip_ref[0, :width, :].astype(jnp.float32)
    for chip in range(1, trip_ref.shape[0]):
        norm_grads += trip_ref[chip, :width, :].astype(jnp.float32)
    inner = (extra_ref[0:1] + extra_ref[1:2] + extra_ref[2:3]) / model
    inverse = inverse_ref[0:1]
    stream = stream_ref[...].astype(jnp.float32)
    heads = values_ref.shape[2] - SPARE
    low = in_low((heads, lanes))
    for chip in range(values_ref.shape[0]):
        for core in range(2):
            block = values_ref[chip, core].astype(jnp.float32)[:heads]
            for piece in range(2):
                at = ((chip * 2 + piece) * 2 + core) * heads
                features_ref[at : at + heads, :] = jnp.where(low == (piece == 0), block, 0.0)
    features = features_ref[...].astype(jnp.bfloat16)
    outputs = stream + by_pieces((weight_ref, partner_ref), features, first_pair)
    units = stream * inverse
    back = cotangent_ref[...].astype(jnp.float32)
    back = back + inverse * (norm_grads * gain_ref[...] - units * inner)
    extra = as_rows(parts_of(norms_ref[0:1]), (SPARE, lanes))
    outputs, back = (
        jnp.concatenate([block, extra], axis=0).astype(jnp.bfloat16) for block in (outputs, back)
    )
    for section in range(out_ref.shape[0]):
        out_ref[section] = jnp.where(ahead_ref[0] == section, outputs, back)


def spread_kernel(width, from_ref, trip_ref, code_ref, out_ref):
    rows = trip_ref.shape[2]
    blocks = [trip_ref[from_ref[index], :width, :] for index in range(2)]
    blocks = jnp.concatenate(blocks, axis=1)
    blocks = jnp.concatenate([blocks, jnp.zeros((LANES - width, 2 * rows), jnp.bfloat16)], axis=0)
    line = lax.broadcasted_iota(jnp.int32, (out_ref.shape[0], 2 * rows), 0)
    select = (line == code_ref[...]).astype(jnp.float32).astype(jnp.bfloat16)
    spread = product(select, blocks, (1, 1))
    total = jnp.zeros((SPARE, rows), jnp.float32)
    for section in range(trip_ref.shape[0]):
        total += trip_ref[section, width:, :].astype(jnp.float32)
    total = jnp.sum(jnp.sum(total, axis=0, keepdims=True), axis=1, keepdims=True)
    lane = lax.broadcasted_iota(jnp.int32, (1, LANES), 1)
    for index, part in enumerate(parts_of(total)):
        spread = spread + jnp.where(lane == width + index, part, 0.0)
    out_ref[...] = spread.astype(jnp.bfloat16)


def join_kernel(
    width, trip_ref, gradient_ref, weight_ref, first_ref, second_ref,
    passed_ref, returned_ref, new_weight_ref, new_first_ref, new_second_ref, rows_ref,
):
    _, _, capacity, micro_rows, _ = passed_ref.shape
    slots = 2 * capacity * micro_rows
    norms = jnp.zeros((1, LANES), jnp.float32)
    for chip in range(trip_ref.shape[0] // 4):
        for core in range(2):
            peers = [(chip * 2 + pair) * 2 + core for pair in range(2)]
            block = trip_ref[peers[0]].astype(jnp.float32) + trip_ref[peers[1]].astype(jnp.float32)
            norms += block[0:1]
            for piece in range(2):
                at = peers[piece] * width
                rows_ref[:, at : at + width] = block[piece * slots : (piece + 1) * slots, :width]
    at = 0
    for ref in (passed_ref, returned_ref):
        for slot in range(capacity):
            ref[0, 0, slot] = rows_ref[at : at + micro_rows, :].astype(jnp.bfloat16)
            at += micro_rows
    lane = lax.broadcasted_iota(jnp.int32, (1, LANES), 1)
    inside = (lane >= width) & (lane < width + 3)
    total = jnp.sum(jnp.where(inside, norms, 0.0), axis=1, keepdims=True)
    scale = jnp.minimum(1.0, CLIP_NORM / jnp.sqrt(total + 1e-06))
    span = 8 * width
    for at in range(0, gradient_ref.shape[1], span):
        here = slice(at, at + span)
        clipped = gradient_ref[:, here] * scale
        first = BETA_ONE * first_ref[0, :, here] + (1.0 - BETA_ONE) * clipped
        second = BETA_TWO * second_ref[0, :, here] + (1.0 - BETA_TWO) * clipped * clipped
        wide = weight_ref[0, :, here].astype(jnp.float32)
        updated = wide - LEARN_RATE * (first / (jnp.sqrt(second) + ADAM_EPS) + DECAY * wide)
        new_weight_ref[0, :, here] = updated.astype(jnp.bfloat16)
        new_first_ref[0, :, here] = first
        new_second_ref[0, :, here] = second


def slot_rows_of(placed, capacity, micro_rows):
    ids = jnp.arange(placed.shape[0], dtype=jnp.int32)
    twins = (placed[:, None] == placed[None, :]) & (ids[:, None] < ids[None, :])
    slots = placed * capacity + jnp.sum(twins.astype(jnp.int32), axis=0)
    return (slots[:, None] * micro_rows + jnp.arange(micro_rows, dtype=jnp.int32)).reshape(-1)


def on_core(kernel, out_shape, scalars, arrays, scratch=(), held_in=pltpu.VMEM, limit=24 * 2**20):
    size = sum(a.size * a.dtype.itemsize for a in arrays)
    size += sum(o.size * o.dtype.itemsize for o in out_shape)
    return pl.pallas_call(
        kernel,
        out_shape=out_shape,
        in_specs=[pl.BlockSpec(memory_space=pltpu.SMEM)] * len(scalars)
        + [pl.BlockSpec(memory_space=held_in)] * len(arrays),
        out_specs=[pl.BlockSpec(memory_space=pltpu.VMEM)] * len(out_shape),
        scratch_shapes=list(scratch),
        compiler_params=pltpu.CompilerParams(vmem_limit_bytes=limit),
        cost_estimate=pl.CostEstimate(flops=0, bytes_accessed=size, transcendentals=0),
    )(*scalars, *arrays)


def body(placing, acts, cotan, gain, w_value, w_out, moment_one, moment_two):
    team = lax.axis_size("team")
    chips = 2 * team
    peers = 2 * chips
    sections = lax.axis_size("section")
    section_now, pair_now = lax.axis_index("section"), lax.axis_index("pair")
    team_now = lax.axis_index("team")
    _, _, capacity, micro_rows, model = acts.shape
    slot_rows = capacity * micro_rows
    width = model // peers
    heads = w_value.shape[1]
    rows = peers * micro_rows
    half = rows // 2
    weights, out_weights = w_value[0], w_out[0]
    brief, full = jnp.bfloat16, jnp.float32
    core = lax.axis_index("core").astype(jnp.int32).reshape(1)
    pair = pair_now.astype(jnp.int32).reshape(1)

    def shape(dims, kind=brief):
        return jax.ShapeDtypeStruct(dims, kind)

    (held,) = on_core(
        split_kernel,
        [shape((chips, 2 * slot_rows, 4 * width))],
        [],
        [acts, cotan],
        [pltpu.VMEM(acts.shape, brief), pltpu.VMEM(cotan.shape, brief), pltpu.SemaphoreType.DMA((2,))],
        held_in=pl.ANY,
        limit=None,
    )
    pair_out_weights, pair_weights = moved(out_weights, "pair"), moved(weights, "pair")
    cols = swap(held, CHIP)
    placed = lax.dynamic_index_in_dim(placing[:, :, 0], section_now, 0, keepdims=False)
    slots = slot_rows_of(placed, capacity, micro_rows)
    slots = lax.dynamic_slice_in_dim(slots, pair_now * half, half, 0)
    holder, place = slots // slot_rows, slots % slot_rows
    at = ((holder % 2) * chips + holder // 2) * (2 * slot_rows) + place
    none = jnp.full_like(at, -(2**20))
    at = jnp.stack([jnp.concatenate([at, none]), jnp.concatenate([none, at])])
    code = holder * (4 * slot_rows) + place
    code = [code + kind * slot_rows + piece * 2 * slot_rows for kind in range(2) for piece in range(2)]
    code = jnp.concatenate(code)[None]
    own_gain = [
        lax.dynamic_slice_in_dim(
            gain[0], ((2 * team_now + piece) * 2 + core[0]) * width, width, 0
        )
        for piece in range(2)
    ]
    own_gain = jnp.concatenate(
        [jnp.broadcast_to(part.astype(full)[:, None], (width, half)) for part in own_gain], axis=1
    )
    cols, at, code, own_gain = lax.optimization_barrier((cols, at, code, own_gain))
    cols = lax.all_gather(cols, "core", axis=0).reshape(peers * 2 * slot_rows, 4 * width)

    mine, other, stream, cotangent = on_core(
        functools.partial(features_kernel, heads),
        [shape((team, heads, rows))] * 2 + [shape((width, rows))] * 2,
        [core, pair],
        [cols, at, out_weights, pair_out_weights],
    )
    arrived = moved(other, "core")
    (payload,) = on_core(
        functools.partial(payload_kernel, width, 0),
        [shape((team, width + heads, rows))],
        [],
        [mine, arrived, stream],
    )
    payload, pair_weights = lax.optimization_barrier((payload, pair_weights))
    first_trip = swap(payload, TEAM)
    other_trip = moved(first_trip, "core")
    value_grads, mine, other, sent = on_core(
        functools.partial(dnormed_kernel, width),
        [shape((heads, rows))]
        + [shape((team, width, rows))] * 2
        + [shape((team + 1, width, rows))],
        [core, pair],
        [first_trip, weights, pair_weights],
    )
    arrived = moved(other, "core")
    pair_trip = moved(sent, "pair")
    own, half_gradient, inverse = on_core(
        functools.partial(values_kernel, width, heads),
        [
            shape((heads + SPARE, rows)),
            shape((heads, model), full),
            shape((SPARE, rows), full),
        ],
        [core, pair],
        [first_trip, other_trip, gain, weights, pair_weights, value_grads],
        [pltpu.VMEM((model, rows), brief)],
    )
    (payload,) = on_core(
        functools.partial(payload_kernel, 0, width),
        [shape((team, width + heads + SPARE, rows))],
        [],
        [mine, arrived, own],
    )
    second_trip = swap(payload, TEAM)
    gradient, norms = on_core(
        functools.partial(gradient_kernel, width),
        [shape((heads, model), full), shape((SPARE, rows), full)],
        [core, pair],
        [pair_trip, moved(pair_trip, "core"), gain, half_gradient],
        [pltpu.VMEM((model, rows), brief)],
    )
    gathered = lax.all_gather(second_trip[:, width:], "core", axis=1)
    extra = jnp.sum(gathered[:, :, heads:].astype(full), axis=(0, 1))

    ahead = ((section_now + 1) % sections).astype(jnp.int32).reshape(1)
    (both,) = on_core(
        functools.partial(finish_kernel, model),
        [shape((sections, width + SPARE, rows))],
        [pair, ahead],
        [
            second_trip,
            gathered,
            extra,
            out_weights,
            pair_out_weights,
            stream,
            cotangent,
            own_gain,
            inverse,
            norms,
        ],
        [pltpu.VMEM((model // 2, rows), full)],
    )
    third_trip = swap(both, "section")
    behind = jnp.stack([(section_now + sections - 1) % sections, (section_now + 1) % sections])

    (spread,) = on_core(
        functools.partial(spread_kernel, width),
        [shape((peers * 4 * slot_rows, LANES))],
        [behind.astype(jnp.int32)],
        [third_trip, code],
    )
    final = swap(spread.reshape(peers, 4 * slot_rows, LANES), PEER)
    return on_core(
        functools.partial(join_kernel, width),
        [shape(acts.shape)] * 2
        + [shape(w_value.shape), shape(moment_one.shape, full), shape(moment_two.shape, full)],
        [],
        [final, gradient, w_value, moment_one, moment_two],
        [pltpu.VMEM((2 * slot_rows, model), full)],
    )


def solution(mesh):
    sections, peers = mesh.devices.shape
    fine = Mesh(mesh.devices.reshape(sections, peers // 4, 2, 2), ("section",) + PEER)
    slots = P("section", PEER, None, None, None)
    matrix = P("section", PEER, None)
    return jax.shard_map(
        body,
        mesh=fine,
        in_specs=(P(), slots, slots, P("section", None), matrix, matrix, matrix, matrix),
        out_specs=(slots, slots, matrix, matrix, matrix),
        check_vma=False,
    )
```

```python
import functools

import jax
import jax.numpy as jnp
from jax import lax
from jax.experimental import pallas as pl
from jax.experimental.pallas import tpu as pltpu
from jax.sharding import Mesh, PartitionSpec as P

NORM_EPS = 1e-05
CLIP_NORM = 1.0
LEARN_RATE = 0.001
BETA_ONE = 0.9
BETA_TWO = 0.95
ADAM_EPS = 1e-08
DECAY = 0.1
CHIP = ("team", "pair")
PEER = CHIP + ("core",)
TEAM = "team"
SPARE = 8
LANES = 128


def swap(blocks, axis):
    return lax.all_to_all(blocks, axis, split_axis=0, concat_axis=0, tiled=True)


def moved(block, axis):
    return lax.ppermute(block, axis, [(0, 1), (1, 0)])


def product(left, right, contract):
    dims = (((contract[0],), (contract[1],)), ((), ()))
    return lax.dot_general(left, right, dims, preferred_element_type=jnp.float32)


def turned(values):
    return pltpu.roll(values, values.shape[1] // 2, 1)


def in_low(shape):
    return lax.broadcasted_iota(jnp.int32, shape, 1) < shape[1] // 2


def pieces_apart(packed, first_pair):
    low, other = in_low(packed.shape), turned(packed)
    first, second = jnp.where(low, packed, other), jnp.where(low, other, packed)
    return jnp.where(first_pair, first, second), jnp.where(first_pair, second, first)


def by_pieces(weight_refs, features, first_pair):
    results = []
    for ref in weight_refs:
        both = product(ref[...], features, (1, 0))
        results.append(both + turned(both))
    own, partner = results
    low = in_low(own.shape)
    ahead, behind = jnp.where(first_pair, own, partner), jnp.where(first_pair, partner, own)
    return jnp.where(low, ahead, behind)


def parts_of(values):
    high = lax.reduce_precision(values, 8, 7)
    middle = lax.reduce_precision(values - high, 8, 7)
    return [high, middle, values - high - middle]


def as_rows(parts, shape):
    line = lax.broadcasted_iota(jnp.int32, shape, 0)
    rows = jnp.zeros(shape, jnp.float32)
    for index, part in enumerate(parts):
        rows = jnp.where(line == index, part, rows)
    return rows


def split_kernel(acts_ref, cotan_ref, out_ref, acts_here, cotan_here, arrived):
    chips, _, width = out_ref.shape
    pairs = ((acts_ref, acts_here), (cotan_ref, cotan_here))
    copies = [pltpu.make_async_copy(a, b, arrived.at[n]) for n, (a, b) in enumerate(pairs)]
    for copy in copies:
        copy.start()
    for copy in copies:
        copy.wait()
    capacity = acts_here.shape[2]
    held = [ref[0, 0, slot] for ref in (acts_here, cotan_here) for slot in range(capacity)]
    held = jnp.concatenate([rows.astype(jnp.float32) for rows in held], axis=0)
    for chip in range(chips):
        at = chip // 2 * width
        out_ref[chip] = held[:, at : at + width].astype(jnp.bfloat16)


def partial_sums(weight_refs, packed, first_core, first_pair, width, mine_ref, other_ref):
    pieces = [piece.astype(jnp.bfloat16) for piece in pieces_apart(packed, first_pair)]
    team, span = mine_ref.shape[0], 4 * width
    group = min(team, 640 // span)
    low = in_low((width, packed.shape[1]))
    for first in range(0, team, group):
        columns = slice(first * span, (first + group) * span)
        part = sum(product(ref[:, columns], p, (0, 0)) for ref, p in zip(weight_refs, pieces))
        for local in range(group):
            parts = [part[local * span + n * width : local * span + (n + 1) * width] for n in range(4)]
            near, beyond = jnp.where(low, parts[0], parts[2]), jnp.where(low, parts[1], parts[3])
            mine, other = jnp.where(first_core, near, beyond), jnp.where(first_core, beyond, near)
            mine_ref[first + local] = mine.astype(jnp.bfloat16)
            other_ref[first + local] = other.astype(jnp.bfloat16)


def features_kernel(
    heads, core_ref, pair_ref, cols_ref, at_ref, weight_ref, partner_ref,
    mine_ref, other_ref, stream_ref, cotangent_ref,
):
    width, rows = stream_ref.shape
    slot_rows = cols_ref.shape[0] // (8 * mine_ref.shape[0])
    first_core, first_pair = core_ref[0] == 0, pair_ref[0] == 0
    line = lax.broadcasted_iota(jnp.int32, (cols_ref.shape[0], rows), 0)
    cols = cols_ref[...]

    def picked(first):
        total = 0.0
        for piece in range(2):
            select = (line == at_ref[piece : piece + 1, :] + first).astype(jnp.float32)
            both = product(cols, select.astype(jnp.bfloat16), (0, 0))
            total = total + both[2 * piece * width : 2 * (piece + 1) * width]
        return jnp.where(first_core, total[:width], total[width:])

    stream, cotangent = picked(0), picked(slot_rows)
    stream_ref[...] = stream.astype(jnp.bfloat16)
    cotangent_ref[...] = cotangent.astype(jnp.bfloat16)
    refs = (weight_ref, partner_ref)
    partial_sums(refs, cotangent, first_core, first_pair, heads, mine_ref, other_ref)


def payload_kernel(sums_at, own_at, mine_ref, arrived_ref, own_ref, out_ref):
    own = own_ref[...]
    count = mine_ref.shape[1]
    for chip in range(mine_ref.shape[0]):
        block = mine_ref[chip].astype(jnp.float32) + arrived_ref[chip].astype(jnp.float32)
        out_ref[chip, sums_at : sums_at + count, :] = block.astype(jnp.bfloat16)
        out_ref[chip, own_at : own_at + own.shape[0], :] = own


def summed_grads(width, trip_ref):
    total = trip_ref[0, width:, :].astype(jnp.float32)
    for chip in range(1, trip_ref.shape[0]):
        total += trip_ref[chip, width:, :].astype(jnp.float32)
    return total.astype(jnp.bfloat16)


def dnormed_kernel(
    width, core_ref, pair_ref, trip_ref, weight_ref, partner_ref,
    grads_ref, mine_ref, other_ref,
):
    grads = summed_grads(width, trip_ref)
    grads_ref[...] = grads
    first_core, first_pair = core_ref[0] == 0, pair_ref[0] == 0
    refs = (weight_ref, partner_ref)
    grads = grads.astype(jnp.float32)
    partial_sums(refs, grads, first_core, first_pair, width, mine_ref, other_ref)


def normalise(width, first_core, mine_ref, other_ref, gain_ref, normed_ref):
    chips, _, lanes = mine_ref.shape
    squares = jnp.zeros((width, lanes), jnp.float32)
    for chip in range(chips):
        for ref in (mine_ref, other_ref):
            block = ref[chip, :width, :].astype(jnp.float32)
            squares += block * block
    total = jnp.broadcast_to(jnp.sum(squares, axis=0, keepdims=True), (SPARE, lanes))
    inverses = lax.rsqrt((total + turned(total)) / gain_ref.shape[1] + NORM_EPS)
    inverse = inverses[0:1]
    top = lax.broadcasted_iota(jnp.int32, (16, lanes), 0) == 0
    one = top.astype(jnp.float32).astype(jnp.bfloat16)
    low = in_low((width, lanes))
    span = 8 * width
    for first in range(0, chips, 2):
        at = first // 2 * span
        gains = jnp.broadcast_to(gain_ref[:, at : at + span], (16, span))
        gains = product(gains, one, (0, 0))
        for local in range(2):
            mine, other = (ref[first + local, :width, :] for ref in (mine_ref, other_ref))
            near, beyond = jnp.where(first_core, mine, other), jnp.where(first_core, other, mine)
            for core, block in ((0, near), (1, beyond)):
                units = block.astype(jnp.float32) * inverse
                for piece in range(2):
                    line = ((local * 2 + piece) * 2 + core) * width
                    scaled = units * gains[line : line + width]
                    scaled = jnp.where(low == (piece == 0), scaled, 0.0)
                    normed_ref[pl.ds(at + line, width), :] = scaled.astype(jnp.bfloat16)
    return inverses


def values_kernel(
    width, heads, core_ref, pair_ref, mine_ref, other_ref, gain_ref, weight_ref, partner_ref,
    grads_ref, own_ref, gradient_ref, inverse_ref, normed_ref,
):
    lanes = mine_ref.shape[2]
    first_core, first_pair = core_ref[0] == 0, pair_ref[0] == 0
    inverse_ref[...] = normalise(width, first_core, mine_ref, other_ref, gain_ref, normed_ref)
    values = by_pieces((weight_ref, partner_ref), normed_ref[...], first_pair)
    grads = grads_ref[...].astype(jnp.float32)
    own = pieces_apart(grads, first_pair)[0].astype(jnp.bfloat16)
    span = 8 * width
    for at in range(0, gain_ref.shape[1], span):
        gradient_ref[:, at : at + span] = product(own, normed_ref[at : at + span, :], (1, 1))
    inner = jnp.broadcast_to(jnp.sum(grads * values, axis=0, keepdims=True), (SPARE, lanes))
    inner = inner + turned(inner)
    extra = as_rows(parts_of(inner), (SPARE, lanes))
    own_ref[...] = jnp.concatenate([values, extra], axis=0).astype(jnp.bfloat16)


def gradient_kernel(
    width, core_ref, pair_ref, mine_ref, other_ref, gain_ref, half_ref,
    gradient_ref, norms_ref, normed_ref,
):
    lanes = norms_ref.shape[1]
    first_core, first_pair = core_ref[0] == 0, pair_ref[0] == 0
    normalise(width, first_core, mine_ref, other_ref, gain_ref, normed_ref)
    grads = summed_grads(width, mine_ref).astype(jnp.float32)
    own = pieces_apart(grads, first_pair)[0].astype(jnp.bfloat16)
    norms = jnp.zeros((half_ref.shape[0], lanes), jnp.float32)
    span = 8 * width
    for at in range(0, gain_ref.shape[1], span):
        block = product(own, normed_ref[at : at + span, :], (1, 1)) + half_ref[:, at : at + span]
        gradient_ref[:, at : at + span] = block
        for lane in range(0, span, lanes):
            norms += block[:, lane : lane + lanes] * block[:, lane : lane + lanes]
    norms_ref[...] = jnp.broadcast_to(jnp.sum(norms, axis=0, keepdims=True), norms_ref.shape)


def finish_kernel(
    model, pair_ref, ahead_ref, trip_ref, values_ref, extra_ref, weight_ref, partner_ref, stream_ref,
    cotangent_ref, gain_ref, inverse_ref, norms_ref, out_ref, features_ref,
):
    width, lanes = stream_ref.shape
    first_pair = pair_ref[0] == 0
    norm_grads = trip_ref[0, :width, :].astype(jnp.float32)
    for chip in range(1, trip_ref.shape[0]):
        norm_grads += trip_ref[chip, :width, :].astype(jnp.float32)
    inner = (extra_ref[0:1] + extra_ref[1:2] + extra_ref[2:3]) / model
    inverse = inverse_ref[0:1]
    stream = stream_ref[...].astype(jnp.float32)
    heads = values_ref.shape[2] - SPARE
    low = in_low((heads, lanes))
    for chip in range(values_ref.shape[0]):
        for core in range(2):
            block = values_ref[chip, core].astype(jnp.float32)[:heads]
            for piece in range(2):
                at = ((chip * 2 + piece) * 2 + core) * heads
                features_ref[at : at + heads, :] = jnp.where(low == (piece == 0), block, 0.0)
    features = features_ref[...].astype(jnp.bfloat16)
    outputs = stream + by_pieces((weight_ref, partner_ref), features, first_pair)
    units = stream * inverse
    back = cotangent_ref[...].astype(jnp.float32)
    back = back + inverse * (norm_grads * gain_ref[...] - units * inner)
    extra = as_rows(parts_of(norms_ref[0:1]), (SPARE, lanes))
    outputs, back = (
        jnp.concatenate([block, extra], axis=0).astype(jnp.bfloat16) for block in (outputs, back)
    )
    for section in range(out_ref.shape[0]):
        out_ref[section] = jnp.where(ahead_ref[0] == section, outputs, back)


def spread_kernel(width, from_ref, trip_ref, code_ref, out_ref):
    rows = trip_ref.shape[2]
    blocks = [trip_ref[from_ref[index], :width, :] for index in range(2)]
    blocks = jnp.concatenate(blocks, axis=1)
    blocks = jnp.concatenate([blocks, jnp.zeros((LANES - width, 2 * rows), jnp.bfloat16)], axis=0)
    line = lax.broadcasted_iota(jnp.int32, (out_ref.shape[0], 2 * rows), 0)
    select = (line == code_ref[...]).astype(jnp.float32).astype(jnp.bfloat16)
    spread = product(select, blocks, (1, 1))
    total = jnp.zeros((SPARE, rows), jnp.float32)
    for section in range(trip_ref.shape[0]):
        total += trip_ref[section, width:, :].astype(jnp.float32)
    total = jnp.sum(jnp.sum(total, axis=0, keepdims=True), axis=1, keepdims=True)
    lane = lax.broadcasted_iota(jnp.int32, (1, LANES), 1)
    for index, part in enumerate(parts_of(total)):
        spread = spread + jnp.where(lane == width + index, part, 0.0)
    out_ref[...] = spread.astype(jnp.bfloat16)


def join_kernel(
    width, trip_ref, gradient_ref, weight_ref, first_ref, second_ref,
    passed_ref, returned_ref, new_weight_ref, new_first_ref, new_second_ref, rows_ref,
):
    _, _, capacity, micro_rows, _ = passed_ref.shape
    slots = 2 * capacity * micro_rows
    norms = jnp.zeros((1, LANES), jnp.float32)
    for chip in range(trip_ref.shape[0] // 4):
        for core in range(2):
            peers = [(chip * 2 + pair) * 2 + core for pair in range(2)]
            block = trip_ref[peers[0]].astype(jnp.float32) + trip_ref[peers[1]].astype(jnp.float32)
            norms += block[0:1]
            for piece in range(2):
                at = peers[piece] * width
                rows_ref[:, at : at + width] = block[piece * slots : (piece + 1) * slots, :width]
    at = 0
    for ref in (passed_ref, returned_ref):
        for slot in range(capacity):
            ref[0, 0, slot] = rows_ref[at : at + micro_rows, :].astype(jnp.bfloat16)
            at += micro_rows
    lane = lax.broadcasted_iota(jnp.int32, (1, LANES), 1)
    inside = (lane >= width) & (lane < width + 3)
    total = jnp.sum(jnp.where(inside, norms, 0.0), axis=1, keepdims=True)
    scale = jnp.minimum(1.0, CLIP_NORM / jnp.sqrt(total + 1e-06))
    span = 8 * width
    for at in range(0, gradient_ref.shape[1], span):
        here = slice(at, at + span)
        clipped = gradient_ref[:, here] * scale
        first = BETA_ONE * first_ref[0, :, here] + (1.0 - BETA_ONE) * clipped
        second = BETA_TWO * second_ref[0, :, here] + (1.0 - BETA_TWO) * clipped * clipped
        wide = weight_ref[0, :, here].astype(jnp.float32)
        updated = wide - LEARN_RATE * (first / (jnp.sqrt(second) + ADAM_EPS) + DECAY * wide)
        new_weight_ref[0, :, here] = updated.astype(jnp.bfloat16)
        new_first_ref[0, :, here] = first
        new_second_ref[0, :, here] = second


def slot_rows_of(placed, capacity, micro_rows):
    ids = jnp.arange(placed.shape[0], dtype=jnp.int32)
    twins = (placed[:, None] == placed[None, :]) & (ids[:, None] < ids[None, :])
    slots = placed * capacity + jnp.sum(twins.astype(jnp.int32), axis=0)
    return (slots[:, None] * micro_rows + jnp.arange(micro_rows, dtype=jnp.int32)).reshape(-1)


def on_core(kernel, out_shape, scalars, arrays, scratch=(), held_in=pltpu.VMEM, limit=24 * 2**20):
    size = sum(a.size * a.dtype.itemsize for a in arrays)
    size += sum(o.size * o.dtype.itemsize for o in out_shape)
    return pl.pallas_call(
        kernel,
        out_shape=out_shape,
        in_specs=[pl.BlockSpec(memory_space=pltpu.SMEM)] * len(scalars)
        + [pl.BlockSpec(memory_space=held_in)] * len(arrays),
        out_specs=[pl.BlockSpec(memory_space=pltpu.VMEM)] * len(out_shape),
        scratch_shapes=list(scratch),
        compiler_params=pltpu.CompilerParams(vmem_limit_bytes=limit),
        cost_estimate=pl.CostEstimate(flops=0, bytes_accessed=size, transcendentals=0),
    )(*scalars, *arrays)


def body(placing, acts, cotan, gain, w_value, w_out, moment_one, moment_two):
    team = lax.axis_size("team")
    chips = 2 * team
    peers = 2 * chips
    sections = lax.axis_size("section")
    section_now, pair_now = lax.axis_index("section"), lax.axis_index("pair")
    team_now = lax.axis_index("team")
    _, _, capacity, micro_rows, model = acts.shape
    slot_rows = capacity * micro_rows
    width = model // peers
    heads = w_value.shape[1]
    rows = peers * micro_rows
    half = rows // 2
    weights, out_weights = w_value[0], w_out[0]
    brief, full = jnp.bfloat16, jnp.float32
    core = lax.axis_index("core").astype(jnp.int32).reshape(1)
    pair = pair_now.astype(jnp.int32).reshape(1)

    def shape(dims, kind=brief):
        return jax.ShapeDtypeStruct(dims, kind)

    (held,) = on_core(
        split_kernel,
        [shape((chips, 2 * slot_rows, 4 * width))],
        [],
        [acts, cotan],
        [pltpu.VMEM(acts.shape, brief), pltpu.VMEM(cotan.shape, brief), pltpu.SemaphoreType.DMA((2,))],
        held_in=pl.ANY,
        limit=None,
    )
    pair_out_weights, pair_weights = moved(out_weights, "pair"), moved(weights, "pair")
    cols = swap(held, CHIP)
    placed = lax.dynamic_index_in_dim(placing[:, :, 0], section_now, 0, keepdims=False)
    slots = slot_rows_of(placed, capacity, micro_rows)
    slots = lax.dynamic_slice_in_dim(slots, pair_now * half, half, 0)
    holder, place = slots // slot_rows, slots % slot_rows
    at = ((holder % 2) * chips + holder // 2) * (2 * slot_rows) + place
    none = jnp.full_like(at, -(2**20))
    at = jnp.stack([jnp.concatenate([at, none]), jnp.concatenate([none, at])])
    code = holder * (4 * slot_rows) + place
    code = [code + kind * slot_rows + piece * 2 * slot_rows for kind in range(2) for piece in range(2)]
    code = jnp.concatenate(code)[None]
    own_gain = [
        lax.dynamic_slice_in_dim(
            gain[0], ((2 * team_now + piece) * 2 + core[0]) * width, width, 0
        )
        for piece in range(2)
    ]
    own_gain = jnp.concatenate(
        [jnp.broadcast_to(part.astype(full)[:, None], (width, half)) for part in own_gain], axis=1
    )
    cols, at, code, own_gain = lax.optimization_barrier((cols, at, code, own_gain))
    cols = lax.all_gather(cols, "core", axis=0).reshape(peers * 2 * slot_rows, 4 * width)

    mine, other, stream, cotangent = on_core(
        functools.partial(features_kernel, heads),
        [shape((team, heads, rows))] * 2 + [shape((width, rows))] * 2,
        [core, pair],
        [cols, at, out_weights, pair_out_weights],
    )
    arrived = moved(other, "core")
    (payload,) = on_core(
        functools.partial(payload_kernel, width, 0),
        [shape((team, width + heads, rows))],
        [],
        [mine, arrived, stream],
    )
    payload, pair_weights = lax.optimization_barrier((payload, pair_weights))
    first_trip = swap(payload, TEAM)
    other_trip = moved(first_trip, "core")
    pair_trip = moved(first_trip, "pair")
    value_grads, mine, other = on_core(
        functools.partial(dnormed_kernel, width),
        [shape((heads, rows))] + [shape((team, width, rows))] * 2,
        [core, pair],
        [first_trip, weights, pair_weights],
    )
    arrived = moved(other, "core")
    own, half_gradient, inverse = on_core(
        functools.partial(values_kernel, width, heads),
        [
            shape((heads + SPARE, rows)),
            shape((heads, model), full),
            shape((SPARE, rows), full),
        ],
        [core, pair],
        [first_trip, other_trip, gain, weights, pair_weights, value_grads],
        [pltpu.VMEM((model, rows), brief)],
    )
    (payload,) = on_core(
        functools.partial(payload_kernel, 0, width),
        [shape((team, width + heads + SPARE, rows))],
        [],
        [mine, arrived, own],
    )
    second_trip = swap(payload, TEAM)
    gradient, norms = on_core(
        functools.partial(gradient_kernel, width),
        [shape((heads, model), full), shape((SPARE, rows), full)],
        [core, pair],
        [pair_trip, moved(pair_trip, "core"), gain, half_gradient],
        [pltpu.VMEM((model, rows), brief)],
    )
    gathered = lax.all_gather(second_trip[:, width:], "core", axis=1)
    extra = jnp.sum(gathered[:, :, heads:].astype(full), axis=(0, 1))

    ahead = ((section_now + 1) % sections).astype(jnp.int32).reshape(1)
    (both,) = on_core(
        functools.partial(finish_kernel, model),
        [shape((sections, width + SPARE, rows))],
        [pair, ahead],
        [
            second_trip,
            gathered,
            extra,
            out_weights,
            pair_out_weights,
            stream,
            cotangent,
            own_gain,
            inverse,
            norms,
        ],
        [pltpu.VMEM((model // 2, rows), full)],
    )
    third_trip = swap(both, "section")
    behind = jnp.stack([(section_now + sections - 1) % sections, (section_now + 1) % sections])

    (spread,) = on_core(
        functools.partial(spread_kernel, width),
        [shape((peers * 4 * slot_rows, LANES))],
        [behind.astype(jnp.int32)],
        [third_trip, code],
    )
    final = swap(spread.reshape(peers, 4 * slot_rows, LANES), PEER)
    return on_core(
        functools.partial(join_kernel, width),
        [shape(acts.shape)] * 2
        + [shape(w_value.shape), shape(moment_one.shape, full), shape(moment_two.shape, full)],
        [],
        [final, gradient, w_value, moment_one, moment_two],
        [pltpu.VMEM((2 * slot_rows, model), full)],
    )


def solution(mesh):
    sections, peers = mesh.devices.shape
    fine = Mesh(mesh.devices.reshape(sections, peers // 4, 2, 2), ("section",) + PEER)
    slots = P("section", PEER, None, None, None)
    matrix = P("section", PEER, None)
    return jax.shard_map(
        body,
        mesh=fine,
        in_specs=(P(), slots, slots, P("section", None), matrix, matrix, matrix, matrix),
        out_specs=(slots, slots, matrix, matrix, matrix),
        check_vma=False,
    )
```
